32 devices in a mesh: dp: 4 (over y, x), ctx: 8 (over z, core).
Axes of the slice: x: 2, y: 2, z: 4, core: 2. Of those that a mesh axis runs over, the one named last changes fastest.
Arguments:
- tokens: bfloat16 [8, 1024, 768], P('dp', 'ctx'), may hold values from -6 to 6
- segments: int32 [8, 1024], P('dp', 'ctx'), may hold values from 0 to 7, as said below
- cotangent: bfloat16 [8, 1024, 768], P('dp', 'ctx'), may hold values from -6 to 6
- ln1_gain: bfloat16 [768], P(('dp', 'ctx')), may hold values from 0.5 to 1.5
- ln1_bias: bfloat16 [768], P(('dp', 'ctx')), may hold values from -2 to 2
- w_qkv: bfloat16 [768, 2304], P(('dp', 'ctx')), may hold values from -0.21875 to 0.21875
- bias_query: bfloat16 [768], P(('dp', 'ctx')), may hold values from -3 to 3
- bias_value: bfloat16 [768], P(('dp', 'ctx')), may hold values from -3 to 3
- w_out: bfloat16 [768, 768], P(('dp', 'ctx')), may hold values from -1.75 to 1.75
- bias_out: bfloat16 [768], P(('dp', 'ctx')), may hold values from -3 to 3
- ln2_gain: bfloat16 [768], P(('dp', 'ctx')), may hold values from 0.5 to 1.5
- ln2_bias: bfloat16 [768], P(('dp', 'ctx')), may hold values from -2 to 2
- w_up: bfloat16 [768, 3072], P(('dp', 'ctx')), may hold values from -0.21875 to 0.21875
- bias_up: bfloat16 [3072], P(('dp', 'ctx')), may hold values from -3 to 3
- w_down: bfloat16 [3072, 768], P(('dp', 'ctx')), may hold values from -0.109375 to 0.109375
- bias_down: bfloat16 [768], P(('dp', 'ctx')), may hold values from -3 to 3
Outputs:
- output: bfloat16 [8, 1024, 768], P('dp', 'ctx')
- grad_tokens: bfloat16 [8, 1024, 768], P('dp', 'ctx')
- grad_ln1_gain: float32 [768], P(('dp', 'ctx'))
- grad_ln1_bias: float32 [768], P(('dp', 'ctx'))
- grad_w_qkv: float32 [768, 2304], P(('dp', 'ctx'))
- grad_bias_query: float32 [768], P(('dp', 'ctx'))
- grad_bias_value: float32 [768], P(('dp', 'ctx'))
- grad_w_out: float32 [768, 768], P(('dp', 'ctx'))
- grad_bias_out: float32 [768], P(('dp', 'ctx'))
- grad_ln2_gain: float32 [768], P(('dp', 'ctx'))
- grad_ln2_bias: float32 [768], P(('dp', 'ctx'))
- grad_w_up: float32 [768, 3072], P(('dp', 'ctx'))
- grad_bias_up: float32 [3072], P(('dp', 'ctx'))
- grad_w_down: float32 [3072, 768], P(('dp', 'ctx'))
- grad_bias_down: float32 [768], P(('dp', 'ctx'))
The draws below stay inside these ranges and needn't reach their ends.
Inputs may be any that keep to these rules, and one draw needn't show every extreme that they name: `segments`: along each sequence the document number starts at 0 and rises by one where a new document begins; documents hold 128 to 512 tokens, the last of a sequence possibly fewer. Of the 2 sequences of each dp index, one is a single document; in one dp index a sequence consists of documents of exactly 128 tokens but its last.
All inputs are finite; a program needn't handle non-finite values.
Results may differ from the reference program's by a relative error of at most 0.035.
Values may be sent and summed in bfloat16 or wider, within the bound.
No kernel may reach another device: no remote copies, remote signals or barrier semaphores. Data moves between devices by JAX's collectives and lax.ppermute only.
A program may use at most 256 MiB of HBM per device.

```python
import jax
import jax.numpy as jnp
from jax import lax

D = 768
HEADS = 12
HEAD_DIM = 64
FF = 3072
SEQS = 2
LENGTH = 1024
SEQS_ALL = 8
DOC_SHORT = 128
DOC_LONG = 512
DOCS = 9


def draw_segments(key, part):
    key = jax.random.fold_in(key, 11)
    first_key, second_key, third_key = jax.random.split(key, 3)
    doc_lengths = jax.random.randint(first_key, (SEQS_ALL, DOCS), DOC_SHORT, DOC_LONG + 1)
    doc_ends = jnp.cumsum(doc_lengths, axis=1)
    places = jnp.arange(LENGTH, dtype=jnp.int32)
    numbers = jnp.sum((places[None, :, None] >= doc_ends[:, None, :]).astype(jnp.int32), axis=2)
    short_numbers = places // DOC_SHORT
    chosen = jax.random.randint(second_key, (SEQS_ALL // SEQS,), 0, SEQS)
    group_pick = jax.random.randint(third_key, (), 0, SEQS_ALL // SEQS)
    row_index = jnp.arange(SEQS_ALL, dtype=jnp.int32)
    chosen_rows = jnp.repeat(chosen, SEQS)
    single_doc = row_index % SEQS == chosen_rows
    short_row = (row_index % SEQS == (chosen_rows + 1) % SEQS) & (row_index // SEQS == group_pick)
    numbers = jnp.where(short_row[:, None], short_numbers[None, :], numbers)
    return jnp.where(single_doc[:, None], 0, numbers).astype(jnp.int32)


def shard_levels(stream_key, dims, shards, low, high):
    loudness, own = 1.0, jax.random.fold_in(stream_key, 6)
    for dim, shards_of in shards:
        steps = jnp.exp(jax.random.uniform(jax.random.fold_in(own, dim), (shards_of,), jnp.float32, low / len(shards), high / len(shards)))
        loudness = loudness * jnp.repeat(steps, dims[dim] // shards_of).reshape([-1 if axis == dim else 1 for axis in range(len(dims))])
    return loudness


def normal_values(key, extent, deviation, limit, cuts=(), held_as=jnp.bfloat16):
    gain = shard_levels(key, extent, cuts, -0.22, 0.18) if cuts else 1.0
    values = jax.random.normal(key, extent, jnp.float32) * deviation * gain
    return jnp.minimum(jnp.maximum(values, -limit), limit).astype(held_as)


def setup_inputs(seed: int = 0) -> dict:
    keys = jax.random.split(jax.random.key(seed), 17)
    return {
        "tokens": normal_values(keys[0], (SEQS_ALL, LENGTH, D), 1.0, 6.0, ((0, 4), (1, 8))),
        "segments": draw_segments(jax.random.fold_in(keys[16], 71), 0),
        "cotangent": normal_values(keys[2], (SEQS_ALL, LENGTH, D), 1.0, 6.0, ((0, 4), (1, 8))),
        "ln1_gain": jnp.clip(1.0 + 0.1 * jax.random.normal(keys[3], (D,), jnp.float32), 0.5, 1.5).astype(jnp.bfloat16),
        "ln1_bias": normal_values(keys[4], (D,), 0.3, 2.0, ((0, 32),)),
        "w_qkv": normal_values(keys[5], (D, 3 * D), D ** -0.5, 0.21875, ((0, 32),)),
        "bias_query": normal_values(keys[6], (D,), 0.5, 3.0, ((0, 32),)),
        "bias_value": normal_values(keys[7], (D,), 0.5, 3.0, ((0, 32),)),
        "w_out": normal_values(keys[8], (D, D), (D // 64) ** -0.5, 1.75, ((0, 32),)),
        "bias_out": normal_values(keys[9], (D,), 0.5, 3.0, ((0, 32),)),
        "ln2_gain": jnp.clip(1.0 + 0.1 * jax.random.normal(keys[10], (D,), jnp.float32), 0.5, 1.5).astype(jnp.bfloat16),
        "ln2_bias": normal_values(keys[11], (D,), 0.3, 2.0, ((0, 32),)),
        "w_up": normal_values(keys[12], (D, FF), D ** -0.5, 0.21875, ((0, 32),)),
        "bias_up": normal_values(keys[13], (FF,), 0.5, 3.0, ((0, 32),)),
        "w_down": normal_values(keys[14], (FF, D), FF ** -0.5, 0.109375, ((0, 32),)),
        "bias_down": normal_values(keys[15], (D,), 0.5, 3.0, ((0, 32),)),
    }


EPSILON = 1e-05
NEGATIVE = -1e+30
SCALING = 0.125

@jax.custom_vjp
def low(v):
    return lax.optimization_barrier(v.astype(jnp.bfloat16)).astype(jnp.float32)

@jax.custom_vjp
def low_back(v):
    return v

def low_keep(v):
    return (low(v), None)

def low_pass(kept, grad):
    return (grad,)

def back_keep(v):
    return (v, None)

def back_low(kept, grad):
    return (low(grad),)
low.defvjp(low_keep, low_pass)
low_back.defvjp(back_keep, back_low)

def layer_norm(values, gain_vec, shift_vec):
    center = values - lax.optimization_barrier(jnp.mean(values, axis=-1, keepdims=True))
    spread = lax.optimization_barrier(jnp.mean(center * center, axis=-1, keepdims=True))
    return center * lax.rsqrt(spread + EPSILON) * gain_vec + shift_vec

def product(left, right):
    return jnp.dot(left, right, precision=lax.Precision.HIGHEST)

def attend(queries, keys_all, values_all, segment, places):
    length = queries.shape[0]
    block_rows = min(512, length)
    blocks = length // block_rows
    query_blocks = queries.reshape(blocks, block_rows, HEADS, HEAD_DIM)
    seg_blocks = segment.reshape(blocks, block_rows)
    place_blocks = places.reshape(blocks, block_rows)

    def one_block(inputs):
        query_part, seg_part, place_part = inputs
        scores = jnp.einsum('qhd,khd->hqk', query_part, keys_all, precision=lax.Precision.HIGHEST)
        scores = low_back(scores)
        allowed = (seg_part[:, None] == segment[None, :]) & (place_part[:, None] >= places[None, :])
        scores = jnp.where(allowed[None], scores, NEGATIVE)
        row_max = lax.optimization_barrier(jnp.max(scores, axis=-1, keepdims=True))
        expanded = jnp.where(allowed[None], jnp.exp(scores - row_max), 0.0)
        weights = low(expanded / lax.optimization_barrier(jnp.sum(expanded, axis=-1, keepdims=True)))
        return jnp.einsum('hqk,khd->qhd', weights, values_all, precision=lax.Precision.HIGHEST)
    mixed_heads = lax.map(jax.checkpoint(one_block), (query_blocks, seg_blocks, place_blocks))
    return mixed_heads.reshape(length, HEADS * HEAD_DIM)

def forward(params, tokens, segment):
    gain_one, shift_one, w_qkv, bias_query, bias_value, w_out, bias_out, gain_two, shift_two, w_up, bias_up, w_down, bias_down = params
    length = tokens.shape[0]
    model_width = HEADS * HEAD_DIM
    places = jnp.arange(length, dtype=jnp.int32)
    normed = low(layer_norm(tokens, gain_one, shift_one))
    projected = product(normed, w_qkv)
    queries = low_back(low((projected[:, :model_width] + bias_query) * SCALING))
    keys_all = low_back(low(projected[:, model_width:2 * model_width]))
    values_all = low_back(low(projected[:, 2 * model_width:] + bias_value))
    head_shape = (length, HEADS, HEAD_DIM)
    attended = attend(queries.reshape(head_shape), keys_all.reshape(head_shape), values_all.reshape(head_shape), segment, places)
    attended = low_back(low(attended))
    residual = tokens + low_back(product(attended, w_out)) + bias_out
    normed_two = low(layer_norm(residual, gain_two, shift_two))
    hidden = low_back(product(normed_two, w_up) + bias_up)
    active = low(jax.nn.gelu(hidden))
    return residual + product(active, w_down) + bias_down

def reference(tokens, segments, cotangent, ln1_gain, ln1_bias, w_qkv, bias_query, bias_value, w_out, bias_out, ln2_gain, ln2_bias, w_up, bias_up, w_down, bias_down):
    params = tuple((member.astype(jnp.float32) for member in (ln1_gain, ln1_bias, w_qkv, bias_query, bias_value, w_out, bias_out, ln2_gain, ln2_bias, w_up, bias_up, w_down, bias_down)))

    def per_sequence(totals, inputs):
        seq_tokens, seq_segment, seq_cot = inputs

        def forward_only(weights, row_block):
            return forward(weights, row_block, seq_segment)
        result, pullback = jax.vjp(forward_only, params, seq_tokens.astype(jnp.float32))
        grad_params, grad_rows = pullback(seq_cot.astype(jnp.float32))
        totals = jax.tree.map(lambda acc_sum, addend: acc_sum + addend, totals, grad_params)
        return (totals, (result.astype(jnp.bfloat16), grad_rows.astype(jnp.bfloat16)))
    start_totals = jax.tree.map(jnp.zeros_like, params)
    totals, outputs = lax.scan(per_sequence, start_totals, (tokens, segments, cotangent))
    return (outputs[0], outputs[1], totals[0], totals[1], totals[2], totals[3], totals[4], totals[5], totals[6], totals[7], totals[8], totals[9], totals[10], totals[11], totals[12])
```

```python
import functools
import math

import jax
import jax.numpy as jnp
from jax import lax
from jax.experimental import pallas as pl
from jax.experimental.pallas import tpu as pltpu
from jax.sharding import PartitionSpec as P

HEADS = 12
HEAD_DIM = 64


EPSILON = 1e-05
NEGATIVE = -1e30
SCALING = 0.125


def layer_norm(values, gain_vec, shift_vec):
    center = values - jnp.mean(values, axis=-1, keepdims=True)
    spread = jnp.mean(center * center, axis=-1, keepdims=True)
    return center * lax.rsqrt(spread + EPSILON) * gain_vec + shift_vec


def split_heads(tensor):
    return tensor.reshape(tensor.shape[0], tensor.shape[1], HEADS, HEAD_DIM)


def visible(seg_query, seg_key, place_query, place_key):
    same_doc = seg_query[:, :, None] == seg_key[:, None, :]
    causal = place_query[None, :, None] >= place_key[None, None, :]
    return (same_doc & causal)[:, None]


def forward_block(
    carry, query_heads, key_rows, value_rows, seg_query, seg_key, place_query, place_key
):
    row_max, row_sum, acc_out = carry
    scores = jnp.einsum(
        "sqhd,skhd->shqk", query_heads, split_heads(key_rows), preferred_element_type=jnp.float32
    )
    allowed = visible(seg_query, seg_key, place_query, place_key)
    scores = jnp.where(allowed, scores, NEGATIVE)
    new_max = jnp.maximum(row_max, jnp.max(scores, axis=-1))
    expanded = jnp.where(allowed, jnp.exp(scores - new_max[..., None]), 0.0)
    factor = jnp.exp(row_max - new_max)
    row_sum = jnp.sum(expanded, axis=-1)
    added = jnp.einsum(
        "shqk,skhd->sqhd",
        expanded.astype(jnp.bfloat16),
        split_heads(value_rows),
        preferred_element_type=jnp.float32,
    )
    acc_out = acc_out * jnp.swapaxes(factor, 1, 2)[..., None] + added
    return (new_max, row_sum, acc_out)


def grad_block(
    query_heads,
    key_heads,
    value_heads,
    grad_heads,
    log_total,
    delta_sum,
    seg_query,
    seg_key,
    place_query,
    place_key,
):
    scores = jnp.einsum(
        "sqhd,skhd->shqk", query_heads, key_heads, preferred_element_type=jnp.float32
    )
    allowed = visible(seg_query, seg_key, place_query, place_key)
    shift_total = jnp.swapaxes(log_total, 1, 2)[..., None]
    probs = jnp.where(allowed, jnp.exp(scores - shift_total), 0.0)
    grad_probs = jnp.einsum(
        "sqhd,skhd->shqk", grad_heads, value_heads, preferred_element_type=jnp.float32
    )
    grad_scores = (probs * (grad_probs - jnp.swapaxes(delta_sum, 1, 2)[..., None])).astype(
        jnp.bfloat16
    )
    return (grad_scores, probs.astype(jnp.bfloat16))


def query_side(mine, theirs):
    query_heads, grad_heads, log_total, delta_sum, seg_mine, place_mine = mine
    key_rows, value_rows, seg_theirs = theirs
    place_theirs = jnp.arange(key_rows.shape[1], dtype=jnp.int32)
    key_heads = split_heads(key_rows)
    outcome = grad_block(
        query_heads,
        key_heads,
        split_heads(value_rows),
        grad_heads,
        log_total,
        delta_sum,
        seg_mine,
        seg_theirs,
        place_mine,
        place_theirs,
    )
    return jnp.einsum("shqk,skhd->sqhd", outcome[0], key_heads, preferred_element_type=jnp.float32)


def key_side(mine, theirs):
    key_heads, value_heads, seg_mine, place_mine = mine
    query_rows, grad_rows, total_high, total_low, delta_high, delta_low, seg_theirs = theirs
    place_theirs = jnp.arange(query_rows.shape[1], dtype=jnp.int32)
    query_heads = split_heads(query_rows)
    grad_heads = split_heads(grad_rows)
    log_total = total_high.astype(jnp.float32) + total_low.astype(jnp.float32)
    delta_sum = delta_high.astype(jnp.float32) + delta_low.astype(jnp.float32)
    grad_scores, probs = grad_block(
        query_heads,
        key_heads,
        value_heads,
        grad_heads,
        log_total,
        delta_sum,
        seg_theirs,
        seg_mine,
        place_theirs,
        place_mine,
    )
    grad_key = jnp.einsum(
        "shqk,sqhd->skhd", grad_scores, query_heads, preferred_element_type=jnp.float32
    )
    grad_value = jnp.einsum(
        "shqk,sqhd->skhd", probs, grad_heads, preferred_element_type=jnp.float32
    )
    return (grad_key, grad_value)


def contract_rows(left, right):
    return lax.dot_general(
        left, right, (((0,), (0,)), ((), ())), preferred_element_type=jnp.float32
    )


def contract_cols(left, right):
    return lax.dot_general(
        left, right, (((1,), (1,)), ((), ())), preferred_element_type=jnp.float32
    )


def local_general(
    tokens,
    segments,
    cotangent,
    ln1_gain,
    ln1_bias,
    w_qkv,
    bias_query,
    bias_value,
    w_out,
    bias_out,
    ln2_gain,
    ln2_bias,
    w_up,
    bias_up,
    w_down,
    bias_down,
):
    count, span_rows, model_width = tokens.shape
    total_rows = count * span_rows
    places = lax.axis_index("ctx") * span_rows + jnp.arange(span_rows, dtype=jnp.int32)
    gathered = (
        lax.all_gather(ln1_gain, ("dp", "ctx"), axis=0, tiled=True),
        lax.all_gather(ln1_bias, ("dp", "ctx"), axis=0, tiled=True),
        lax.all_gather(w_qkv, ("dp", "ctx"), axis=0, tiled=True),
        lax.all_gather(bias_query, ("dp", "ctx"), axis=0, tiled=True),
        lax.all_gather(bias_value, ("dp", "ctx"), axis=0, tiled=True),
        lax.all_gather(w_out, ("dp", "ctx"), axis=0, tiled=True),
        lax.all_gather(bias_out, ("dp", "ctx"), axis=0, tiled=True),
        lax.all_gather(ln2_gain, ("dp", "ctx"), axis=0, tiled=True),
        lax.all_gather(ln2_bias, ("dp", "ctx"), axis=0, tiled=True),
        lax.all_gather(w_up, ("dp", "ctx"), axis=0, tiled=True),
        lax.all_gather(bias_up, ("dp", "ctx"), axis=0, tiled=True),
        lax.all_gather(w_down, ("dp", "ctx"), axis=0, tiled=True),
        lax.all_gather(bias_down, ("dp", "ctx"), axis=0, tiled=True),
    )
    (
        gain_one,
        shift_one,
        qkv_full,
        query_shift,
        value_shift,
        out_full,
        out_shift,
        gain_two,
        shift_two,
        up_full,
        up_shift,
        down_full,
        down_shift,
    ) = gathered
    flat = tokens.reshape(total_rows, model_width).astype(jnp.float32)
    normed = layer_norm(flat, gain_one.astype(jnp.float32), shift_one.astype(jnp.float32)).astype(
        jnp.bfloat16
    )
    projected = jnp.dot(normed, qkv_full, preferred_element_type=jnp.float32)
    row_shape = (count, span_rows, model_width)
    query_rows = (
        ((projected[:, :model_width] + query_shift.astype(jnp.float32)) * SCALING)
        .astype(jnp.bfloat16)
        .reshape(row_shape)
    )
    key_rows = projected[:, model_width : 2 * model_width].astype(jnp.bfloat16).reshape(row_shape)
    value_rows = (
        (projected[:, 2 * model_width :] + value_shift.astype(jnp.float32))
        .astype(jnp.bfloat16)
        .reshape(row_shape)
    )
    query_heads = split_heads(query_rows)
    start_state = (
        jnp.full((count, HEADS, span_rows), NEGATIVE, jnp.float32),
        jnp.zeros((count, HEADS, span_rows), jnp.float32),
        jnp.zeros((count, span_rows, HEADS, HEAD_DIM), jnp.float32),
    )
    piece_keys = lax.all_gather(key_rows, "ctx", axis=1, tiled=True)
    piece_values = lax.all_gather(value_rows, "ctx", axis=1, tiled=True)
    piece_segs = lax.all_gather(segments, "ctx", axis=1, tiled=True)
    piece_places = jnp.arange(piece_keys.shape[1], dtype=jnp.int32)
    row_max, row_sum, acc_out = forward_block(
        start_state,
        query_heads,
        piece_keys,
        piece_values,
        segments,
        piece_segs,
        places,
        piece_places,
    )
    attended_exact = acc_out / jnp.swapaxes(row_sum, 1, 2)[..., None]
    log_total = jnp.swapaxes(row_max + jnp.log(row_sum), 1, 2)
    attended = attended_exact.reshape(total_rows, model_width).astype(jnp.bfloat16)
    residual = (
        flat
        + jnp.dot(attended, out_full, preferred_element_type=jnp.float32)
        + out_shift.astype(jnp.float32)
    )
    normed_two = layer_norm(
        residual, gain_two.astype(jnp.float32), shift_two.astype(jnp.float32)
    ).astype(jnp.bfloat16)
    hidden = jnp.dot(normed_two, up_full, preferred_element_type=jnp.float32) + up_shift.astype(
        jnp.float32
    )
    active = jax.nn.gelu(hidden).astype(jnp.bfloat16)
    result = (
        residual
        + jnp.dot(active, down_full, preferred_element_type=jnp.float32)
        + down_shift.astype(jnp.float32)
    )
    output = result.astype(jnp.bfloat16).reshape(row_shape)
    regathered = (
        lax.all_gather(ln1_gain, ("dp", "ctx"), axis=0, tiled=True),
        lax.all_gather(ln1_bias, ("dp", "ctx"), axis=0, tiled=True),
        lax.all_gather(w_qkv, ("dp", "ctx"), axis=0, tiled=True),
        lax.all_gather(bias_query, ("dp", "ctx"), axis=0, tiled=True),
        lax.all_gather(bias_value, ("dp", "ctx"), axis=0, tiled=True),
        lax.all_gather(w_out, ("dp", "ctx"), axis=0, tiled=True),
        lax.all_gather(bias_out, ("dp", "ctx"), axis=0, tiled=True),
        lax.all_gather(ln2_gain, ("dp", "ctx"), axis=0, tiled=True),
        lax.all_gather(ln2_bias, ("dp", "ctx"), axis=0, tiled=True),
        lax.all_gather(w_up, ("dp", "ctx"), axis=0, tiled=True),
        lax.all_gather(bias_up, ("dp", "ctx"), axis=0, tiled=True),
        lax.all_gather(w_down, ("dp", "ctx"), axis=0, tiled=True),
        lax.all_gather(bias_down, ("dp", "ctx"), axis=0, tiled=True),
    )
    (
        gain_one,
        shift_one,
        qkv_full,
        query_shift,
        value_shift,
        out_full,
        out_shift,
        gain_two,
        shift_two,
        up_full,
        up_shift,
        down_full,
        down_shift,
    ) = regathered
    upstream = cotangent.reshape(total_rows, model_width)
    upstream_wide = upstream.astype(jnp.float32)
    grad_w_down = contract_rows(active, upstream)
    grad_bias_down = jnp.sum(upstream_wide, axis=0)
    grad_active = contract_cols(upstream, down_full)
    gelu_back = jax.vjp(jax.nn.gelu, hidden)[1]
    grad_hidden = gelu_back(grad_active)[0].astype(jnp.bfloat16)
    grad_bias_up = jnp.sum(grad_hidden.astype(jnp.float32), axis=0)
    grad_w_up = contract_rows(normed_two, grad_hidden)
    grad_normed_two = contract_cols(grad_hidden, up_full)
    norm_two_back = jax.vjp(
        layer_norm, residual, gain_two.astype(jnp.float32), shift_two.astype(jnp.float32)
    )[1]
    grad_from_norm, grad_ln2_gain, grad_ln2_bias = norm_two_back(grad_normed_two)
    grad_residual = upstream_wide + grad_from_norm
    grad_bias_out = jnp.sum(grad_residual, axis=0)
    grad_residual_low = grad_residual.astype(jnp.bfloat16)
    grad_w_out = contract_rows(attended, grad_residual_low)
    grad_attended = (
        contract_cols(grad_residual_low, out_full).astype(jnp.bfloat16).reshape(row_shape)
    )
    grad_heads = split_heads(grad_attended)
    delta_sum = jnp.sum(grad_heads.astype(jnp.float32) * attended_exact, axis=-1)
    total_high = log_total.astype(jnp.bfloat16)
    total_low = (log_total - total_high.astype(jnp.float32)).astype(jnp.bfloat16)
    delta_high = delta_sum.astype(jnp.bfloat16)
    delta_low = (delta_sum - delta_high.astype(jnp.float32)).astype(jnp.bfloat16)
    total_used = total_high.astype(jnp.float32) + total_low.astype(jnp.float32)
    delta_used = delta_high.astype(jnp.float32) + delta_low.astype(jnp.float32)
    key_heads = split_heads(key_rows)
    value_heads = split_heads(value_rows)
    query_mine = (query_heads, grad_heads, total_used, delta_used, segments, places)
    key_mine = (key_heads, value_heads, segments, places)
    grad_query = query_side(
        query_mine,
        (
            lax.all_gather(key_rows, "ctx", axis=1, tiled=True),
            lax.all_gather(value_rows, "ctx", axis=1, tiled=True),
            lax.all_gather(segments, "ctx", axis=1, tiled=True),
        ),
    )
    grad_key, grad_value = key_side(
        key_mine,
        (
            lax.all_gather(query_rows, "ctx", axis=1, tiled=True),
            lax.all_gather(grad_attended, "ctx", axis=1, tiled=True),
            lax.all_gather(total_high, "ctx", axis=1, tiled=True),
            lax.all_gather(total_low, "ctx", axis=1, tiled=True),
            lax.all_gather(delta_high, "ctx", axis=1, tiled=True),
            lax.all_gather(delta_low, "ctx", axis=1, tiled=True),
            lax.all_gather(segments, "ctx", axis=1, tiled=True),
        ),
    )
    query_part = (grad_query.astype(jnp.bfloat16) * SCALING).reshape(total_rows, model_width)
    key_part = grad_key.astype(jnp.bfloat16).reshape(total_rows, model_width)
    value_part = grad_value.astype(jnp.bfloat16).reshape(total_rows, model_width)
    grad_projected = jnp.concatenate([query_part, key_part, value_part], axis=1)
    grad_bias_query = jnp.sum(query_part.astype(jnp.float32), axis=0)
    grad_bias_value = jnp.sum(value_part.astype(jnp.float32), axis=0)
    grad_w_qkv = contract_rows(normed, grad_projected)
    grad_normed = contract_cols(grad_projected, qkv_full)
    norm_one_back = jax.vjp(
        layer_norm, flat, gain_one.astype(jnp.float32), shift_one.astype(jnp.float32)
    )[1]
    grad_from_first, grad_ln1_gain, grad_ln1_bias = norm_one_back(grad_normed)
    grad_tokens = (grad_residual + grad_from_first).astype(jnp.bfloat16).reshape(row_shape)
    owned = (
        lax.psum_scatter(grad_ln1_gain, ("dp", "ctx"), scatter_dimension=0, tiled=True),
        lax.psum_scatter(grad_ln1_bias, ("dp", "ctx"), scatter_dimension=0, tiled=True),
        lax.psum_scatter(grad_w_qkv, ("dp", "ctx"), scatter_dimension=0, tiled=True),
        lax.psum_scatter(grad_bias_query, ("dp", "ctx"), scatter_dimension=0, tiled=True),
        lax.psum_scatter(grad_bias_value, ("dp", "ctx"), scatter_dimension=0, tiled=True),
        lax.psum_scatter(grad_w_out, ("dp", "ctx"), scatter_dimension=0, tiled=True),
        lax.psum_scatter(grad_bias_out, ("dp", "ctx"), scatter_dimension=0, tiled=True),
        lax.psum_scatter(grad_ln2_gain, ("dp", "ctx"), scatter_dimension=0, tiled=True),
        lax.psum_scatter(grad_ln2_bias, ("dp", "ctx"), scatter_dimension=0, tiled=True),
        lax.psum_scatter(grad_w_up, ("dp", "ctx"), scatter_dimension=0, tiled=True),
        lax.psum_scatter(grad_bias_up, ("dp", "ctx"), scatter_dimension=0, tiled=True),
        lax.psum_scatter(grad_w_down, ("dp", "ctx"), scatter_dimension=0, tiled=True),
        lax.psum_scatter(grad_bias_down, ("dp", "ctx"), scatter_dimension=0, tiled=True),
    )
    return (
        output,
        grad_tokens,
        owned[0],
        owned[1],
        owned[2],
        owned[3],
        owned[4],
        owned[5],
        owned[6],
        owned[7],
        owned[8],
        owned[9],
        owned[10],
        owned[11],
        owned[12],
    )


AXES = ("dp", "ctx")
WORK = {
    "attend": 8.0,
    "hidden": 5.5,
    "feed": 4.5,
    "attend_back": 15.0,
    "attend_grad": 2.5,
    "project_out": 2.4,
}
PACE = 1.15e9 * 0.05
LANES = 128
BIG = -1e30
ROOT = math.sqrt(2.0 / math.pi)
CUBIC = 0.044715
F32 = jnp.float32
BF16 = jnp.bfloat16


def dot(left, right, contract=((1,), (0,))):
    return lax.dot_general(left, right, (contract, ((), ())), preferred_element_type=F32)


def normalize(values):
    center = values - jnp.mean(values, axis=-1, keepdims=True)
    factor = lax.rsqrt(jnp.mean(center * center, axis=-1, keepdims=True) + EPSILON)
    return center * factor, factor


def norm_back(grad, normal, factor):
    return factor * (
        grad
        - jnp.mean(grad, axis=-1, keepdims=True)
        - normal * jnp.mean(grad * normal, axis=-1, keepdims=True)
    )


def size_of(shape, dtype):
    lanes = -(-shape[-1] // LANES) * LANES
    rows = -(-shape[-2] // 16) * 16 if len(shape) > 1 else 16
    lead = math.prod(shape[:-2]) if len(shape) > 2 else 1
    return lead * rows * lanes * jnp.dtype(dtype).itemsize


def run(name, body, place, args, outs, scratch=(), flops=0, extra=4 << 20):
    held = sum(size_of(s, d) for s, d in scratch)
    whole = pl.BlockSpec(memory_space=pltpu.VMEM)
    return pl.pallas_call(
        body,
        name=name,
        out_shape=[jax.ShapeDtypeStruct(s, d) for s, d in outs],
        in_specs=[pl.BlockSpec(memory_space=pltpu.SMEM)] + [whole] * len(args),
        out_specs=[whole] * len(outs),
        scratch_shapes=[pltpu.VMEM(s, d) for s, d in scratch],
        compiler_params=pltpu.CompilerParams(vmem_limit_bytes=min(held + extra, 56 << 20)),
        cost_estimate=pl.CostEstimate(
            flops=int(WORK.get(name, 1.5) * PACE), bytes_accessed=1, transcendentals=0
        ),
    )(place, *args)


def rows_at(start, size, align):
    return pl.ds(pl.multiple_of(start, align), size)


class Grid:
    def __init__(self, dp, ctx):
        self.dp, self.ctx = dp, ctx
        self.ny, self.nx, self.nz = 2, dp // 2, ctx // 2

    def move(self, value, step):
        pairs = []
        for i in range(self.dp * self.ctx):
            core, z = i % 2, (i // 2) % self.nz
            x, y = (i // self.ctx) % self.nx, i // (self.ctx * self.nx)
            y, x, z, core = step(y, x, z, core)
            pairs.append((i, ((y * self.nx + x) * self.nz + z) * 2 + core))
        return lax.ppermute(value, AXES, pairs)

    def core(self, value):
        return self.move(value, lambda y, x, z, c: (y, x, z, 1 - c))

    def along_x(self, value):
        return self.move(value, lambda y, x, z, c: (y, 1 - x, z, c))

    def along_y(self, value):
        return self.move(value, lambda y, x, z, c: (1 - y, x, z, c))

    def along_xy(self, value):
        return self.move(value, lambda y, x, z, c: (1 - y, 1 - x, z, c))

    def along_z(self, value, hop):
        return self.move(value, lambda y, x, z, c: (y, x, (z + hop) % self.nz, c))


    def lines(self):
        return [[2 * z + core for z in range(self.nz)] for core in range(2)]

    def gather_z(self, value):
        return lax.all_gather(value, "ctx", axis=0, tiled=True, axis_index_groups=self.lines())

    def gather_chips(self, value):
        count = self.dp * self.ctx
        groups = [list(range(core, count, 2)) for core in range(2)]
        return lax.all_gather(value, AXES, axis=0, tiled=True, axis_index_groups=groups)

    def scatter_z(self, value):
        return lax.psum_scatter(
            value, "ctx", scatter_dimension=0, tiled=True, axis_index_groups=self.lines()
        )


def from_z(z, hop):
    return lax.rem(z - hop + 4, 4)


def order_kernel(place, own, r1, r2, r3, out):
    z = place[2]
    out[z] = own[...]
    out[from_z(z, 1)] = r1[...]
    out[from_z(z, 2)] = r2[...]
    out[from_z(z, 3)] = r3[...]


def block_index(place):
    y, x = place[0], place[1]
    return (2 * y + x, 2 * y + 1 - x, 2 * (1 - y) + x, 2 * (1 - y) + 1 - x)


def fold(block):
    rows = block.shape[0] // 2
    return jnp.concatenate([block[:rows], block[rows:]], axis=1)


def unfold(ref, lanes):
    return jnp.concatenate([ref[:, :lanes], ref[:, lanes:]], axis=0)


def seen(seg_col, seg_row, i, span):
    keys = span * (i + 1)
    same = seg_col[i * span : (i + 1) * span] == seg_row[:, :keys]
    place_q = i * span + lax.broadcasted_iota(jnp.int32, (span, keys), 0)
    place_k = lax.broadcasted_iota(jnp.int32, (span, keys), 1)
    return jnp.where(same & (place_q >= place_k), 0.0, BIG).astype(F32)


def attend_kernel(
    place,
    own,
    other,
    b0,
    bx,
    by,
    bxy,
    seg_row,
    seg_col,
    weight,
    vectors,
    normed,
    rows,
    out,
    exact,
    totals,
    spare,
):
    core, second = place[3], place[2] % 2 == 1
    lines, run_rows, width = own.shape
    group = width // 4
    span = 2 * run_rows
    part = b0.shape[0] * b0.shape[1]
    cut = weight.shape[1]
    for index, piece in zip(block_index(place), (b0, bx, by, bxy)):
        for k in range(piece.shape[0]):
            here = rows_at(index * part + k * piece.shape[1], piece.shape[1], 16)
            weight[here] = piece[k, :, :cut]
    vectors[...] = jnp.transpose(weight[:, 4 * LANES :].astype(F32))[64:80]
    gain, shift = vectors[0:1, :], vectors[1:2, :]
    mine = pl.ds(pl.multiple_of(core * 2 * group, LANES), 2 * group)
    bias_q, bias_v = vectors[2:3, mine], vectors[3:4, mine]
    bias_q = jnp.where(second, bias_q[:, group:], bias_q[:, :group])
    bias_v = jnp.where(second, bias_v[:, group:], bias_v[:, :group])
    for i in range(lines):
        spare[i, rows_at(core * run_rows, run_rows, 16)] = own[i]
        spare[i, rows_at((1 - core) * run_rows, run_rows, 16)] = other[i]
    for i in range(lines):
        here = slice(i * span, (i + 1) * span)
        value = (normalize(spare[i].astype(F32))[0] * gain + shift).astype(BF16)
        normed[here] = value
        projected = dot(value, weight[:, : 3 * group])
        rows[here, :group] = ((projected[:, :group] + bias_q) * SCALING).astype(BF16)
        rows[here, group : 2 * group] = projected[:, group : 2 * group].astype(BF16)
        rows[here, 2 * group :] = (projected[:, 2 * group :] + bias_v).astype(BF16)
    for i in range(lines):
        here = slice(i * span, (i + 1) * span)
        keys = span * (i + 1)
        bias = seen(seg_col, seg_row, i, span)
        heads = []
        for h in range(3):
            at = h * HEAD_DIM
            query = rows[here, at : at + HEAD_DIM]
            key = rows[:keys, group + at : group + at + HEAD_DIM]
            value = rows[:keys, 2 * group + at : 2 * group + at + HEAD_DIM]
            scores = dot(query, key, ((1,), (1,))) + bias
            peak = jnp.max(scores, axis=-1, keepdims=True)
            expanded = jnp.exp(scores - peak)
            total = jnp.sum(expanded, axis=-1, keepdims=True)
            mixed = dot(expanded.astype(BF16), value) / total
            heads.append(mixed.astype(BF16))
            exact[here, at : at + HEAD_DIM] = mixed
            totals[here, h : h + 1] = peak + jnp.log(total)
        out[i] = fold(jnp.concatenate(heads, axis=1))


def out_kernel(place, own, r1, r2, r3, weight, attended, *partial):
    z = place[2]
    span, group = attended.shape[1:]
    attended[z] = unfold(own.at[z], group)
    for hop, piece in ((1, r1), (2, r2), (3, r3)):
        attended[from_z(z, hop)] = unfold(piece, group)
    for s in range(2):
        partial[s][...] = (
            dot(attended[2 * s], weight[:group]) + dot(attended[2 * s + 1], weight[group:])
        ).astype(BF16)


def place_rows(core, target, own, other):
    run_rows = own.shape[0] // 2
    for s in range(2):
        for which, piece in ((core, own), (1 - core, other)):
            target[rows_at((2 * s + which) * run_rows, run_rows, 16)] = piece[
                s * run_rows : (s + 1) * run_rows
            ]


def hidden_kernel(
    place,
    tokens_own,
    tokens_other,
    part_first,
    part_second,
    other_first,
    other_second,
    cot_own,
    cot_other,
    up,
    vectors,
    bias_up,
    cot,
    residual,
    normed,
    active,
    slope,
    tokens,
):
    place_rows(place[3], cot, cot_own, cot_other)
    place_rows(place[3], tokens, tokens_own, tokens_other)
    gain, shift, bias_out = vectors[5:6, :], vectors[6:7, :], vectors[4:5, :]
    span = tokens.shape[0] // 2
    for s in range(2):
        here = slice(s * span, (s + 1) * span)
        one, two = ((part_first, other_first), (part_second, other_second))[s]
        wide = tokens[here].astype(F32) + (one[...].astype(F32) + two[...].astype(F32)) + bias_out
        residual[here] = wide
        low = (normalize(wide)[0] * gain + shift).astype(BF16)
        normed[here] = low
        hidden = dot(low, up[...]) + bias_up[...]
        square = hidden * hidden
        bent = jnp.tanh(ROOT * (hidden + CUBIC * (square * hidden)))
        active[here] = (0.5 * hidden * (1.0 + bent)).astype(BF16)
        slope[here] = 0.5 * (1.0 + bent) + 0.5 * hidden * (1.0 - bent * bent) * (
            ROOT * (1.0 + 3.0 * CUBIC * square)
        )


def down_weights_kernel(place, active, cot, down_own, down_other, spare):
    core = place[3]
    spare[...] = dot(active[...], cot[...], ((0,), (0,))).astype(BF16)
    width = cot.shape[1]
    for which, target in ((core, down_own), (1 - core, down_other)):
        for j in range(8):
            for k in range(2):
                target[48 * j : 48 * j + 48, k * width : (k + 1) * width] = spare[
                    rows_at(192 * j + 96 * which + 48 * k, 48, 16)
                ]


def feed_kernel(
    place,
    residual,
    active,
    slope,
    cot,
    up,
    down,
    grad_hidden,
    result,
    grad_normed,
    low_first,
    low_second,
    sums,
    sum_up,
):
    span = cot.shape[0] // 2
    for s in range(2):
        here = slice(s * span, (s + 1) * span)
        upstream = cot[here]
        grad = (dot(upstream, down[...], ((1,), (1,))) * slope[here]).astype(BF16)
        grad_hidden[here] = grad
        back = dot(grad, up[...], ((1,), (1,)))
        grad_normed[here] = back
        (low_first, low_second)[s][...] = back.astype(BF16)
        result[here] = dot(active[here], down[...])
        rows = jnp.concatenate(
            [
                jnp.sum(back * normalize(residual[here])[0], axis=0, keepdims=True),
                jnp.sum(back, axis=0, keepdims=True),
                0.5 * jnp.sum(upstream.astype(F32), axis=0, keepdims=True),
            ],
            axis=0,
        )
        total = jnp.sum(grad.astype(F32), axis=0, keepdims=True)
        if s == 0:
            sums[...] = rows
            sum_up[...] = total
        else:
            sums[...] = sums[...] + rows
            sum_up[...] = sum_up[...] + total


def up_weights_kernel(place, normed, grad_hidden, grad_up):
    grad_up[...] = dot(normed[...], grad_hidden[...], ((0,), (0,))).astype(BF16)


def attend_grad_kernel(
    place,
    back_own,
    other_first,
    other_second,
    residual,
    cot,
    vectors,
    weight,
    attended,
    grad_residual,
    blocks,
    out_own,
    out_other,
    sum_out,
    spare,
):
    core = place[3]
    gain = vectors[5:6, :]
    span = cot.shape[0] // 2
    group = attended.shape[2]
    half = 2 * group
    products = [None, None]
    for s in range(2):
        here = slice(s * span, (s + 1) * span)
        normal, factor = normalize(residual[here])
        wide = cot[here].astype(F32) + norm_back(
            (back_own[here] + (other_first, other_second)[s][...].astype(F32)) * gain,
            normal,
            factor,
        )
        grad_residual[here] = wide
        low = wide.astype(BF16)
        grad = dot(low, weight[...], ((1,), (1,))).astype(BF16)
        total = 0.5 * jnp.sum(wide, axis=0, keepdims=True)
        sum_out[...] = total if s == 0 else sum_out[...] + total
        for g in range(2):
            blocks[2 * s + g] = fold(grad[:, g * group : (g + 1) * group])
            product = dot(attended[2 * s + g], low, ((0,), (0,)))
            products[g] = product if s == 0 else products[g] + product
    for g in range(2):
        spare[g * group : (g + 1) * group] = products[g].astype(BF16)
    out_own[...] = spare[:, rows_at(core * half, half, LANES)]
    out_other[...] = spare[:, rows_at((1 - core) * half, half, LANES)]


def attend_back_kernel(
    place,
    rows,
    exact,
    totals,
    seg_row,
    seg_col,
    own,
    r1,
    r2,
    r3,
    weight,
    normed,
    tokens_own,
    tokens_other,
    sums,
    o_own,
    o_x,
    o_y,
    o_xy,
    back_own,
    back_first,
    back_second,
    back_third,
    grad,
    keys_grad,
    joined,
    product,
    small,
):
    z, core = place[2], place[3]
    second = z % 2 == 1
    lines, run_rows, width = tokens_own.shape
    span, group = 2 * run_rows, width // 4
    grad[rows_at(z * span, span, span)] = unfold(own.at[z], group)
    for hop, piece in ((1, r1), (2, r2), (3, r3)):
        grad[rows_at(from_z(z, hop) * span, span, span)] = unfold(piece, group)
    for i in (3, 2, 1, 0):
        here = slice(i * span, (i + 1) * span)
        keys = span * (i + 1)
        bias = seen(seg_col, seg_row, i, span)
        for h in range(3):
            at = h * HEAD_DIM
            lanes = slice(at, at + HEAD_DIM)
            query = rows[here, lanes]
            key = rows[:keys, group + at : group + at + HEAD_DIM]
            value = rows[:keys, 2 * group + at : 2 * group + at + HEAD_DIM]
            upstream = grad[here, lanes]
            delta = jnp.sum(upstream.astype(F32) * exact[here, lanes], axis=-1, keepdims=True)
            probs = jnp.exp(dot(query, key, ((1,), (1,))) + bias - totals[here, h : h + 1])
            slopes = dot(upstream, value, ((1,), (1,)))
            grad_scores = (probs * (slopes - delta)).astype(BF16)
            grad_query = dot(grad_scores, key).astype(BF16)
            joined[here, lanes] = (grad_query.astype(F32) * SCALING).astype(BF16)
            grad_key = dot(grad_scores, query, ((0,), (0,)))
            grad_value = dot(probs.astype(BF16), upstream, ((0,), (0,)))
            if i == 3:
                keys_grad[2 * h] = grad_key
                keys_grad[2 * h + 1] = grad_value
            else:
                keys_grad[2 * h, :keys] = keys_grad[2 * h, :keys] + grad_key
                keys_grad[2 * h + 1, :keys] = keys_grad[2 * h + 1, :keys] + grad_value
    for h in range(3):
        for k in range(2):
            at = (k + 1) * group + h * HEAD_DIM
            joined[:, at : at + HEAD_DIM] = keys_grad[2 * h + k].astype(BF16)
    small[...] = jnp.zeros_like(small)
    small[4:16] = sums[4:16]
    mine = pl.ds(pl.multiple_of(core * 2 * group, LANES), 2 * group)
    empty = jnp.zeros((1, group), F32)
    for row, at in ((2, 0), (3, 2 * group)):
        total = jnp.sum(joined[:, at : at + group].astype(F32), axis=0, keepdims=True)
        small[row : row + 1, mine] = jnp.where(
            second,
            jnp.concatenate([empty, total], axis=1),
            jnp.concatenate([total, empty], axis=1),
        )
    for i in range(lines):
        for which, tokens in ((core, tokens_own), (1 - core, tokens_other)):
            here = rows_at(i * span + which * run_rows, run_rows, 16)
            step = dot(joined[here], weight[:, : 3 * group], ((1,), (1,)))
            if tokens is tokens_own:
                back_own[i] = step
            else:
                low = step.astype(BF16)
                for target, start in ((back_first, 0), (back_second, 192), (back_third, 384)):
                    first = max(start, i * run_rows)
                    last = min(start + target.shape[0], (i + 1) * run_rows)
                    if first < last:
                        target[first - start : last - start] = low[
                            first - i * run_rows : last - i * run_rows
                        ]
            normal = normalize(tokens[i].astype(F32))[0]
            small[0:1] = small[0:1] + jnp.sum(step * normal, axis=0, keepdims=True)
            small[1:2] = small[1:2] + jnp.sum(step, axis=0, keepdims=True)
    product[:, : 3 * group] = dot(normed[...], joined[...], ((0,), (0,))).astype(BF16)
    product[:, 3 * group :] = jnp.transpose(small[...])[:, :64].astype(BF16)
    size = o_own.shape[0]
    for index, target in zip(block_index(place), (o_own, o_x, o_y, o_xy)):
        target[...] = product[rows_at(index * size, size, 16)]


def split_kernel(targets, size, block, place):
    y, x = place[0], place[1]
    own, over_x, over_y, low, high = targets
    block(y, x, slice(0, size), own)
    block(y, 1 - x, slice(0, size), over_x)
    block(1 - y, x, slice(0, size), over_y)
    block(1 - y, 1 - x, slice(0, size // 2), low)
    block(1 - y, 1 - x, slice(size // 2, size), high)


def split_down_kernel(place, own, other, *targets):
    core, size = place[3], targets[0].shape[0]

    def block(y, x, rows, target):
        here = rows_at(x * size + rows.start, rows.stop - rows.start, 16)
        target[...] = jnp.where(y == core, own[here], other[here])

    split_kernel(targets, size, block, place)


def split_up_kernel(place, up, out_own, out_other, *targets):
    core, size = place[3], targets[0].shape[0]
    cut = up.shape[1]

    def block(y, x, rows, target):
        count = rows.stop - rows.start
        target[:, :cut] = up[rows_at((2 * y + x) * size + rows.start, count, 16)]
        here = rows_at(x * size + rows.start, count, 16)
        target[:, cut:] = jnp.where(y == core, out_own[here], out_other[here])

    split_kernel(targets, size, block, place)


def collect_kernel(place, over_x, over_y, low, high, sum_x, sum_y):
    half = low.shape[0]
    sum_x[:half] = over_x[:half]
    sum_x[half:] = (over_x[half:].astype(F32) + high[...].astype(F32)).astype(BF16)
    sum_y[:half] = (over_y[:half].astype(F32) + low[...].astype(F32)).astype(BF16)
    sum_y[half:] = over_y[half:]


def add_kernel(place, own, first, second, out):
    out[...] = (own[...].astype(F32) + (first[...].astype(F32) + second[...].astype(F32))).astype(
        BF16
    )


def spread_kernel(place, own, from_x, from_y, low, high, out):
    half = low.shape[0]
    blocks = block_index(place)
    for index, piece in zip(blocks, (own, from_x, from_y)):
        out[index] = piece[...]
    out[blocks[3], :half] = low[...]
    out[blocks[3], half:] = high[...]


def sum_plane_kernel(place, a, b, c, d, own, z1, z2, z3, spare):
    z = place[2]
    spare[...] = (
        (a[...].astype(F32) + b[...].astype(F32)) + (c[...].astype(F32) + d[...].astype(F32))
    ).astype(BF16)
    size = own.shape[0]
    for hop, target in enumerate((own, z1, z2, z3)):
        target[...] = spare[rows_at(lax.rem(z + hop, 4) * size, size, 16)]


def line_qkv_kernel(place, own, r1, r2, r3, out):
    second = place[2] % 2 == 1
    group = out.shape[1] // 2 - LANES // 2
    same = own[...].astype(F32) + r2[...].astype(F32)
    cross = r1[...].astype(F32) + r3[...].astype(F32)
    out[:, :group] = jnp.where(second, cross, same)[:, :group]
    out[:, group : 2 * group] = jnp.where(second, same, cross)[:, :group]
    out[:, 2 * group : 2 * group + 64] = (same + cross)[:, group:]
    out[:, 2 * group + 64 :] = jnp.zeros((out.shape[0], 64), F32)


def out_split_kernel(place, b0, bx, by, bxy, own, other, spare):
    core = place[3]
    first = b0.shape[2] - own.shape[1]
    size = b0.shape[0] * b0.shape[1]
    for index, piece in zip(block_index(place), (b0, bx, by, bxy)):
        for k in range(piece.shape[0]):
            here = rows_at(index * size + k * piece.shape[1], piece.shape[1], 16)
            spare[here] = piece[k, :, first:]
    half = own.shape[0]
    own[...] = spare[rows_at(core * half, half, 16)]
    other[...] = spare[rows_at((1 - core) * half, half, 16)]


def out_halves_kernel(place, own, other, out):
    core = place[3]
    half = out.shape[0]
    for which, piece in ((core, own), (1 - core, other)):
        out[:, rows_at(which * half, half, LANES)] = piece[...]


def down_halves_kernel(place, own, other, down):
    core = place[3]
    width = down.shape[1]
    for which, piece in ((core, own), (1 - core, other)):
        for j in range(8):
            for k in range(2):
                down[rows_at(192 * j + 96 * which + 48 * k, 48, 16)] = piece[
                    48 * j : 48 * j + 48, k * width : (k + 1) * width
                ]


def final_kernel(place, own, r1, r2, r3, grad_residual, tokens, vectors, out, held):
    z, core = place[2], place[3]
    rows = tokens.shape[0] // 2
    held[z] = own[z]
    for hop, piece in ((1, r1), (2, r2), (3, r3)):
        held[from_z(z, hop)] = piece[...]
    gain = vectors[0:1, :]
    for s in range(2):
        here = slice(s * rows, (s + 1) * rows)
        there = rows_at((2 * s + core) * rows, rows, 16)
        normal, factor = normalize(tokens[here].astype(F32))
        grad = (held[2 * s].astype(F32) + held[2 * s + 1].astype(F32)) * gain
        out[here] = (grad_residual[there] + norm_back(grad, normal, factor)).astype(BF16)


def split_local(
    grid,
    tokens,
    segments,
    cotangent,
    ln1_gain,
    ln1_bias,
    w_qkv,
    bias_query,
    bias_value,
    w_out,
    bias_out,
    ln2_gain,
    ln2_bias,
    w_up,
    bias_up,
    w_down,
    bias_down,
):
    count, run_rows, width = tokens.shape
    own_rows = count * run_rows
    all_rows = 2 * own_rows
    span = 2 * run_rows
    half = width // 2
    group = half // 2
    hidden_half = w_up.shape[1] // 2
    shard = w_qkv.shape[0]
    dp, ctx = lax.axis_index("dp"), lax.axis_index("ctx")
    y, x, z, core = dp // grid.nx, dp % grid.nx, ctx // 2, ctx % 2
    place = jnp.stack([y, x, z, core]).astype(jnp.int32)
    first_core = core == 0

    def pick(array, index, axis):
        return lax.dynamic_index_in_dim(array, index, axis, keepdims=False)

    def both(own, other, axis):
        return jnp.where(
            first_core,
            jnp.concatenate([own, other], axis),
            jnp.concatenate([other, own], axis),
        )

    def z_all(value):
        return [value] + [grid.along_z(value, hop) for hop in (1, 2, 3)]

    def after(values, *waited):
        return lax.optimization_barrier((values, waited))[0]

    def z_blocks(blocks):
        return [grid.along_z(pick(blocks, lax.rem(z + hop, 4), 0), hop) for hop in (1, 2, 3)]

    flat = tokens.reshape(own_rows, width)
    small = jnp.stack(
        [ln1_gain, ln1_bias, bias_query, bias_value, bias_out, ln2_gain, ln2_bias, bias_down], axis=1
    )
    lifted = bias_up.reshape(4, shard).T
    seg_lanes = jnp.pad(segments.astype(BF16).reshape(8, 32), ((0, shard - 8), (0, 0)))
    vector_lanes = jnp.concatenate(
        [small, lifted, jnp.zeros((shard, 4), BF16), seg_lanes, jnp.zeros((shard, 16), BF16)],
        axis=1,
    )
    split_qkv = w_qkv.reshape(shard, 3, 2, half)
    split_up = w_up.reshape(shard, 2, hidden_half)
    split_out = w_out.reshape(shard, 2, half)
    cut = 3 * group + 64

    def columns(which):
        chosen = pick(split_qkv, which, 2)
        return jnp.concatenate(
            [
                chosen[:, :, :group].reshape(shard, 3 * group),
                vector_lanes,
                chosen[:, :, group:].reshape(shard, 3 * group),
                vector_lanes,
                pick(split_out, which, 1),
                pick(split_up, which, 1),
            ],
            axis=1,
        )

    piece = both(columns(core), grid.core(columns(1 - core)), 0)
    flat_other = grid.core(flat)
    cot_own = cotangent.reshape(own_rows, width)
    cot_other = grid.core(cot_own)
    second_group = lax.rem(z, 2) == 1
    lanes_out = piece[:, 2 * cut : 2 * cut + half]
    first, last = piece[:, :cut], piece[:, cut : 2 * cut]
    piece_same = jnp.concatenate([jnp.where(second_group, last, first), lanes_out], axis=1)
    piece_cross = jnp.concatenate([jnp.where(second_group, first, last), lanes_out], axis=1)
    line_one = [
        piece_same,
        grid.along_z(piece_cross, 1),
        grid.along_z(piece_same, 2),
        grid.along_z(piece_cross, 3),
    ]
    waiting_tokens = after(tokens, line_one)
    token_pieces = [
        grid.along_z(pick(waiting_tokens, lax.rem(z + hop, 4) // 2, 0), hop) for hop in (1, 2, 3)
    ]
    piece_b = jnp.concatenate([w_down[: 2 * shard], w_down[2 * shard :]], axis=1)

    def order(name, pieces):
        return run(name, order_kernel, place, pieces, [((4,) + pieces[0].shape, BF16)])[0]

    def kernel(name, body, args, outs, scratch=(), extra=4 << 20, **options):
        bound = functools.partial(body, **options) if options else body
        return run(name, bound, place, args, outs, scratch, extra=extra)

    line_one = after(line_one, flat_other, cot_other)
    plane_one = order("order_qkv", line_one)
    from_x, from_y, from_xy = (
        grid.along_x(plane_one),
        grid.along_y(plane_one),
        grid.along_xy(plane_one),
    )
    weight_up = grid.gather_chips(piece[:, 2 * cut + half :])
    token_pieces = after(token_pieces, plane_one)
    gathered = order("order_tokens", [pick(tokens, z // 2, 0)] + token_pieces)
    gathered_other = grid.core(gathered)
    line_b = z_all(after(piece_b, token_pieces))
    segs = plane_one.reshape(4, 2, shard, cut + half)[:, :, :8, 3 * group + 16 : 3 * group + 48]
    segs = segs.reshape(4, 2, 2, 4 * 32).transpose(2, 0, 1, 3).reshape(2, 8 * run_rows)
    segs = pick(segs, z // 2, 0).astype(F32)

    weight_qkv, vectors, normed, packed, out_blocks, exact, totals = kernel(
        "attend",
        attend_kernel,
        [
            gathered,
            gathered_other,
            plane_one,
            from_x,
            from_y,
            from_xy,
            segs.reshape(1, -1),
            segs.reshape(-1, 1),
        ],
        [
            ((width, cut), BF16),
            ((16, width), F32),
            ((4 * span, width), BF16),
            ((4 * span, 3 * group), BF16),
            ((4, run_rows, 2 * group), BF16),
            ((4 * span, group), F32),
            ((4 * span, LANES), F32),
        ],
        [((4, span, width), BF16)],
        extra=14 << 20,
    )
    out_pieces = z_blocks(out_blocks)

    weight_out = kernel(
        "out_split",
        out_split_kernel,
        [plane_one, from_x, from_y, from_xy],
        [((half, half), BF16)] * 2,
        [((width, half), BF16)],
    )
    weight_out = kernel(
        "out_halves",
        out_halves_kernel,
        [weight_out[0], grid.core(weight_out[1])],
        [((half, width), BF16)],
    )[0]

    def spread(name, plane, over, when):
        size = plane.shape[0] // 2
        low, high = grid.along_x(over[1][:size]), grid.along_y(over[0][size:])
        return kernel(
            name,
            spread_kernel,
            [plane, *over, *after((low, high), when)],
            [((4,) + plane.shape, BF16)],
        )[0]

    plane_b = order("order_b", after(line_b, out_blocks)).reshape(8 * shard, 2 * width)
    out_pieces = after(out_pieces, plane_b)
    bias_up_half = lax.dynamic_slice_in_dim(
        vectors[8:12].reshape(4, 4 * 8, shard).transpose(1, 0, 2).reshape(1, 2 * hidden_half),
        core * hidden_half,
        hidden_half,
        axis=1,
    )
    attended, *partial = kernel(
        "project_out",
        out_kernel,
        [out_blocks] + out_pieces + [weight_out],
        [((4, span, group), BF16)] + [((own_rows, width), BF16)] * 2,
    )
    over_b = after((grid.along_x(plane_b), grid.along_y(plane_b)), partial)
    cot, residual, normed_two, active, slope = kernel(
        "hidden",
        hidden_kernel,
        [
            flat,
            flat_other,
            *partial,
            *[grid.core(member) for member in partial],
            cot_own,
            cot_other,
            after(weight_up, over_b),
            vectors,
            bias_up_half,
        ],
        [
            ((all_rows, width), BF16),
            ((all_rows, width), F32),
            ((all_rows, width), BF16),
            ((all_rows, hidden_half), BF16),
            ((all_rows, hidden_half), F32),
        ],
        [((all_rows, width), BF16)],
        extra=14 << 20,
    )
    down_own, down_other = kernel(
        "down_weights",
        down_weights_kernel,
        [active, cot],
        [((half, 2 * width), BF16)] * 2,
        [((hidden_half, width), BF16)],
        extra=10 << 20,
    )
    down_recv = grid.core(down_other)
    mixed_down = spread("spread_down", plane_b, over_b, down_own).reshape(2, half, 2 * width)
    weight_down = kernel(
        "down_halves",
        down_halves_kernel,
        [pick(mixed_down, core, 0), grid.core(pick(mixed_down, 1 - core, 0))],
        [((hidden_half, width), BF16)],
    )[0]

    def halve(array, which):
        return pick(array.reshape(2, 2, run_rows, width), which, 1).reshape(own_rows, width)

    size = 8 * shard

    def split(name, body, parts, lanes):
        return kernel(
            name, body, parts, [((size, lanes), BF16)] * 3 + [((size // 2, lanes), BF16)] * 2
        )

    def diagonal(parts):
        return grid.along_x(parts[3]), grid.along_y(parts[4])

    def collect(name, parts, low, high):
        sum_x, sum_y = kernel(
            name, collect_kernel, [parts[1], parts[2], low, high], [(parts[1].shape, BF16)] * 2
        )
        return parts[0], grid.along_x(sum_x), grid.along_y(sum_y), sum_x

    def finish(name, parts):
        total = kernel(name, add_kernel, parts, [(parts[0].shape, BF16)])[0]
        return grid.scatter_z(total).astype(F32)

    down_parts = split("split_down", split_down_kernel, [down_own, down_recv], 2 * width)
    down_low, down_high = diagonal(down_parts)
    grad_hidden, result, back_two, *back_low, sums_two, sum_up = kernel(
        "feed",
        feed_kernel,
        after([residual, active, slope, cot, weight_up, weight_down], down_parts),
        [
            ((all_rows, hidden_half), BF16),
            ((all_rows, width), F32),
            ((all_rows, width), F32),
            ((own_rows, width), BF16),
            ((own_rows, width), BF16),
            ((3, width), F32),
            ((1, hidden_half), F32),
        ],
        extra=14 << 20,
    )
    back_other = [grid.core(member) for member in back_low]
    result_other = grid.core(halve(result, 1 - core))
    grad_up = kernel(
        "up_weights",
        up_weights_kernel,
        [normed_two, grad_hidden],
        [((width, hidden_half), BF16)],
        extra=10 << 20,
    )[0]

    output = (
        halve(residual, core)
        + (halve(result, core) + result_other)
        + vectors[7:8]
    ).astype(BF16)

    grad_residual, grad_blocks, out_own, out_other, sum_out = kernel(
        "attend_grad",
        attend_grad_kernel,
        after(
            [back_two, *back_other, residual, cot, vectors, weight_out, attended],
            grad_up,
            result_other,
        ),
        [
            ((all_rows, width), F32),
            ((4, run_rows, 2 * group), BF16),
            ((half, half), BF16),
            ((half, half), BF16),
            ((1, width), F32),
        ],
        [((half, width), BF16)],
    )
    grad_pieces = z_blocks(grad_blocks)
    out_recv = grid.core(out_other)
    down_low, down_high = after((down_low, down_high), grad_blocks)
    down_parts = collect("collect_down", down_parts, down_low, down_high)

    up_parts = split("split_up", split_up_kernel, [grad_up, out_own, out_recv], hidden_half + half)
    up_low, up_high = diagonal(up_parts)

    lifted_sum = jnp.where(
        first_core,
        jnp.concatenate([sum_up, jnp.zeros_like(sum_up)], axis=1),
        jnp.concatenate([jnp.zeros_like(sum_up), sum_up], axis=1),
    )
    lifted_rows = lifted_sum.reshape(32, 4, shard).transpose(1, 0, 2).reshape(4, width)
    sums = jnp.concatenate(
        [jnp.zeros((4, width), F32), sum_out, sums_two, lifted_rows, jnp.zeros((4, width), F32)],
        axis=0,
    )
    grad_pieces = after(grad_pieces, up_parts, down_parts[3])
    back_results = kernel(
        "attend_back",
        attend_back_kernel,
        [packed, exact, totals, segs.reshape(1, -1), segs.reshape(-1, 1), grad_blocks]
        + grad_pieces
        + [weight_qkv, normed, gathered, gathered_other, sums],
        [((size, cut), BF16)] * 4
        + [((4, run_rows, width), F32)]
        + [((192, width), BF16), ((192, width), BF16), ((128, width), BF16)],
        [
            ((4 * span, group), BF16),
            ((6, 4 * span, HEAD_DIM), F32),
            ((4 * span, 3 * group), BF16),
            ((width, cut), BF16),
            ((LANES, width), F32),
        ],
        extra=14 << 20,
    )
    qkv_parts, back_own, back_low = back_results[:4], back_results[4], back_results[5:]
    back_recv = jnp.concatenate([grid.core(member) for member in back_low], axis=0)
    back_sum = (back_own + back_recv.reshape(back_own.shape).astype(F32)).astype(BF16)
    back_pieces = z_blocks(back_sum)
    qkv_recv = [grid.along_x(qkv_parts[1]), grid.along_y(qkv_parts[2]), grid.along_xy(qkv_parts[3])]

    up_low, up_high = after((up_low, up_high), back_own)
    up_parts = collect("collect_up", up_parts, up_low, up_high)
    down_sum = finish("finish_down", after(list(down_parts[:3]), up_parts[3]))
    qkv_own, *qkv_sends = kernel(
        "plane_qkv",
        sum_plane_kernel,
        [qkv_parts[0]] + after(qkv_recv, back_sum),
        [((2 * shard, cut), BF16)] * 4,
        [((size, cut), BF16)],
    )
    up_sum = finish("finish_up", after(list(up_parts[:3]), qkv_own))
    qkv_line = [qkv_own] + [grid.along_z(qkv_sends[hop - 1], hop) for hop in (1, 2, 3)]
    qkv_sum = kernel(
        "line_qkv", line_qkv_kernel, qkv_line, [((2 * shard, 6 * group + LANES), F32)]
    )[0]
    grad_tokens = kernel(
        "final",
        final_kernel,
        [back_sum] + back_pieces + [grad_residual, flat, vectors],
        [((own_rows, width), BF16)],
        [((4, run_rows, width), BF16)],
    )[0]
    def rows_of(array, which):
        return lax.dynamic_slice_in_dim(array, which * shard, shard, axis=0)

    def exchange(array):
        return rows_of(array, core), grid.core(rows_of(array, 1 - core))

    grad_down = jnp.concatenate([down_sum[:, :width], down_sum[:, width:]], axis=0)
    up_mine, up_theirs = exchange(up_sum)
    grad_up_own = both(up_mine[:, :hidden_half], up_theirs[:, :hidden_half], 1)
    grad_out_own = both(up_mine[:, hidden_half:], up_theirs[:, hidden_half:], 1)
    qkv_mine, qkv_theirs = exchange(qkv_sum)
    grad_qkv_own = both(
        *[
            part[:, : 6 * group].reshape(shard, 2, 3, group).transpose(0, 2, 1, 3)[:, :, None]
            for part in (qkv_mine, qkv_theirs)
        ],
        2,
    ).reshape(shard, 6 * half)
    small_sum = (qkv_mine[:, 6 * group : 6 * group + 16] + qkv_theirs[:, 6 * group : 6 * group + 16]).T
    return (
        output.reshape(tokens.shape),
        grad_tokens.reshape(tokens.shape),
        small_sum[0],
        small_sum[1],
        grad_qkv_own,
        small_sum[2],
        small_sum[3],
        grad_out_own,
        small_sum[4],
        small_sum[5],
        small_sum[6],
        grad_up_own,
        small_sum[8:12].reshape(4 * shard),
        grad_down,
        small_sum[7],
    )


def build_local(mesh):
    dp, ctx = mesh.shape["dp"], mesh.shape["ctx"]
    if (dp, ctx) != (4, 8):
        return local_general
    grid = Grid(dp, ctx)
    return lambda *args: split_local(grid, *args)


def solution(mesh):
    return jax.shard_map(
        build_local(mesh),
        mesh=mesh,
        in_specs=(
            P("dp", "ctx", None),
            P("dp", "ctx"),
            P("dp", "ctx", None),
            P(("dp", "ctx")),
            P(("dp", "ctx")),
            P(("dp", "ctx"), None),
            P(("dp", "ctx")),
            P(("dp", "ctx")),
            P(("dp", "ctx"), None),
            P(("dp", "ctx")),
            P(("dp", "ctx")),
            P(("dp", "ctx")),
            P(("dp", "ctx"), None),
            P(("dp", "ctx")),
            P(("dp", "ctx"), None),
            P(("dp", "ctx")),
        ),
        out_specs=(
            P("dp", "ctx", None),
            P("dp", "ctx", None),
            P(("dp", "ctx")),
            P(("dp", "ctx")),
            P(("dp", "ctx"), None),
            P(("dp", "ctx")),
            P(("dp", "ctx")),
            P(("dp", "ctx"), None),
            P(("dp", "ctx")),
            P(("dp", "ctx")),
            P(("dp", "ctx")),
            P(("dp", "ctx"), None),
            P(("dp", "ctx")),
            P(("dp", "ctx"), None),
            P(("dp", "ctx")),
        ),
        check_vma=False,
    )
```

```python
import functools
import math

import jax
import jax.numpy as jnp
from jax import lax
from jax.experimental import pallas as pl
from jax.experimental.pallas import tpu as pltpu
from jax.sharding import PartitionSpec as P

HEADS = 12
HEAD_DIM = 64


EPSILON = 1e-05
NEGATIVE = -1e30
SCALING = 0.125


def layer_norm(values, gain_vec, shift_vec):
    center = values - jnp.mean(values, axis=-1, keepdims=True)
    spread = jnp.mean(center * center, axis=-1, keepdims=True)
    return center * lax.rsqrt(spread + EPSILON) * gain_vec + shift_vec


def split_heads(tensor):
    return tensor.reshape(tensor.shape[0], tensor.shape[1], HEADS, HEAD_DIM)


def visible(seg_query, seg_key, place_query, place_key):
    same_doc = seg_query[:, :, None] == seg_key[:, None, :]
    causal = place_query[None, :, None] >= place_key[None, None, :]
    return (same_doc & causal)[:, None]


def forward_block(
    carry, query_heads, key_rows, value_rows, seg_query, seg_key, place_query, place_key
):
    row_max, row_sum, acc_out = carry
    scores = jnp.einsum(
        "sqhd,skhd->shqk", query_heads, split_heads(key_rows), preferred_element_type=jnp.float32
    )
    allowed = visible(seg_query, seg_key, place_query, place_key)
    scores = jnp.where(allowed, scores, NEGATIVE)
    new_max = jnp.maximum(row_max, jnp.max(scores, axis=-1))
    expanded = jnp.where(allowed, jnp.exp(scores - new_max[..., None]), 0.0)
    factor = jnp.exp(row_max - new_max)
    row_sum = jnp.sum(expanded, axis=-1)
    added = jnp.einsum(
        "shqk,skhd->sqhd",
        expanded.astype(jnp.bfloat16),
        split_heads(value_rows),
        preferred_element_type=jnp.float32,
    )
    acc_out = acc_out * jnp.swapaxes(factor, 1, 2)[..., None] + added
    return (new_max, row_sum, acc_out)


def grad_block(
    query_heads,
    key_heads,
    value_heads,
    grad_heads,
    log_total,
    delta_sum,
    seg_query,
    seg_key,
    place_query,
    place_key,
):
    scores = jnp.einsum(
        "sqhd,skhd->shqk", query_heads, key_heads, preferred_element_type=jnp.float32
    )
    allowed = visible(seg_query, seg_key, place_query, place_key)
    shift_total = jnp.swapaxes(log_total, 1, 2)[..., None]
    probs = jnp.where(allowed, jnp.exp(scores - shift_total), 0.0)
    grad_probs = jnp.einsum(
        "sqhd,skhd->shqk", grad_heads, value_heads, preferred_element_type=jnp.float32
    )
    grad_scores = (probs * (grad_probs - jnp.swapaxes(delta_sum, 1, 2)[..., None])).astype(
        jnp.bfloat16
    )
    return (grad_scores, probs.astype(jnp.bfloat16))


def query_side(mine, theirs):
    query_heads, grad_heads, log_total, delta_sum, seg_mine, place_mine = mine
    key_rows, value_rows, seg_theirs = theirs
    place_theirs = jnp.arange(key_rows.shape[1], dtype=jnp.int32)
    key_heads = split_heads(key_rows)
    outcome = grad_block(
        query_heads,
        key_heads,
        split_heads(value_rows),
        grad_heads,
        log_total,
        delta_sum,
        seg_mine,
        seg_theirs,
        place_mine,
        place_theirs,
    )
    return jnp.einsum("shqk,skhd->sqhd", outcome[0], key_heads, preferred_element_type=jnp.float32)


def key_side(mine, theirs):
    key_heads, value_heads, seg_mine, place_mine = mine
    query_rows, grad_rows, total_high, total_low, delta_high, delta_low, seg_theirs = theirs
    place_theirs = jnp.arange(query_rows.shape[1], dtype=jnp.int32)
    query_heads = split_heads(query_rows)
    grad_heads = split_heads(grad_rows)
    log_total = total_high.astype(jnp.float32) + total_low.astype(jnp.float32)
    delta_sum = delta_high.astype(jnp.float32) + delta_low.astype(jnp.float32)
    grad_scores, probs = grad_block(
        query_heads,
        key_heads,
        value_heads,
        grad_heads,
        log_total,
        delta_sum,
        seg_theirs,
        seg_mine,
        place_theirs,
        place_mine,
    )
    grad_key = jnp.einsum(
        "shqk,sqhd->skhd", grad_scores, query_heads, preferred_element_type=jnp.float32
    )
    grad_value = jnp.einsum(
        "shqk,sqhd->skhd", probs, grad_heads, preferred_element_type=jnp.float32
    )
    return (grad_key, grad_value)


def contract_rows(left, right):
    return lax.dot_general(
        left, right, (((0,), (0,)), ((), ())), preferred_element_type=jnp.float32
    )


def contract_cols(left, right):
    return lax.dot_general(
        left, right, (((1,), (1,)), ((), ())), preferred_element_type=jnp.float32
    )


def local_general(
    tokens,
    segments,
    cotangent,
    ln1_gain,
    ln1_bias,
    w_qkv,
    bias_query,
    bias_value,
    w_out,
    bias_out,
    ln2_gain,
    ln2_bias,
    w_up,
    bias_up,
    w_down,
    bias_down,
):
    count, span_rows, model_width = tokens.shape
    total_rows = count * span_rows
    places = lax.axis_index("ctx") * span_rows + jnp.arange(span_rows, dtype=jnp.int32)
    gathered = (
        lax.all_gather(ln1_gain, ("dp", "ctx"), axis=0, tiled=True),
        lax.all_gather(ln1_bias, ("dp", "ctx"), axis=0, tiled=True),
        lax.all_gather(w_qkv, ("dp", "ctx"), axis=0, tiled=True),
        lax.all_gather(bias_query, ("dp", "ctx"), axis=0, tiled=True),
        lax.all_gather(bias_value, ("dp", "ctx"), axis=0, tiled=True),
        lax.all_gather(w_out, ("dp", "ctx"), axis=0, tiled=True),
        lax.all_gather(bias_out, ("dp", "ctx"), axis=0, tiled=True),
        lax.all_gather(ln2_gain, ("dp", "ctx"), axis=0, tiled=True),
        lax.all_gather(ln2_bias, ("dp", "ctx"), axis=0, tiled=True),
        lax.all_gather(w_up, ("dp", "ctx"), axis=0, tiled=True),
        lax.all_gather(bias_up, ("dp", "ctx"), axis=0, tiled=True),
        lax.all_gather(w_down, ("dp", "ctx"), axis=0, tiled=True),
        lax.all_gather(bias_down, ("dp", "ctx"), axis=0, tiled=True),
    )
    (
        gain_one,
        shift_one,
        qkv_full,
        query_shift,
        value_shift,
        out_full,
        out_shift,
        gain_two,
        shift_two,
        up_full,
        up_shift,
        down_full,
        down_shift,
    ) = gathered
    flat = tokens.reshape(total_rows, model_width).astype(jnp.float32)
    normed = layer_norm(flat, gain_one.astype(jnp.float32), shift_one.astype(jnp.float32)).astype(
        jnp.bfloat16
    )
    projected = jnp.dot(normed, qkv_full, preferred_element_type=jnp.float32)
    row_shape = (count, span_rows, model_width)
    query_rows = (
        ((projected[:, :model_width] + query_shift.astype(jnp.float32)) * SCALING)
        .astype(jnp.bfloat16)
        .reshape(row_shape)
    )
    key_rows = projected[:, model_width : 2 * model_width].astype(jnp.bfloat16).reshape(row_shape)
    value_rows = (
        (projected[:, 2 * model_width :] + value_shift.astype(jnp.float32))
        .astype(jnp.bfloat16)
        .reshape(row_shape)
    )
    query_heads = split_heads(query_rows)
    start_state = (
        jnp.full((count, HEADS, span_rows), NEGATIVE, jnp.float32),
        jnp.zeros((count, HEADS, span_rows), jnp.float32),
        jnp.zeros((count, span_rows, HEADS, HEAD_DIM), jnp.float32),
    )
    piece_keys = lax.all_gather(key_rows, "ctx", axis=1, tiled=True)
    piece_values = lax.all_gather(value_rows, "ctx", axis=1, tiled=True)
    piece_segs = lax.all_gather(segments, "ctx", axis=1, tiled=True)
    piece_places = jnp.arange(piece_keys.shape[1], dtype=jnp.int32)
    row_max, row_sum, acc_out = forward_block(
        start_state,
        query_heads,
        piece_keys,
        piece_values,
        segments,
        piece_segs,
        places,
        piece_places,
    )
    attended_exact = acc_out / jnp.swapaxes(row_sum, 1, 2)[..., None]
    log_total = jnp.swapaxes(row_max + jnp.log(row_sum), 1, 2)
    attended = attended_exact.reshape(total_rows, model_width).astype(jnp.bfloat16)
    residual = (
        flat
        + jnp.dot(attended, out_full, preferred_element_type=jnp.float32)
        + out_shift.astype(jnp.float32)
    )
    normed_two = layer_norm(
        residual, gain_two.astype(jnp.float32), shift_two.astype(jnp.float32)
    ).astype(jnp.bfloat16)
    hidden = jnp.dot(normed_two, up_full, preferred_element_type=jnp.float32) + up_shift.astype(
        jnp.float32
    )
    active = jax.nn.gelu(hidden).astype(jnp.bfloat16)
    result = (
        residual
        + jnp.dot(active, down_full, preferred_element_type=jnp.float32)
        + down_shift.astype(jnp.float32)
    )
    output = result.astype(jnp.bfloat16).reshape(row_shape)
    regathered = (
        lax.all_gather(ln1_gain, ("dp", "ctx"), axis=0, tiled=True),
        lax.all_gather(ln1_bias, ("dp", "ctx"), axis=0, tiled=True),
        lax.all_gather(w_qkv, ("dp", "ctx"), axis=0, tiled=True),
        lax.all_gather(bias_query, ("dp", "ctx"), axis=0, tiled=True),
        lax.all_gather(bias_value, ("dp", "ctx"), axis=0, tiled=True),
        lax.all_gather(w_out, ("dp", "ctx"), axis=0, tiled=True),
        lax.all_gather(bias_out, ("dp", "ctx"), axis=0, tiled=True),
        lax.all_gather(ln2_gain, ("dp", "ctx"), axis=0, tiled=True),
        lax.all_gather(ln2_bias, ("dp", "ctx"), axis=0, tiled=True),
        lax.all_gather(w_up, ("dp", "ctx"), axis=0, tiled=True),
        lax.all_gather(bias_up, ("dp", "ctx"), axis=0, tiled=True),
        lax.all_gather(w_down, ("dp", "ctx"), axis=0, tiled=True),
        lax.all_gather(bias_down, ("dp", "ctx"), axis=0, tiled=True),
    )
    (
        gain_one,
        shift_one,
        qkv_full,
        query_shift,
        value_shift,
        out_full,
        out_shift,
        gain_two,
        shift_two,
        up_full,
        up_shift,
        down_full,
        down_shift,
    ) = regathered
    upstream = cotangent.reshape(total_rows, model_width)
    upstream_wide = upstream.astype(jnp.float32)
    grad_w_down = contract_rows(active, upstream)
    grad_bias_down = jnp.sum(upstream_wide, axis=0)
    grad_active = contract_cols(upstream, down_full)
    gelu_back = jax.vjp(jax.nn.gelu, hidden)[1]
    grad_hidden = gelu_back(grad_active)[0].astype(jnp.bfloat16)
    grad_bias_up = jnp.sum(grad_hidden.astype(jnp.float32), axis=0)
    grad_w_up = contract_rows(normed_two, grad_hidden)
    grad_normed_two = contract_cols(grad_hidden, up_full)
    norm_two_back = jax.vjp(
        layer_norm, residual, gain_two.astype(jnp.float32), shift_two.astype(jnp.float32)
    )[1]
    grad_from_norm, grad_ln2_gain, grad_ln2_bias = norm_two_back(grad_normed_two)
    grad_residual = upstream_wide + grad_from_norm
    grad_bias_out = jnp.sum(grad_residual, axis=0)
    grad_residual_low = grad_residual.astype(jnp.bfloat16)
    grad_w_out = contract_rows(attended, grad_residual_low)
    grad_attended = (
        contract_cols(grad_residual_low, out_full).astype(jnp.bfloat16).reshape(row_shape)
    )
    grad_heads = split_heads(grad_attended)
    delta_sum = jnp.sum(grad_heads.astype(jnp.float32) * attended_exact, axis=-1)
    total_high = log_total.astype(jnp.bfloat16)
    total_low = (log_total - total_high.astype(jnp.float32)).astype(jnp.bfloat16)
    delta_high = delta_sum.astype(jnp.bfloat16)
    delta_low = (delta_sum - delta_high.astype(jnp.float32)).astype(jnp.bfloat16)
    total_used = total_high.astype(jnp.float32) + total_low.astype(jnp.float32)
    delta_used = delta_high.astype(jnp.float32) + delta_low.astype(jnp.float32)
    key_heads = split_heads(key_rows)
    value_heads = split_heads(value_rows)
    query_mine = (query_heads, grad_heads, total_used, delta_used, segments, places)
    key_mine = (key_heads, value_heads, segments, places)
    grad_query = query_side(
        query_mine,
        (
            lax.all_gather(key_rows, "ctx", axis=1, tiled=True),
            lax.all_gather(value_rows, "ctx", axis=1, tiled=True),
            lax.all_gather(segments, "ctx", axis=1, tiled=True),
        ),
    )
    grad_key, grad_value = key_side(
        key_mine,
        (
            lax.all_gather(query_rows, "ctx", axis=1, tiled=True),
            lax.all_gather(grad_attended, "ctx", axis=1, tiled=True),
            lax.all_gather(total_high, "ctx", axis=1, tiled=True),
            lax.all_gather(total_low, "ctx", axis=1, tiled=True),
            lax.all_gather(delta_high, "ctx", axis=1, tiled=True),
            lax.all_gather(delta_low, "ctx", axis=1, tiled=True),
            lax.all_gather(segments, "ctx", axis=1, tiled=True),
        ),
    )
    query_part = (grad_query.astype(jnp.bfloat16) * SCALING).reshape(total_rows, model_width)
    key_part = grad_key.astype(jnp.bfloat16).reshape(total_rows, model_width)
    value_part = grad_value.astype(jnp.bfloat16).reshape(total_rows, model_width)
    grad_projected = jnp.concatenate([query_part, key_part, value_part], axis=1)
    grad_bias_query = jnp.sum(query_part.astype(jnp.float32), axis=0)
    grad_bias_value = jnp.sum(value_part.astype(jnp.float32), axis=0)
    grad_w_qkv = contract_rows(normed, grad_projected)
    grad_normed = contract_cols(grad_projected, qkv_full)
    norm_one_back = jax.vjp(
        layer_norm, flat, gain_one.astype(jnp.float32), shift_one.astype(jnp.float32)
    )[1]
    grad_from_first, grad_ln1_gain, grad_ln1_bias = norm_one_back(grad_normed)
    grad_tokens = (grad_residual + grad_from_first).astype(jnp.bfloat16).reshape(row_shape)
    owned = (
        lax.psum_scatter(grad_ln1_gain, ("dp", "ctx"), scatter_dimension=0, tiled=True),
        lax.psum_scatter(grad_ln1_bias, ("dp", "ctx"), scatter_dimension=0, tiled=True),
        lax.psum_scatter(grad_w_qkv, ("dp", "ctx"), scatter_dimension=0, tiled=True),
        lax.psum_scatter(grad_bias_query, ("dp", "ctx"), scatter_dimension=0, tiled=True),
        lax.psum_scatter(grad_bias_value, ("dp", "ctx"), scatter_dimension=0, tiled=True),
        lax.psum_scatter(grad_w_out, ("dp", "ctx"), scatter_dimension=0, tiled=True),
        lax.psum_scatter(grad_bias_out, ("dp", "ctx"), scatter_dimension=0, tiled=True),
        lax.psum_scatter(grad_ln2_gain, ("dp", "ctx"), scatter_dimension=0, tiled=True),
        lax.psum_scatter(grad_ln2_bias, ("dp", "ctx"), scatter_dimension=0, tiled=True),
        lax.psum_scatter(grad_w_up, ("dp", "ctx"), scatter_dimension=0, tiled=True),
        lax.psum_scatter(grad_bias_up, ("dp", "ctx"), scatter_dimension=0, tiled=True),
        lax.psum_scatter(grad_w_down, ("dp", "ctx"), scatter_dimension=0, tiled=True),
        lax.psum_scatter(grad_bias_down, ("dp", "ctx"), scatter_dimension=0, tiled=True),
    )
    return (
        output,
        grad_tokens,
        owned[0],
        owned[1],
        owned[2],
        owned[3],
        owned[4],
        owned[5],
        owned[6],
        owned[7],
        owned[8],
        owned[9],
        owned[10],
        owned[11],
        owned[12],
    )


AXES = ("dp", "ctx")
WORK = {
    "attend": 8.0,
    "hidden": 5.5,
    "feed": 4.5,
    "attend_back": 10.0,
    "project_back": 5.0,
    "attend_grad": 2.5,
    "project_out": 2.4,
}
PACE = 1.15e9 * 0.01
LANES = 128
BIG = -1e30
ROOT = math.sqrt(2.0 / math.pi)
CUBIC = 0.044715
F32 = jnp.float32
BF16 = jnp.bfloat16


def dot(left, right, contract=((1,), (0,))):
    return lax.dot_general(left, right, (contract, ((), ())), preferred_element_type=F32)


def normalize(values):
    center = values - jnp.mean(values, axis=-1, keepdims=True)
    factor = lax.rsqrt(jnp.mean(center * center, axis=-1, keepdims=True) + EPSILON)
    return center * factor, factor


def norm_back(grad, normal, factor):
    return factor * (
        grad
        - jnp.mean(grad, axis=-1, keepdims=True)
        - normal * jnp.mean(grad * normal, axis=-1, keepdims=True)
    )


def size_of(shape, dtype):
    lanes = -(-shape[-1] // LANES) * LANES
    rows = -(-shape[-2] // 16) * 16 if len(shape) > 1 else 16
    lead = math.prod(shape[:-2]) if len(shape) > 2 else 1
    return lead * rows * lanes * jnp.dtype(dtype).itemsize


def run(name, body, place, args, outs, scratch=(), far=(), extra=8 << 20):
    held = sum(size_of(s, d) for s, d in scratch)
    held += sum(size_of(args[i].shape, args[i].dtype) for i in far)
    held += sum(size_of(s, d) for s, d in outs)
    whole = pl.BlockSpec(memory_space=pltpu.VMEM)
    specs = [pl.BlockSpec(memory_space=pltpu.HBM) if i in far else whole for i in range(len(args))]
    buffers = [pltpu.VMEM(s, d) for s, d in scratch]

    def fetching(place, *refs):
        near, sems = list(refs[: -len(far) - 1]), refs[-1]
        copies = []
        for k, (i, ref) in enumerate(zip(far, refs[-len(far) - 1 : -1])):
            copies.append(pltpu.make_async_copy(near[i], ref, sems.at[k]))
            copies[-1].start()
            near[i] = ref
        for copy in copies:
            copy.wait()
        body(place, *near)

    if far:
        buffers += [pltpu.VMEM(args[i].shape, args[i].dtype) for i in far]
        buffers += [pltpu.SemaphoreType.DMA((len(far),))]
    return pl.pallas_call(
        fetching if far else body,
        name=name,
        out_shape=[jax.ShapeDtypeStruct(s, d) for s, d in outs],
        in_specs=[pl.BlockSpec(memory_space=pltpu.SMEM)] + specs,
        out_specs=[whole] * len(outs),
        scratch_shapes=buffers,
        compiler_params=pltpu.CompilerParams(vmem_limit_bytes=min(held + extra, 56 << 20)),
        cost_estimate=pl.CostEstimate(
            flops=int(WORK.get(name, 1.5) * PACE), bytes_accessed=1, transcendentals=0
        ),
    )(place, *args)


def rows_at(start, size, align):
    return pl.ds(pl.multiple_of(start, align), size)


class Grid:
    def __init__(self, dp, ctx):
        self.dp, self.ctx = dp, ctx
        self.ny, self.nx, self.nz = 2, dp // 2, ctx // 2

    def move(self, value, step):
        pairs = []
        for i in range(self.dp * self.ctx):
            core, z = i % 2, (i // 2) % self.nz
            x, y = (i // self.ctx) % self.nx, i // (self.ctx * self.nx)
            y, x, z, core = step(y, x, z, core)
            pairs.append((i, ((y * self.nx + x) * self.nz + z) * 2 + core))
        return lax.ppermute(value, AXES, pairs)

    def core(self, value):
        return self.move(value, lambda y, x, z, c: (y, x, z, 1 - c))

    def along_x(self, value):
        return self.move(value, lambda y, x, z, c: (y, 1 - x, z, c))

    def along_y(self, value):
        return self.move(value, lambda y, x, z, c: (1 - y, x, z, c))

    def along_xy(self, value):
        return self.move(value, lambda y, x, z, c: (1 - y, 1 - x, z, c))

    def along_z(self, value, hop):
        return self.move(value, lambda y, x, z, c: (y, x, (z + hop) % self.nz, c))


    def lines(self):
        return [[2 * z + core for z in range(self.nz)] for core in range(2)]

    def gather_z(self, value):
        return lax.all_gather(value, "ctx", axis=0, tiled=True, axis_index_groups=self.lines())

    def gather_chips(self, value):
        count = self.dp * self.ctx
        groups = [list(range(core, count, 2)) for core in range(2)]
        return lax.all_gather(value, AXES, axis=0, tiled=True, axis_index_groups=groups)

    def scatter_z(self, value):
        return lax.psum_scatter(
            value, "ctx", scatter_dimension=0, tiled=True, axis_index_groups=self.lines()
        )


def from_z(z, hop):
    return lax.rem(z - hop + 4, 4)


def order_kernel(place, own, r1, r2, r3, out):
    z = place[2]
    out[z] = own[...]
    out[from_z(z, 1)] = r1[...]
    out[from_z(z, 2)] = r2[...]
    out[from_z(z, 3)] = r3[...]


def block_index(place):
    y, x = place[0], place[1]
    return (2 * y + x, 2 * y + 1 - x, 2 * (1 - y) + x, 2 * (1 - y) + 1 - x)


def fold(block):
    rows = block.shape[0] // 2
    return jnp.concatenate([block[:rows], block[rows:]], axis=1)


def deal(place, blocks, targets):
    for hop, target in enumerate(targets):
        target[...] = blocks[lax.rem(place[2] + hop, 4)]


def unfold(ref, lanes):
    return jnp.concatenate([ref[:, :lanes], ref[:, lanes:]], axis=0)


def seen(seg_col, seg_row, i, span):
    keys = span * (i + 1)
    same = seg_col[i * span : (i + 1) * span] == seg_row[:, :keys]
    place_q = i * span + lax.broadcasted_iota(jnp.int32, (span, keys), 0)
    place_k = lax.broadcasted_iota(jnp.int32, (span, keys), 1)
    return jnp.where(same & (place_q >= place_k), 0.0, BIG).astype(F32)


def attend_kernel(
    place,
    own,
    other,
    b0,
    bx,
    by,
    bxy,
    seg_row,
    seg_col,
    weight,
    vectors,
    normed,
    rows,
    exact,
    totals,
    out_own,
    out_1,
    out_2,
    out_3,
    lifted,
    spare,
    out,
):
    core, second = place[3], place[2] % 2 == 1
    lines, run_rows, width = own.shape
    group = width // 4
    span = 2 * run_rows
    part = b0.shape[0] * b0.shape[1]
    cut = weight.shape[1]
    for index, piece in zip(block_index(place), (b0, bx, by, bxy)):
        for k in range(piece.shape[0]):
            here = rows_at(index * part + k * piece.shape[1], piece.shape[1], 16)
            weight[here] = piece[k, :, :cut]
    vectors[...] = jnp.transpose(weight[:, 4 * LANES :].astype(F32))[64:80]
    gain, shift = vectors[0:1, :], vectors[1:2, :]
    mine = pl.ds(pl.multiple_of(core * 2 * group, LANES), 2 * group)
    bias_q, bias_v = vectors[2:3, mine], vectors[3:4, mine]
    bias_q = jnp.where(second, bias_q[:, group:], bias_q[:, :group])
    bias_v = jnp.where(second, bias_v[:, group:], bias_v[:, :group])
    for i in range(lines):
        spare[i, rows_at(core * run_rows, run_rows, 16)] = own[i]
        spare[i, rows_at((1 - core) * run_rows, run_rows, 16)] = other[i]
    for i in range(lines):
        here = slice(i * span, (i + 1) * span)
        value = (normalize(spare[i].astype(F32))[0] * gain + shift).astype(BF16)
        normed[here] = value
        projected = dot(value, weight[:, : 3 * group])
        rows[here, :group] = ((projected[:, :group] + bias_q) * SCALING).astype(BF16)
        rows[here, group : 2 * group] = projected[:, group : 2 * group].astype(BF16)
        rows[here, 2 * group :] = (projected[:, 2 * group :] + bias_v).astype(BF16)
    for i in range(lines):
        here = slice(i * span, (i + 1) * span)
        keys = span * (i + 1)
        bias = seen(seg_col, seg_row, i, span)
        heads = []
        for h in range(3):
            at = h * HEAD_DIM
            query = rows[here, at : at + HEAD_DIM]
            key = rows[:keys, group + at : group + at + HEAD_DIM]
            value = rows[:keys, 2 * group + at : 2 * group + at + HEAD_DIM]
            scores = dot(query, key, ((1,), (1,))) + bias
            peak = jnp.max(scores, axis=-1, keepdims=True)
            expanded = jnp.exp(scores - peak)
            total = jnp.sum(expanded, axis=-1, keepdims=True)
            mixed = dot(expanded.astype(BF16), value) / total
            heads.append(mixed.astype(BF16))
            exact[here, at : at + HEAD_DIM] = mixed
            totals[here, h : h + 1] = peak + jnp.log(total)
        out[i] = fold(jnp.concatenate(heads, axis=1))
    deal(place, out, (out_own, out_1, out_2, out_3))
    held = vectors[8:12, mine]
    few = 2 * group // 16
    for j in range(16):
        for k in range(4):
            at = (4 * j + k) * few
            lifted[:, at : at + few] = held[k : k + 1, j * few : (j + 1) * few]


def out_kernel(place, own, r1, r2, r3, weight, attended, *partial):
    z = place[2]
    span, group = attended.shape[1:]
    attended[z] = unfold(own, group)
    for hop, piece in ((1, r1), (2, r2), (3, r3)):
        attended[from_z(z, hop)] = unfold(piece, group)
    for s in range(2):
        partial[s][...] = (
            dot(attended[2 * s], weight[:group]) + dot(attended[2 * s + 1], weight[group:])
        ).astype(BF16)


def place_rows(core, target, own, other):
    run_rows = own.shape[0] // 2
    for s in range(2):
        for which, piece in ((core, own), (1 - core, other)):
            target[rows_at((2 * s + which) * run_rows, run_rows, 16)] = piece[
                s * run_rows : (s + 1) * run_rows
            ]


def hidden_kernel(
    place,
    tokens_own,
    tokens_other,
    part_first,
    part_second,
    other_first,
    other_second,
    cot_own,
    cot_other,
    up,
    vectors,
    bias_up,
    cot,
    residual,
    normed,
    active,
    slope,
    tokens,
):
    place_rows(place[3], cot, cot_own, cot_other)
    place_rows(place[3], tokens, tokens_own, tokens_other)
    gain, shift, bias_out = vectors[5:6, :], vectors[6:7, :], vectors[4:5, :]
    span = tokens.shape[0] // 2
    for s in range(2):
        here = slice(s * span, (s + 1) * span)
        one, two = ((part_first, other_first), (part_second, other_second))[s]
        wide = tokens[here].astype(F32) + (one[...].astype(F32) + two[...].astype(F32)) + bias_out
        residual[here] = wide
        low = (normalize(wide)[0] * gain + shift).astype(BF16)
        normed[here] = low
        hidden = dot(low, up[...]) + bias_up[...]
        square = hidden * hidden
        bent = jnp.tanh(ROOT * (hidden + CUBIC * (square * hidden)))
        active[here] = (0.5 * hidden * (1.0 + bent)).astype(BF16)
        slope[here] = 0.5 * (1.0 + bent) + 0.5 * hidden * (1.0 - bent * bent) * (
            ROOT * (1.0 + 3.0 * CUBIC * square)
        )


def down_weights_kernel(place, active, cot, down_own, *targets):
    *targets, spare = targets
    core = place[3]
    spare[...] = dot(active[...], cot[...], ((0,), (0,))).astype(BF16)
    width = cot.shape[1]
    for j in range(8):
        for k in range(2):
            lanes = slice(k * width, (k + 1) * width)
            here = 192 * j + 48 * k
            down_own[48 * j : 48 * j + 48, lanes] = spare[rows_at(here + 96 * core, 48, 16)]
            targets[j // 3][48 * (j % 3) : 48 * (j % 3) + 48, lanes] = spare[
                rows_at(here + 96 * (1 - core), 48, 16)
            ]


def feed_kernel(
    place,
    residual,
    active,
    slope,
    cot,
    up,
    down,
    grad_hidden,
    result,
    grad_normed,
    low_first,
    low_second,
    sums,
    lifted,
):
    span = cot.shape[0] // 2
    for s in range(2):
        here = slice(s * span, (s + 1) * span)
        upstream = cot[here]
        grad = (dot(upstream, down[...], ((1,), (1,))) * slope[here]).astype(BF16)
        grad_hidden[here] = grad
        back = dot(grad, up[...], ((1,), (1,)))
        grad_normed[here] = back
        (low_first, low_second)[s][...] = back.astype(BF16)
        result[here] = dot(active[here], down[...])
        rows = jnp.concatenate(
            [
                jnp.sum(back * normalize(residual[here])[0], axis=0, keepdims=True),
                jnp.sum(back, axis=0, keepdims=True),
                0.5 * jnp.sum(upstream.astype(F32), axis=0, keepdims=True),
            ],
            axis=0,
        )
        total = jnp.sum(grad.astype(F32), axis=0, keepdims=True)
        if s == 0:
            sums[...] = rows
        else:
            sums[...] = sums[...] + rows
            held = first + total
        first = total
    few = held.shape[1] // 64
    for j in range(16):
        for k in range(4):
            at = (4 * j + k) * few
            lifted[k : k + 1, j * few : (j + 1) * few] = held[:, at : at + few]


def up_weights_kernel(place, normed, grad_hidden, grad_up):
    grad_up[...] = dot(normed[...], grad_hidden[...], ((0,), (0,))).astype(BF16)


def attend_grad_kernel(
    place,
    back_own,
    other_first,
    other_second,
    residual,
    cot,
    vectors,
    weight,
    attended,
    grad_residual,
    deal_own,
    deal_1,
    deal_2,
    deal_3,
    out_own,
    out_other,
    sum_out,
    spare,
    blocks,
):
    core = place[3]
    gain = vectors[5:6, :]
    span = cot.shape[0] // 2
    group = attended.shape[2]
    half = 2 * group
    products = [None, None]
    for s in range(2):
        here = slice(s * span, (s + 1) * span)
        normal, factor = normalize(residual[here])
        wide = cot[here].astype(F32) + norm_back(
            (back_own[here] + (other_first, other_second)[s][...].astype(F32)) * gain,
            normal,
            factor,
        )
        grad_residual[here] = wide
        low = wide.astype(BF16)
        grad = dot(low, weight[...], ((1,), (1,))).astype(BF16)
        total = 0.5 * jnp.sum(wide, axis=0, keepdims=True)
        sum_out[...] = total if s == 0 else sum_out[...] + total
        for g in range(2):
            blocks[2 * s + g] = fold(grad[:, g * group : (g + 1) * group])
            product = dot(attended[2 * s + g], low, ((0,), (0,)))
            products[g] = product if s == 0 else products[g] + product
    deal(place, blocks, (deal_own, deal_1, deal_2, deal_3))
    for g in range(2):
        spare[g * group : (g + 1) * group] = products[g].astype(BF16)
    out_own[...] = spare[:, rows_at(core * half, half, LANES)]
    out_other[...] = spare[:, rows_at((1 - core) * half, half, LANES)]


def attend_back_kernel(
    place,
    rows,
    exact,
    totals,
    seg_row,
    seg_col,
    own,
    r1,
    r2,
    r3,
    joined,
    grad,
    keys_grad,
):
    z = place[2]
    span, group = rows.shape[0] // 4, grad.shape[1]
    grad[rows_at(z * span, span, span)] = unfold(own, group)
    for hop, piece in ((1, r1), (2, r2), (3, r3)):
        grad[rows_at(from_z(z, hop) * span, span, span)] = unfold(piece, group)
    for i in (3, 2, 1, 0):
        here = slice(i * span, (i + 1) * span)
        keys = span * (i + 1)
        bias = seen(seg_col, seg_row, i, span)
        for h in range(3):
            at = h * HEAD_DIM
            lanes = slice(at, at + HEAD_DIM)
            query = rows[here, lanes]
            key = rows[:keys, group + at : group + at + HEAD_DIM]
            value = rows[:keys, 2 * group + at : 2 * group + at + HEAD_DIM]
            upstream = grad[here, lanes]
            delta = jnp.sum(upstream.astype(F32) * exact[here, lanes], axis=-1, keepdims=True)
            probs = jnp.exp(dot(query, key, ((1,), (1,))) + bias - totals[here, h : h + 1])
            slopes = dot(upstream, value, ((1,), (1,)))
            grad_scores = (probs * (slopes - delta)).astype(BF16)
            grad_query = dot(grad_scores, key).astype(BF16)
            joined[here, lanes] = (grad_query.astype(F32) * SCALING).astype(BF16)
            grad_key = dot(grad_scores, query, ((0,), (0,)))
            grad_value = dot(probs.astype(BF16), upstream, ((0,), (0,)))
            if i == 3:
                keys_grad[2 * h] = grad_key
                keys_grad[2 * h + 1] = grad_value
            else:
                keys_grad[2 * h, :keys] = keys_grad[2 * h, :keys] + grad_key
                keys_grad[2 * h + 1, :keys] = keys_grad[2 * h + 1, :keys] + grad_value
    for h in range(3):
        for k in range(2):
            at = (k + 1) * group + h * HEAD_DIM
            joined[:, at : at + HEAD_DIM] = keys_grad[2 * h + k].astype(BF16)


def project_back_kernel(
    place,
    joined,
    weight,
    normed,
    tokens_own,
    tokens_other,
    sum_out,
    sums_two,
    lifted,
    o_own,
    o_x,
    o_y,
    o_xy,
    back_own,
    back_first,
    back_second,
    back_third,
    product,
    small,
):
    core = place[3]
    second = place[2] % 2 == 1
    lines, run_rows, width = tokens_own.shape
    span, group = 2 * run_rows, width // 4
    small[...] = jnp.zeros_like(small)
    small[4:5] = sum_out[...]
    small[5:8] = sums_two[...]
    small[8:12, pl.ds(pl.multiple_of(core * 2 * group, LANES), 2 * group)] = lifted[...]
    mine = pl.ds(pl.multiple_of(core * 2 * group, LANES), 2 * group)
    empty = jnp.zeros((1, group), F32)
    for row, at in ((2, 0), (3, 2 * group)):
        total = jnp.sum(joined[:, at : at + group].astype(F32), axis=0, keepdims=True)
        small[row : row + 1, mine] = jnp.where(
            second,
            jnp.concatenate([empty, total], axis=1),
            jnp.concatenate([total, empty], axis=1),
        )
    for i in range(lines):
        for which, tokens in ((core, tokens_own), (1 - core, tokens_other)):
            here = rows_at(i * span + which * run_rows, run_rows, 16)
            step = dot(joined[here], weight[:, : 3 * group], ((1,), (1,)))
            if tokens is tokens_own:
                back_own[i] = step
            else:
                low = step.astype(BF16)
                for target, start in ((back_first, 0), (back_second, 192), (back_third, 384)):
                    first = max(start, i * run_rows)
                    last = min(start + target.shape[0], (i + 1) * run_rows)
                    if first < last:
                        target[first - start : last - start] = low[
                            first - i * run_rows : last - i * run_rows
                        ]
            normal = normalize(tokens[i].astype(F32))[0]
            small[0:1] = small[0:1] + jnp.sum(step * normal, axis=0, keepdims=True)
            small[1:2] = small[1:2] + jnp.sum(step, axis=0, keepdims=True)
    product[:, : 3 * group] = dot(normed[...], joined[...], ((0,), (0,))).astype(BF16)
    product[:, 3 * group :] = jnp.transpose(small[...])[:, :64].astype(BF16)
    size = o_own.shape[0]
    for index, target in zip(block_index(place), (o_own, o_x, o_y, o_xy)):
        target[...] = product[rows_at(index * size, size, 16)]


def split_kernel(targets, size, block, place):
    y, x = place[0], place[1]
    own, over_x, over_y, low, high = targets
    block(y, x, slice(0, size), own)
    block(y, 1 - x, slice(0, size), over_x)
    block(1 - y, x, slice(0, size), over_y)
    block(1 - y, 1 - x, slice(0, size // 2), low)
    block(1 - y, 1 - x, slice(size // 2, size), high)


def split_down_kernel(place, own, first, second, third, *targets):
    *targets, other = targets
    core, size = place[3], targets[0].shape[0]
    other[:144] = first[...]
    other[144:288] = second[...]
    other[288:] = third[...]

    def block(y, x, rows, target):
        here = rows_at(x * size + rows.start, rows.stop - rows.start, 16)
        target[...] = jnp.where(y == core, own[here], other[here])

    split_kernel(targets, size, block, place)


def split_up_kernel(place, up, out_own, out_other, *targets):
    core, size = place[3], targets[0].shape[0]
    cut = up.shape[1]

    def block(y, x, rows, target):
        count = rows.stop - rows.start
        target[:, :cut] = up[rows_at((2 * y + x) * size + rows.start, count, 16)]
        here = rows_at(x * size + rows.start, count, 16)
        target[:, cut:] = jnp.where(y == core, out_own[here], out_other[here])

    split_kernel(targets, size, block, place)


def collect_kernel(place, over_x, over_y, low, high, sum_x, sum_y):
    half = low.shape[0]
    sum_x[:half] = over_x[:half]
    sum_x[half:] = (over_x[half:].astype(F32) + high[...].astype(F32)).astype(BF16)
    sum_y[:half] = (over_y[:half].astype(F32) + low[...].astype(F32)).astype(BF16)
    sum_y[half:] = over_y[half:]


def spread_kernel(place, own, from_x, from_y, low, high, up, down):
    half = low.shape[0]
    cut = up.shape[2]
    blocks = block_index(place)
    for index, piece in zip(blocks, (own, from_x, from_y)):
        up[index] = piece[:, :cut]
        down[index] = piece[:, cut:]
    up[blocks[3], :half] = low[:, :cut]
    up[blocks[3], half:] = high[:, :cut]
    down[blocks[3], :half] = low[:, cut:]
    down[blocks[3], half:] = high[:, cut:]


def sum_plane_kernel(place, a, b, c, d, own, z1, z2, z3, spare):
    z = place[2]
    spare[...] = (
        (a[...].astype(F32) + b[...].astype(F32)) + (c[...].astype(F32) + d[...].astype(F32))
    ).astype(BF16)
    size = own.shape[0]
    for hop, target in enumerate((own, z1, z2, z3)):
        target[...] = spare[rows_at(lax.rem(z + hop, 4) * size, size, 16)]


def line_deal_kernel(place, own, from_x, from_y, *targets):
    *targets, spare = targets
    spare[...] = (
        own[...].astype(F32) + (from_x[...].astype(F32) + from_y[...].astype(F32))
    ).astype(BF16)
    size = targets[0].shape[0]
    for hop, target in enumerate(targets):
        target[...] = spare[rows_at(lax.rem(place[2] + hop, 4) * size, size, 16)]


def line_down_kernel(place, a, b, c, d, down):
    rows, width = a.shape[0], down.shape[1]
    for k in range(2):
        lanes = slice(k * width, (k + 1) * width)
        down[k * rows : (k + 1) * rows] = (a[:, lanes].astype(F32) + b[:, lanes].astype(F32)) + (
            c[:, lanes].astype(F32) + d[:, lanes].astype(F32)
        )


def line_up_kernel(place, a, b, c, d, own, other, spare):
    core = place[3]
    spare[...] = (a[...].astype(F32) + b[...].astype(F32)) + (
        c[...].astype(F32) + d[...].astype(F32)
    )
    half = own.shape[0]
    own[...] = spare[rows_at(core * half, half, 8)]
    other[...] = spare[rows_at((1 - core) * half, half, 8)]


def line_qkv_kernel(place, own, r1, r2, r3, mine, theirs, spare):
    second = place[2] % 2 == 1
    third = own.shape[1] // 3 // LANES * LANES + 64
    same = own[...].astype(F32) + r2[...].astype(F32)
    cross = r1[...].astype(F32) + r3[...].astype(F32)
    first, last = jnp.where(second, cross, same), jnp.where(second, same, cross)
    for k in range(3):
        here = slice(k * third, (k + 1) * third)
        spare[:, 2 * k * third : (2 * k + 1) * third] = first[:, here]
        spare[:, (2 * k + 1) * third : (2 * k + 2) * third] = last[:, here]
    spare[:, 6 * third : 6 * third + 64] = (same + cross)[:, 3 * third :]
    spare[:, 6 * third + 64 :] = jnp.zeros((spare.shape[0], 64), F32)
    rows = mine.shape[0]
    mine[...] = spare[rows_at(place[3] * rows, rows, 8)]
    theirs[...] = spare[rows_at((1 - place[3]) * rows, rows, 8)]


def out_split_kernel(place, b0, bx, by, bxy, own, other, spare):
    core = place[3]
    first = b0.shape[2] - own.shape[1]
    size = b0.shape[0] * b0.shape[1]
    for index, piece in zip(block_index(place), (b0, bx, by, bxy)):
        for k in range(piece.shape[0]):
            here = rows_at(index * size + k * piece.shape[1], piece.shape[1], 16)
            spare[here] = piece[k, :, first:]
    half = own.shape[0]
    own[...] = spare[rows_at(core * half, half, 16)]
    other[...] = spare[rows_at((1 - core) * half, half, 16)]


def out_halves_kernel(place, own, other, out):
    core = place[3]
    half = out.shape[0]
    for which, piece in ((core, own), (1 - core, other)):
        out[:, rows_at(which * half, half, LANES)] = piece[...]


def down_halves_kernel(place, own, other, down):
    core = place[3]
    width = down.shape[1]
    for which, piece in ((core, own), (1 - core, other)):
        for j in range(8):
            for k in range(2):
                down[rows_at(192 * j + 96 * which + 48 * k, 48, 16)] = piece[
                    48 * j : 48 * j + 48, k * width : (k + 1) * width
                ]


def sum_back_kernel(place, own, first, second, third, *targets):
    *targets, spare = targets
    lines, rows, width = own.shape
    spare[0:192] = first[...].astype(F32)
    spare[192:384] = second[...].astype(F32)
    spare[384:] = third[...].astype(F32)
    for hop, target in enumerate(targets):
        k = lax.rem(place[2] + hop, 4)
        target[...] = (own[k] + spare[rows_at(k * rows, rows, rows)]).astype(BF16)


def final_kernel(place, own, r1, r2, r3, grad_residual, tokens, vectors, out, held):
    z, core = place[2], place[3]
    rows = tokens.shape[0] // 2
    held[z] = own[...]
    for hop, piece in ((1, r1), (2, r2), (3, r3)):
        held[from_z(z, hop)] = piece[...]
    gain = vectors[0:1, :]
    for s in range(2):
        here = slice(s * rows, (s + 1) * rows)
        there = rows_at((2 * s + core) * rows, rows, 16)
        normal, factor = normalize(tokens[here].astype(F32))
        grad = (held[2 * s].astype(F32) + held[2 * s + 1].astype(F32)) * gain
        out[here] = (grad_residual[there] + norm_back(grad, normal, factor)).astype(BF16)


def split_local(
    grid,
    tokens,
    segments,
    cotangent,
    ln1_gain,
    ln1_bias,
    w_qkv,
    bias_query,
    bias_value,
    w_out,
    bias_out,
    ln2_gain,
    ln2_bias,
    w_up,
    bias_up,
    w_down,
    bias_down,
):
    count, run_rows, width = tokens.shape
    own_rows = count * run_rows
    all_rows = 2 * own_rows
    span = 2 * run_rows
    half = width // 2
    group = half // 2
    hidden_half = w_up.shape[1] // 2
    shard = w_qkv.shape[0]
    dp, ctx = lax.axis_index("dp"), lax.axis_index("ctx")
    y, x, z, core = dp // grid.nx, dp % grid.nx, ctx // 2, ctx % 2
    place = jnp.stack([y, x, z, core]).astype(jnp.int32)
    first_core = core == 0

    def pick(array, index, axis):
        return lax.dynamic_index_in_dim(array, index, axis, keepdims=False)

    def both(own, other, axis):
        return jnp.where(
            first_core,
            jnp.concatenate([own, other], axis),
            jnp.concatenate([other, own], axis),
        )

    def z_all(value):
        return [value] + [grid.along_z(value, hop) for hop in (1, 2, 3)]

    def after(values, *waited):
        return lax.optimization_barrier((values, waited))[0]

    def z_send(blocks):
        return [grid.along_z(blocks[hop], hop) for hop in (1, 2, 3)]

    flat = tokens.reshape(own_rows, width)
    small = jnp.stack(
        [ln1_gain, ln1_bias, bias_query, bias_value, bias_out, ln2_gain, ln2_bias, bias_down], axis=1
    )
    lifted = bias_up.reshape(4, shard).T
    seg_lanes = jnp.pad(segments.astype(BF16).reshape(8, 32), ((0, shard - 8), (0, 0)))
    vector_lanes = jnp.concatenate(
        [small, lifted, jnp.zeros((shard, 4), BF16), seg_lanes, jnp.zeros((shard, 16), BF16)],
        axis=1,
    )
    split_qkv = w_qkv.reshape(shard, 3, 2, half)
    split_up = w_up.reshape(shard, 2, hidden_half)
    split_out = w_out.reshape(shard, 2, half)
    cut = 3 * group + 64
    size = 8 * shard

    def columns(which):
        chosen = pick(split_qkv, which, 2)
        return jnp.concatenate(
            [
                chosen[:, :, :group].reshape(shard, 3 * group),
                vector_lanes,
                chosen[:, :, group:].reshape(shard, 3 * group),
                vector_lanes,
                pick(split_out, which, 1),
                pick(split_up, which, 1),
            ],
            axis=1,
        )

    piece = both(columns(core), grid.core(columns(1 - core)), 0)
    flat_other = grid.core(flat)
    cot_own = cotangent.reshape(own_rows, width)
    cot_other = grid.core(cot_own)
    second_group = lax.rem(z, 2) == 1
    lanes_out = piece[:, 2 * cut : 2 * cut + half]
    first, last = piece[:, :cut], piece[:, cut : 2 * cut]
    piece_same = jnp.concatenate([jnp.where(second_group, last, first), lanes_out], axis=1)
    piece_cross = jnp.concatenate([jnp.where(second_group, first, last), lanes_out], axis=1)
    line_one = [
        piece_same,
        grid.along_z(piece_cross, 1),
        grid.along_z(piece_same, 2),
        grid.along_z(piece_cross, 3),
    ]
    def order(name, pieces):
        return run(name, order_kernel, place, pieces, [((4,) + pieces[0].shape, BF16)])[0]

    def kernel(name, body, args, outs, scratch=(), far=(), extra=6 << 20):
        return run(name, body, place, args, outs, scratch, far, extra)

    line_one = after(line_one, flat_other, cot_other)
    def order_rows(name, pieces):
        lanes = pieces[0].shape[1]
        return kernel(
            name, order_kernel, pieces, [((4, 2 * shard, lanes), BF16)], far=(1, 2, 3)
        )[0].reshape(size, lanes)

    plane_one = order("order_qkv", line_one)
    from_x, from_y, from_xy = (
        grid.along_x(plane_one),
        grid.along_y(plane_one),
        grid.along_xy(plane_one),
    )
    piece_b = jnp.concatenate([w_down[: 2 * shard], w_down[2 * shard :]], axis=1)

    rest_piece = jnp.concatenate([piece[:, 2 * cut + half :], piece_b], axis=1)
    rest_line = z_all(after(rest_piece, line_one))
    token_pieces = [
        grid.along_z(pick(tokens, lax.rem(z + hop, 4) // 2, 0), hop) for hop in (1, 2, 3)
    ]
    token_pieces = after(token_pieces, plane_one)
    gathered = order("order_tokens", [pick(tokens, z // 2, 0)] + token_pieces)
    gathered_rows = gathered.reshape(4 * run_rows, width)
    gathered_other = jnp.concatenate(
        [grid.core(gathered_rows[:192]), grid.core(gathered_rows[192:384]), grid.core(gathered_rows[384:])]
    ).reshape(gathered.shape)
    out_parts = run(
        "out_split",
        out_split_kernel,
        place,
        [plane_one, from_x, from_y, from_xy],
        [((half, half), BF16)] * 2,
        [((width, half), BF16)],
    )
    segs = plane_one.reshape(4, 2, shard, cut + half)[:, :, :8, 3 * group + 16 : 3 * group + 48]
    segs = segs.reshape(4, 2, 2, 4 * 32).transpose(2, 0, 1, 3).reshape(2, 8 * run_rows)
    segs = pick(segs, z // 2, 0).astype(F32)

    weight_qkv, vectors, normed, packed, exact, totals, *out_deal, bias_up_half = kernel(
        "attend",
        attend_kernel,
        [
            gathered,
            gathered_other,
            after(plane_one, out_parts),
            from_x,
            from_y,
            from_xy,
            segs.reshape(1, -1),
            segs.reshape(-1, 1),
        ],
        [
            ((width, cut), BF16),
            ((16, width), F32),
            ((4 * span, width), BF16),
            ((4 * span, 3 * group), BF16),
            ((4 * span, group), F32),
            ((4 * span, LANES), F32),
        ]
        + [((run_rows, 2 * group), BF16)] * 4
        + [((1, hidden_half), F32)],
        [((4, span, width), BF16), ((4, run_rows, 2 * group), BF16)],
        far=(3, 4, 5),
        extra=14 << 20,
    )
    out_blocks = out_deal[0]
    out_pieces = z_send(out_deal)

    weight_out = kernel(
        "out_halves",
        out_halves_kernel,
        [out_parts[0], grid.core(out_parts[1])],
        [((half, width), BF16)],
    )[0]

    plane_rest = order_rows("order_rest", [rest_line[0]] + after(rest_line[1:], out_blocks))
    attended, *partial = kernel(
        "project_out",
        out_kernel,
        [out_blocks] + out_pieces + [weight_out],
        [((4, span, group), BF16)] + [((own_rows, width), BF16)] * 2,
        far=(1, 2, 3),
    )
    part_other = [grid.core(member) for member in partial]
    over = after((grid.along_x(plane_rest), grid.along_y(plane_rest)), part_other)
    low, high = grid.along_x(over[1][: 4 * shard]), grid.along_y(over[0][4 * shard :])
    weight_up, mixed_down = kernel(
        "spread",
        spread_kernel,
        [plane_rest, *over, low, high],
        [((4, size, hidden_half), BF16), ((4, size, 2 * width), BF16)],
        far=(1, 2, 3, 4),
    )
    weight_up = weight_up.reshape(width, hidden_half)
    mixed_down = mixed_down.reshape(2, half, 2 * width)
    cot, residual, normed_two, active, slope = kernel(
        "hidden",
        hidden_kernel,
        [
            flat,
            flat_other,
            *partial,
            *part_other,
            cot_own,
            cot_other,
            weight_up,
            vectors,
            bias_up_half,
        ],
        [
            ((all_rows, width), BF16),
            ((all_rows, width), F32),
            ((all_rows, width), BF16),
            ((all_rows, hidden_half), BF16),
            ((all_rows, hidden_half), F32),
        ],
        [((all_rows, width), BF16)],
        far=(0, 1, 6, 7),
        extra=14 << 20,
    )
    weight_down = kernel(
        "down_halves",
        down_halves_kernel,
        [pick(mixed_down, core, 0), grid.core(pick(mixed_down, 1 - core, 0))],
        [((hidden_half, width), BF16)],
    )[0]

    def halve(array, which):
        return pick(array.reshape(2, 2, run_rows, width), which, 1).reshape(own_rows, width)

    def split(name, body, parts, lanes, scratch=()):
        results = [((size, lanes), BF16)] * 3 + [((size // 2, lanes), BF16)] * 2
        return kernel(name, body, parts, results, scratch)

    def diagonal(parts):
        return grid.along_x(parts[3]), grid.along_y(parts[4])

    def collect(name, parts, low, high):
        sum_x, sum_y = kernel(
            name, collect_kernel, [parts[1], parts[2], low, high], [(parts[1].shape, BF16)] * 2, far=(2, 3)
        )
        return parts[0], grid.along_x(sum_x), grid.along_y(sum_y), sum_x

    grad_hidden, result, back_two, *back_low, sums_two, lifted = kernel(
        "feed",
        feed_kernel,
        [residual, active, slope, cot, weight_up, weight_down],
        [
            ((all_rows, hidden_half), BF16),
            ((all_rows, width), F32),
            ((all_rows, width), F32),
            ((own_rows, width), BF16),
            ((own_rows, width), BF16),
            ((3, width), F32),
            ((4, half), F32),
        ],
        extra=14 << 20,
    )
    back_other = [grid.core(member) for member in back_low]
    grad_up = kernel(
        "up_weights",
        up_weights_kernel,
        [normed_two, grad_hidden],
        [((width, hidden_half), BF16)],
        extra=10 << 20,
    )[0]


    down_own, *down_other = kernel(
        "down_weights",
        down_weights_kernel,
        after([active, cot], grad_up),
        [((rows, 2 * width), BF16) for rows in (half, 144, 144, 96)],
        [((hidden_half, width), BF16)],
        extra=10 << 20,
    )
    down_recv = [grid.core(member) for member in down_other]
    grad_residual, *grad_deal, out_own, out_other, sum_out = kernel(
        "attend_grad",
        attend_grad_kernel,
        after(
            [back_two, *back_other, residual, cot, vectors, weight_out, attended],
            down_own,
        ),
        [
            ((all_rows, width), F32),
            *[((run_rows, 2 * group), BF16)] * 4,
            ((half, half), BF16),
            ((half, half), BF16),
            ((1, width), F32),
        ],
        [((half, width), BF16), ((4, run_rows, 2 * group), BF16)],
    )
    grad_blocks = grad_deal[0]
    grad_pieces = z_send(grad_deal)
    out_recv = grid.core(out_other)
    def split(name, body, parts, lanes, scratch=()):
        results = [((size, lanes), BF16)] * 3 + [((size // 2, lanes), BF16)] * 2
        return kernel(name, body, parts, results, scratch)

    down_parts = split(
        "split_down",
        split_down_kernel,
        [down_own] + down_recv,
        2 * width,
        [((half, 2 * width), BF16)],
    )
    down_low, down_high = diagonal(down_parts)
    up_parts = split(
        "split_up",
        split_up_kernel,
        after([grad_up, out_own, out_recv], down_parts),
        hidden_half + half,
    )
    up_low, up_high = diagonal(up_parts)
    down_low, down_high = after((down_low, down_high), grad_pieces)
    down_parts = collect("collect_down", down_parts, down_low, down_high)

    result, residual = after((result, residual), up_parts)
    result_other = grid.core(halve(result, 1 - core))
    output = (
        halve(residual, core)
        + (halve(result, core) + result_other)
        + vectors[7:8]
    ).astype(BF16)

    grad_pieces = after(grad_pieces, up_parts, down_parts[3], output)
    grad_joined = kernel(
        "attend_back",
        attend_back_kernel,
        [packed, exact, totals, segs.reshape(1, -1), segs.reshape(-1, 1), grad_blocks]
        + grad_pieces,
        [((4 * span, 3 * group), BF16)],
        [((4 * span, group), BF16), ((6, 4 * span, HEAD_DIM), F32)],
        far=(0, 1, 2, 6, 7, 8),
        extra=14 << 20,
    )[0]
    def deal_sum(name, parts):
        lanes = parts[0].shape[1]
        dealt = kernel(
            name,
            line_deal_kernel,
            parts,
            [((2 * shard, lanes), BF16)] * 4,
            [((size, lanes), BF16)],
            far=(1, 2),
        )
        return [dealt[0]] + z_send(dealt)

    down_line = deal_sum("deal_down", after(list(down_parts[:3]), grad_joined))
    up_low, up_high = after((up_low, up_high), down_line[0])
    up_parts = collect("collect_up", up_parts, up_low, up_high)
    back_results = kernel(
        "project_back",
        project_back_kernel,
        [after(grad_joined, up_parts[3], down_line[1:]), weight_qkv, normed, gathered, gathered_other]
        + [sum_out, sums_two, lifted],
        [((size, cut), BF16)] * 4
        + [((4, run_rows, width), F32)]
        + [((192, width), BF16), ((192, width), BF16), ((128, width), BF16)],
        [((width, cut), BF16), ((LANES, width), F32)],
        far=(1, 2, 3, 4),
        extra=10 << 20,
    )
    qkv_parts, back_own, back_low = back_results[:4], back_results[4], back_results[5:]
    back_deal = kernel(
        "sum_back",
        sum_back_kernel,
        [back_own] + [grid.core(member) for member in back_low],
        [((run_rows, width), BF16)] * 4,
        [((4 * run_rows, width), F32)],
    )
    back_sum = back_deal[0]
    back_pieces = z_send(back_deal)
    up_ready = after(list(up_parts[:3]), back_sum)
    qkv_parts = [qkv_parts[0]] + after(list(qkv_parts[1:]), up_ready)
    qkv_recv = [grid.along_x(qkv_parts[1]), grid.along_y(qkv_parts[2]), grid.along_xy(qkv_parts[3])]
    up_line = deal_sum("deal_up", after(up_ready, back_pieces))
    qkv_own, *qkv_sends = kernel(
        "plane_qkv",
        sum_plane_kernel,
        [qkv_parts[0]] + after(qkv_recv, back_sum),
        [((2 * shard, cut), BF16)] * 4,
        [((size, cut), BF16)],
        far=(1, 2, 3),
    )
    qkv_line = [qkv_own] + [grid.along_z(qkv_sends[hop - 1], hop) for hop in (1, 2, 3)]
    qkv_mine, qkv_theirs = kernel(
        "line_qkv",
        line_qkv_kernel,
        qkv_line,
        [((shard, 6 * group + LANES), F32)] * 2,
        [((2 * shard, 6 * group + LANES), F32)],
        far=(1, 2, 3),
    )
    qkv_theirs = grid.core(qkv_theirs)
    grad_tokens = kernel(
        "final",
        final_kernel,
        [back_sum] + after(back_pieces, up_ready) + [grad_residual, flat, vectors],
        [((own_rows, width), BF16)],
        [((4, run_rows, width), BF16)],
        far=(1, 2, 3, 5),
    )[0]
    grad_down = kernel(
        "line_down", line_down_kernel, down_line, [((4 * shard, width), F32)], far=(1, 2, 3)
    )[0]
    up_mine, up_other = kernel(
        "line_up",
        line_up_kernel,
        up_line,
        [((shard, hidden_half + half), F32)] * 2,
        [((2 * shard, hidden_half + half), F32)],
        far=(1, 2, 3),
    )
    up_theirs = grid.core(up_other)
    grad_up_own = both(up_mine[:, :hidden_half], up_theirs[:, :hidden_half], 1)
    grad_out_own = both(up_mine[:, hidden_half:], up_theirs[:, hidden_half:], 1)
    grad_qkv_own = both(
        qkv_mine[:, : 6 * group].reshape(shard, 3, 1, half),
        qkv_theirs[:, : 6 * group].reshape(shard, 3, 1, half),
        2,
    ).reshape(shard, 6 * half)
    small_sum = (qkv_mine[:, 6 * group : 6 * group + 16] + qkv_theirs[:, 6 * group : 6 * group + 16]).T
    return (
        output.reshape(tokens.shape),
        grad_tokens.reshape(tokens.shape),
        small_sum[0],
        small_sum[1],
        grad_qkv_own,
        small_sum[2],
        small_sum[3],
        grad_out_own,
        small_sum[4],
        small_sum[5],
        small_sum[6],
        grad_up_own,
        small_sum[8:12].reshape(4 * shard),
        grad_down,
        small_sum[7],
    )


def build_local(mesh):
    dp, ctx = mesh.shape["dp"], mesh.shape["ctx"]
    if (dp, ctx) != (4, 8):
        return local_general
    grid = Grid(dp, ctx)
    return lambda *args: split_local(grid, *args)


def solution(mesh):
    return jax.shard_map(
        build_local(mesh),
        mesh=mesh,
        in_specs=(
            P("dp", "ctx", None),
            P("dp", "ctx"),
            P("dp", "ctx", None),
            P(("dp", "ctx")),
            P(("dp", "ctx")),
            P(("dp", "ctx"), None),
            P(("dp", "ctx")),
            P(("dp", "ctx")),
            P(("dp", "ctx"), None),
            P(("dp", "ctx")),
            P(("dp", "ctx")),
            P(("dp", "ctx")),
            P(("dp", "ctx"), None),
            P(("dp", "ctx")),
            P(("dp", "ctx"), None),
            P(("dp", "ctx")),
        ),
        out_specs=(
            P("dp", "ctx", None),
            P("dp", "ctx", None),
            P(("dp", "ctx")),
            P(("dp", "ctx")),
            P(("dp", "ctx"), None),
            P(("dp", "ctx")),
            P(("dp", "ctx")),
            P(("dp", "ctx"), None),
            P(("dp", "ctx")),
            P(("dp", "ctx")),
            P(("dp", "ctx")),
            P(("dp", "ctx"), None),
            P(("dp", "ctx")),
            P(("dp", "ctx"), None),
            P(("dp", "ctx")),
        ),
        check_vma=False,
    )
```

```python
import functools
import math

import jax
import jax.numpy as jnp
from jax import lax
from jax.experimental import pallas as pl
from jax.experimental.pallas import tpu as pltpu
from jax.sharding import PartitionSpec as P

HEADS = 12
HEAD_DIM = 64


EPSILON = 1e-05
NEGATIVE = -1e30
SCALING = 0.125


def layer_norm(values, gain_vec, shift_vec):
    center = values - jnp.mean(values, axis=-1, keepdims=True)
    spread = jnp.mean(center * center, axis=-1, keepdims=True)
    return center * lax.rsqrt(spread + EPSILON) * gain_vec + shift_vec


def split_heads(tensor):
    return tensor.reshape(tensor.shape[0], tensor.shape[1], HEADS, HEAD_DIM)


def visible(seg_query, seg_key, place_query, place_key):
    same_doc = seg_query[:, :, None] == seg_key[:, None, :]
    causal = place_query[None, :, None] >= place_key[None, None, :]
    return (same_doc & causal)[:, None]


def forward_block(
    carry, query_heads, key_rows, value_rows, seg_query, seg_key, place_query, place_key
):
    row_max, row_sum, acc_out = carry
    scores = jnp.einsum(
        "sqhd,skhd->shqk", query_heads, split_heads(key_rows), preferred_element_type=jnp.float32
    )
    allowed = visible(seg_query, seg_key, place_query, place_key)
    scores = jnp.where(allowed, scores, NEGATIVE)
    new_max = jnp.maximum(row_max, jnp.max(scores, axis=-1))
    expanded = jnp.where(allowed, jnp.exp(scores - new_max[..., None]), 0.0)
    factor = jnp.exp(row_max - new_max)
    row_sum = jnp.sum(expanded, axis=-1)
    added = jnp.einsum(
        "shqk,skhd->sqhd",
        expanded.astype(jnp.bfloat16),
        split_heads(value_rows),
        preferred_element_type=jnp.float32,
    )
    acc_out = acc_out * jnp.swapaxes(factor, 1, 2)[..., None] + added
    return (new_max, row_sum, acc_out)


def grad_block(
    query_heads,
    key_heads,
    value_heads,
    grad_heads,
    log_total,
    delta_sum,
    seg_query,
    seg_key,
    place_query,
    place_key,
):
    scores = jnp.einsum(
        "sqhd,skhd->shqk", query_heads, key_heads, preferred_element_type=jnp.float32
    )
    allowed = visible(seg_query, seg_key, place_query, place_key)
    shift_total = jnp.swapaxes(log_total, 1, 2)[..., None]
    probs = jnp.where(allowed, jnp.exp(scores - shift_total), 0.0)
    grad_probs = jnp.einsum(
        "sqhd,skhd->shqk", grad_heads, value_heads, preferred_element_type=jnp.float32
    )
    grad_scores = (probs * (grad_probs - jnp.swapaxes(delta_sum, 1, 2)[..., None])).astype(
        jnp.bfloat16
    )
    return (grad_scores, probs.astype(jnp.bfloat16))


def query_side(mine, theirs):
    query_heads, grad_heads, log_total, delta_sum, seg_mine, place_mine = mine
    key_rows, value_rows, seg_theirs = theirs
    place_theirs = jnp.arange(key_rows.shape[1], dtype=jnp.int32)
    key_heads = split_heads(key_rows)
    outcome = grad_block(
        query_heads,
        key_heads,
        split_heads(value_rows),
        grad_heads,
        log_total,
        delta_sum,
        seg_mine,
        seg_theirs,
        place_mine,
        place_theirs,
    )
    return jnp.einsum("shqk,skhd->sqhd", outcome[0], key_heads, preferred_element_type=jnp.float32)


def key_side(mine, theirs):
    key_heads, value_heads, seg_mine, place_mine = mine
    query_rows, grad_rows, total_high, total_low, delta_high, delta_low, seg_theirs = theirs
    place_theirs = jnp.arange(query_rows.shape[1], dtype=jnp.int32)
    query_heads = split_heads(query_rows)
    grad_heads = split_heads(grad_rows)
    log_total = total_high.astype(jnp.float32) + total_low.astype(jnp.float32)
    delta_sum = delta_high.astype(jnp.float32) + delta_low.astype(jnp.float32)
    grad_scores, probs = grad_block(
        query_heads,
        key_heads,
        value_heads,
        grad_heads,
        log_total,
        delta_sum,
        seg_theirs,
        seg_mine,
        place_theirs,
        place_mine,
    )
    grad_key = jnp.einsum(
        "shqk,sqhd->skhd", grad_scores, query_heads, preferred_element_type=jnp.float32
    )
    grad_value = jnp.einsum(
        "shqk,sqhd->skhd", probs, grad_heads, preferred_element_type=jnp.float32
    )
    return (grad_key, grad_value)


def contract_rows(left, right):
    return lax.dot_general(
        left, right, (((0,), (0,)), ((), ())), preferred_element_type=jnp.float32
    )


def contract_cols(left, right):
    return lax.dot_general(
        left, right, (((1,), (1,)), ((), ())), preferred_element_type=jnp.float32
    )


def local_general(
    tokens,
    segments,
    cotangent,
    ln1_gain,
    ln1_bias,
    w_qkv,
    bias_query,
    bias_value,
    w_out,
    bias_out,
    ln2_gain,
    ln2_bias,
    w_up,
    bias_up,
    w_down,
    bias_down,
):
    count, span_rows, model_width = tokens.shape
    total_rows = count * span_rows
    places = lax.axis_index("ctx") * span_rows + jnp.arange(span_rows, dtype=jnp.int32)
    gathered = (
        lax.all_gather(ln1_gain, ("dp", "ctx"), axis=0, tiled=True),
        lax.all_gather(ln1_bias, ("dp", "ctx"), axis=0, tiled=True),
        lax.all_gather(w_qkv, ("dp", "ctx"), axis=0, tiled=True),
        lax.all_gather(bias_query, ("dp", "ctx"), axis=0, tiled=True),
        lax.all_gather(bias_value, ("dp", "ctx"), axis=0, tiled=True),
        lax.all_gather(w_out, ("dp", "ctx"), axis=0, tiled=True),
        lax.all_gather(bias_out, ("dp", "ctx"), axis=0, tiled=True),
        lax.all_gather(ln2_gain, ("dp", "ctx"), axis=0, tiled=True),
        lax.all_gather(ln2_bias, ("dp", "ctx"), axis=0, tiled=True),
        lax.all_gather(w_up, ("dp", "ctx"), axis=0, tiled=True),
        lax.all_gather(bias_up, ("dp", "ctx"), axis=0, tiled=True),
        lax.all_gather(w_down, ("dp", "ctx"), axis=0, tiled=True),
        lax.all_gather(bias_down, ("dp", "ctx"), axis=0, tiled=True),
    )
    (
        gain_one,
        shift_one,
        qkv_full,
        query_shift,
        value_shift,
        out_full,
        out_shift,
        gain_two,
        shift_two,
        up_full,
        up_shift,
        down_full,
        down_shift,
    ) = gathered
    flat = tokens.reshape(total_rows, model_width).astype(jnp.float32)
    normed = layer_norm(flat, gain_one.astype(jnp.float32), shift_one.astype(jnp.float32)).astype(
        jnp.bfloat16
    )
    projected = jnp.dot(normed, qkv_full, preferred_element_type=jnp.float32)
    row_shape = (count, span_rows, model_width)
    query_rows = (
        ((projected[:, :model_width] + query_shift.astype(jnp.float32)) * SCALING)
        .astype(jnp.bfloat16)
        .reshape(row_shape)
    )
    key_rows = projected[:, model_width : 2 * model_width].astype(jnp.bfloat16).reshape(row_shape)
    value_rows = (
        (projected[:, 2 * model_width :] + value_shift.astype(jnp.float32))
        .astype(jnp.bfloat16)
        .reshape(row_shape)
    )
    query_heads = split_heads(query_rows)
    start_state = (
        jnp.full((count, HEADS, span_rows), NEGATIVE, jnp.float32),
        jnp.zeros((count, HEADS, span_rows), jnp.float32),
        jnp.zeros((count, span_rows, HEADS, HEAD_DIM), jnp.float32),
    )
    piece_keys = lax.all_gather(key_rows, "ctx", axis=1, tiled=True)
    piece_values = lax.all_gather(value_rows, "ctx", axis=1, tiled=True)
    piece_segs = lax.all_gather(segments, "ctx", axis=1, tiled=True)
    piece_places = jnp.arange(piece_keys.shape[1], dtype=jnp.int32)
    row_max, row_sum, acc_out = forward_block(
        start_state,
        query_heads,
        piece_keys,
        piece_values,
        segments,
        piece_segs,
        places,
        piece_places,
    )
    attended_exact = acc_out / jnp.swapaxes(row_sum, 1, 2)[..., None]
    log_total = jnp.swapaxes(row_max + jnp.log(row_sum), 1, 2)
    attended = attended_exact.reshape(total_rows, model_width).astype(jnp.bfloat16)
    residual = (
        flat
        + jnp.dot(attended, out_full, preferred_element_type=jnp.float32)
        + out_shift.astype(jnp.float32)
    )
    normed_two = layer_norm(
        residual, gain_two.astype(jnp.float32), shift_two.astype(jnp.float32)
    ).astype(jnp.bfloat16)
    hidden = jnp.dot(normed_two, up_full, preferred_element_type=jnp.float32) + up_shift.astype(
        jnp.float32
    )
    active = jax.nn.gelu(hidden).astype(jnp.bfloat16)
    result = (
        residual
        + jnp.dot(active, down_full, preferred_element_type=jnp.float32)
        + down_shift.astype(jnp.float32)
    )
    output = result.astype(jnp.bfloat16).reshape(row_shape)
    regathered = (
        lax.all_gather(ln1_gain, ("dp", "ctx"), axis=0, tiled=True),
        lax.all_gather(ln1_bias, ("dp", "ctx"), axis=0, tiled=True),
        lax.all_gather(w_qkv, ("dp", "ctx"), axis=0, tiled=True),
        lax.all_gather(bias_query, ("dp", "ctx"), axis=0, tiled=True),
        lax.all_gather(bias_value, ("dp", "ctx"), axis=0, tiled=True),
        lax.all_gather(w_out, ("dp", "ctx"), axis=0, tiled=True),
        lax.all_gather(bias_out, ("dp", "ctx"), axis=0, tiled=True),
        lax.all_gather(ln2_gain, ("dp", "ctx"), axis=0, tiled=True),
        lax.all_gather(ln2_bias, ("dp", "ctx"), axis=0, tiled=True),
        lax.all_gather(w_up, ("dp", "ctx"), axis=0, tiled=True),
        lax.all_gather(bias_up, ("dp", "ctx"), axis=0, tiled=True),
        lax.all_gather(w_down, ("dp", "ctx"), axis=0, tiled=True),
        lax.all_gather(bias_down, ("dp", "ctx"), axis=0, tiled=True),
    )
    (
        gain_one,
        shift_one,
        qkv_full,
        query_shift,
        value_shift,
        out_full,
        out_shift,
        gain_two,
        shift_two,
        up_full,
        up_shift,
        down_full,
        down_shift,
    ) = regathered
    upstream = cotangent.reshape(total_rows, model_width)
    upstream_wide = upstream.astype(jnp.float32)
    grad_w_down = contract_rows(active, upstream)
    grad_bias_down = jnp.sum(upstream_wide, axis=0)
    grad_active = contract_cols(upstream, down_full)
    gelu_back = jax.vjp(jax.nn.gelu, hidden)[1]
    grad_hidden = gelu_back(grad_active)[0].astype(jnp.bfloat16)
    grad_bias_up = jnp.sum(grad_hidden.astype(jnp.float32), axis=0)
    grad_w_up = contract_rows(normed_two, grad_hidden)
    grad_normed_two = contract_cols(grad_hidden, up_full)
    norm_two_back = jax.vjp(
        layer_norm, residual, gain_two.astype(jnp.float32), shift_two.astype(jnp.float32)
    )[1]
    grad_from_norm, grad_ln2_gain, grad_ln2_bias = norm_two_back(grad_normed_two)
    grad_residual = upstream_wide + grad_from_norm
    grad_bias_out = jnp.sum(grad_residual, axis=0)
    grad_residual_low = grad_residual.astype(jnp.bfloat16)
    grad_w_out = contract_rows(attended, grad_residual_low)
    grad_attended = (
        contract_cols(grad_residual_low, out_full).astype(jnp.bfloat16).reshape(row_shape)
    )
    grad_heads = split_heads(grad_attended)
    delta_sum = jnp.sum(grad_heads.astype(jnp.float32) * attended_exact, axis=-1)
    total_high = log_total.astype(jnp.bfloat16)
    total_low = (log_total - total_high.astype(jnp.float32)).astype(jnp.bfloat16)
    delta_high = delta_sum.astype(jnp.bfloat16)
    delta_low = (delta_sum - delta_high.astype(jnp.float32)).astype(jnp.bfloat16)
    total_used = total_high.astype(jnp.float32) + total_low.astype(jnp.float32)
    delta_used = delta_high.astype(jnp.float32) + delta_low.astype(jnp.float32)
    key_heads = split_heads(key_rows)
    value_heads = split_heads(value_rows)
    query_mine = (query_heads, grad_heads, total_used, delta_used, segments, places)
    key_mine = (key_heads, value_heads, segments, places)
    grad_query = query_side(
        query_mine,
        (
            lax.all_gather(key_rows, "ctx", axis=1, tiled=True),
            lax.all_gather(value_rows, "ctx", axis=1, tiled=True),
            lax.all_gather(segments, "ctx", axis=1, tiled=True),
        ),
    )
    grad_key, grad_value = key_side(
        key_mine,
        (
            lax.all_gather(query_rows, "ctx", axis=1, tiled=True),
            lax.all_gather(grad_attended, "ctx", axis=1, tiled=True),
            lax.all_gather(total_high, "ctx", axis=1, tiled=True),
            lax.all_gather(total_low, "ctx", axis=1, tiled=True),
            lax.all_gather(delta_high, "ctx", axis=1, tiled=True),
            lax.all_gather(delta_low, "ctx", axis=1, tiled=True),
            lax.all_gather(segments, "ctx", axis=1, tiled=True),
        ),
    )
    query_part = (grad_query.astype(jnp.bfloat16) * SCALING).reshape(total_rows, model_width)
    key_part = grad_key.astype(jnp.bfloat16).reshape(total_rows, model_width)
    value_part = grad_value.astype(jnp.bfloat16).reshape(total_rows, model_width)
    grad_projected = jnp.concatenate([query_part, key_part, value_part], axis=1)
    grad_bias_query = jnp.sum(query_part.astype(jnp.float32), axis=0)
    grad_bias_value = jnp.sum(value_part.astype(jnp.float32), axis=0)
    grad_w_qkv = contract_rows(normed, grad_projected)
    grad_normed = contract_cols(grad_projected, qkv_full)
    norm_one_back = jax.vjp(
        layer_norm, flat, gain_one.astype(jnp.float32), shift_one.astype(jnp.float32)
    )[1]
    grad_from_first, grad_ln1_gain, grad_ln1_bias = norm_one_back(grad_normed)
    grad_tokens = (grad_residual + grad_from_first).astype(jnp.bfloat16).reshape(row_shape)
    owned = (
        lax.psum_scatter(grad_ln1_gain, ("dp", "ctx"), scatter_dimension=0, tiled=True),
        lax.psum_scatter(grad_ln1_bias, ("dp", "ctx"), scatter_dimension=0, tiled=True),
        lax.psum_scatter(grad_w_qkv, ("dp", "ctx"), scatter_dimension=0, tiled=True),
        lax.psum_scatter(grad_bias_query, ("dp", "ctx"), scatter_dimension=0, tiled=True),
        lax.psum_scatter(grad_bias_value, ("dp", "ctx"), scatter_dimension=0, tiled=True),
        lax.psum_scatter(grad_w_out, ("dp", "ctx"), scatter_dimension=0, tiled=True),
        lax.psum_scatter(grad_bias_out, ("dp", "ctx"), scatter_dimension=0, tiled=True),
        lax.psum_scatter(grad_ln2_gain, ("dp", "ctx"), scatter_dimension=0, tiled=True),
        lax.psum_scatter(grad_ln2_bias, ("dp", "ctx"), scatter_dimension=0, tiled=True),
        lax.psum_scatter(grad_w_up, ("dp", "ctx"), scatter_dimension=0, tiled=True),
        lax.psum_scatter(grad_bias_up, ("dp", "ctx"), scatter_dimension=0, tiled=True),
        lax.psum_scatter(grad_w_down, ("dp", "ctx"), scatter_dimension=0, tiled=True),
        lax.psum_scatter(grad_bias_down, ("dp", "ctx"), scatter_dimension=0, tiled=True),
    )
    return (
        output,
        grad_tokens,
        owned[0],
        owned[1],
        owned[2],
        owned[3],
        owned[4],
        owned[5],
        owned[6],
        owned[7],
        owned[8],
        owned[9],
        owned[10],
        owned[11],
        owned[12],
    )


AXES = ("dp", "ctx")
WORK = {
    "attend": 8.0,
    "hidden": 5.5,
    "feed": 4.5,
    "attend_back": 10.0,
    "project_back": 5.0,
    "attend_grad": 2.5,
    "project_out": 2.4,
}
PACE = 1.15e9 * 0.01
LANES = 128
BIG = -1e30
ROOT = math.sqrt(2.0 / math.pi)
CUBIC = 0.044715
F32 = jnp.float32
BF16 = jnp.bfloat16


def dot(left, right, contract=((1,), (0,))):
    return lax.dot_general(left, right, (contract, ((), ())), preferred_element_type=F32)


def normalize(values):
    center = values - jnp.mean(values, axis=-1, keepdims=True)
    factor = lax.rsqrt(jnp.mean(center * center, axis=-1, keepdims=True) + EPSILON)
    return center * factor, factor


def norm_back(grad, normal, factor):
    return factor * (
        grad
        - jnp.mean(grad, axis=-1, keepdims=True)
        - normal * jnp.mean(grad * normal, axis=-1, keepdims=True)
    )


def size_of(shape, dtype):
    lanes = -(-shape[-1] // LANES) * LANES
    rows = -(-shape[-2] // 16) * 16 if len(shape) > 1 else 16
    lead = math.prod(shape[:-2]) if len(shape) > 2 else 1
    return lead * rows * lanes * jnp.dtype(dtype).itemsize


def run(name, body, place, args, outs, scratch=(), far=(), extra=8 << 20):
    held = sum(size_of(s, d) for s, d in scratch)
    held += sum(size_of(args[i].shape, args[i].dtype) for i in far)
    held += sum(size_of(s, d) for s, d in outs)
    whole = pl.BlockSpec(memory_space=pltpu.VMEM)
    specs = [pl.BlockSpec(memory_space=pltpu.HBM) if i in far else whole for i in range(len(args))]
    buffers = [pltpu.VMEM(s, d) for s, d in scratch]

    def fetching(place, *refs):
        near, sems = list(refs[: -len(far) - 1]), refs[-1]
        copies = []
        for k, (i, ref) in enumerate(zip(far, refs[-len(far) - 1 : -1])):
            copies.append(pltpu.make_async_copy(near[i], ref, sems.at[k]))
            copies[-1].start()
            near[i] = ref
        for copy in copies:
            copy.wait()
        body(place, *near)

    if far:
        buffers += [pltpu.VMEM(args[i].shape, args[i].dtype) for i in far]
        buffers += [pltpu.SemaphoreType.DMA((len(far),))]
    return pl.pallas_call(
        fetching if far else body,
        name=name,
        out_shape=[jax.ShapeDtypeStruct(s, d) for s, d in outs],
        in_specs=[pl.BlockSpec(memory_space=pltpu.SMEM)] + specs,
        out_specs=[whole] * len(outs),
        scratch_shapes=buffers,
        compiler_params=pltpu.CompilerParams(vmem_limit_bytes=min(held + extra, 56 << 20)),
        cost_estimate=pl.CostEstimate(
            flops=int(WORK.get(name, 1.5) * PACE), bytes_accessed=1, transcendentals=0
        ),
    )(place, *args)


def rows_at(start, size, align):
    return pl.ds(pl.multiple_of(start, align), size)


class Grid:
    def __init__(self, dp, ctx):
        self.dp, self.ctx = dp, ctx
        self.ny, self.nx, self.nz = 2, dp // 2, ctx // 2

    def move(self, value, step):
        pairs = []
        for i in range(self.dp * self.ctx):
            core, z = i % 2, (i // 2) % self.nz
            x, y = (i // self.ctx) % self.nx, i // (self.ctx * self.nx)
            y, x, z, core = step(y, x, z, core)
            pairs.append((i, ((y * self.nx + x) * self.nz + z) * 2 + core))
        return lax.ppermute(value, AXES, pairs)

    def core(self, value):
        return self.move(value, lambda y, x, z, c: (y, x, z, 1 - c))

    def along_x(self, value):
        return self.move(value, lambda y, x, z, c: (y, 1 - x, z, c))

    def along_y(self, value):
        return self.move(value, lambda y, x, z, c: (1 - y, x, z, c))

    def along_xy(self, value):
        return self.move(value, lambda y, x, z, c: (1 - y, 1 - x, z, c))

    def along_z(self, value, hop):
        return self.move(value, lambda y, x, z, c: (y, x, (z + hop) % self.nz, c))


    def lines(self):
        return [[2 * z + core for z in range(self.nz)] for core in range(2)]

    def gather_z(self, value):
        return lax.all_gather(value, "ctx", axis=0, tiled=True, axis_index_groups=self.lines())

    def gather_chips(self, value):
        count = self.dp * self.ctx
        groups = [list(range(core, count, 2)) for core in range(2)]
        return lax.all_gather(value, AXES, axis=0, tiled=True, axis_index_groups=groups)

    def scatter_z(self, value):
        return lax.psum_scatter(
            value, "ctx", scatter_dimension=0, tiled=True, axis_index_groups=self.lines()
        )


def from_z(z, hop):
    return lax.rem(z - hop + 4, 4)


def order_kernel(place, own, r1, r2, r3, out):
    z = place[2]
    out[z] = own[...]
    out[from_z(z, 1)] = r1[...]
    out[from_z(z, 2)] = r2[...]
    out[from_z(z, 3)] = r3[...]


def block_index(place):
    y, x = place[0], place[1]
    return (2 * y + x, 2 * y + 1 - x, 2 * (1 - y) + x, 2 * (1 - y) + 1 - x)


def fold(block):
    rows = block.shape[0] // 2
    return jnp.concatenate([block[:rows], block[rows:]], axis=1)


def deal(place, blocks, targets):
    for hop, target in enumerate(targets):
        target[...] = blocks[lax.rem(place[2] + hop, 4)]


def unfold(ref, lanes):
    return jnp.concatenate([ref[:, :lanes], ref[:, lanes:]], axis=0)


def seen(seg_col, seg_row, i, span):
    keys = span * (i + 1)
    same = seg_col[i * span : (i + 1) * span] == seg_row[:, :keys]
    place_q = i * span + lax.broadcasted_iota(jnp.int32, (span, keys), 0)
    place_k = lax.broadcasted_iota(jnp.int32, (span, keys), 1)
    return jnp.where(same & (place_q >= place_k), 0.0, BIG).astype(F32)


def attend_kernel(
    place,
    own,
    other,
    b0,
    bx,
    by,
    bxy,
    seg_row,
    seg_col,
    weight,
    vectors,
    normed,
    rows,
    exact,
    totals,
    out_own,
    out_1,
    out_2,
    out_3,
    lifted,
    spare,
    out,
):
    core, second = place[3], place[2] % 2 == 1
    lines, run_rows, width = own.shape
    group = width // 4
    span = 2 * run_rows
    part = b0.shape[0] * b0.shape[1]
    cut = weight.shape[1]
    for index, piece in zip(block_index(place), (b0, bx, by, bxy)):
        for k in range(piece.shape[0]):
            here = rows_at(index * part + k * piece.shape[1], piece.shape[1], 16)
            weight[here] = piece[k, :, :cut]
    vectors[...] = jnp.transpose(weight[:, 4 * LANES :].astype(F32))[64:80]
    gain, shift = vectors[0:1, :], vectors[1:2, :]
    mine = pl.ds(pl.multiple_of(core * 2 * group, LANES), 2 * group)
    bias_q, bias_v = vectors[2:3, mine], vectors[3:4, mine]
    bias_q = jnp.where(second, bias_q[:, group:], bias_q[:, :group])
    bias_v = jnp.where(second, bias_v[:, group:], bias_v[:, :group])
    for i in range(lines):
        spare[i, rows_at(core * run_rows, run_rows, 16)] = own[i]
        spare[i, rows_at((1 - core) * run_rows, run_rows, 16)] = other[i]
    for i in range(lines):
        here = slice(i * span, (i + 1) * span)
        value = (normalize(spare[i].astype(F32))[0] * gain + shift).astype(BF16)
        normed[here] = value
        projected = dot(value, weight[:, : 3 * group])
        rows[here, :group] = ((projected[:, :group] + bias_q) * SCALING).astype(BF16)
        rows[here, group : 2 * group] = projected[:, group : 2 * group].astype(BF16)
        rows[here, 2 * group :] = (projected[:, 2 * group :] + bias_v).astype(BF16)
    for i in range(lines):
        here = slice(i * span, (i + 1) * span)
        keys = span * (i + 1)
        bias = seen(seg_col, seg_row, i, span)
        heads = []
        for h in range(3):
            at = h * HEAD_DIM
            query = rows[here, at : at + HEAD_DIM]
            key = rows[:keys, group + at : group + at + HEAD_DIM]
            value = rows[:keys, 2 * group + at : 2 * group + at + HEAD_DIM]
            scores = dot(query, key, ((1,), (1,))) + bias
            peak = jnp.max(scores, axis=-1, keepdims=True)
            expanded = jnp.exp(scores - peak)
            total = jnp.sum(expanded, axis=-1, keepdims=True)
            mixed = dot(expanded.astype(BF16), value) / total
            heads.append(mixed.astype(BF16))
            exact[here, at : at + HEAD_DIM] = mixed
            totals[here, h : h + 1] = peak + jnp.log(total)
        out[i] = fold(jnp.concatenate(heads, axis=1))
    deal(place, out, (out_own, out_1, out_2, out_3))
    held = vectors[8:12, mine]
    few = 2 * group // 16
    for j in range(16):
        for k in range(4):
            at = (4 * j + k) * few
            lifted[:, at : at + few] = held[k : k + 1, j * few : (j + 1) * few]


def out_kernel(place, own, r1, r2, r3, weight, attended, *partial):
    z = place[2]
    span, group = attended.shape[1:]
    attended[z] = unfold(own, group)
    for hop, piece in ((1, r1), (2, r2), (3, r3)):
        attended[from_z(z, hop)] = unfold(piece, group)
    for s in range(2):
        partial[s][...] = (
            dot(attended[2 * s], weight[:group]) + dot(attended[2 * s + 1], weight[group:])
        ).astype(BF16)


def place_rows(core, target, own, other):
    run_rows = own.shape[0] // 2
    for s in range(2):
        for which, piece in ((core, own), (1 - core, other)):
            target[rows_at((2 * s + which) * run_rows, run_rows, 16)] = piece[
                s * run_rows : (s + 1) * run_rows
            ]


def hidden_kernel(
    place,
    tokens_own,
    tokens_other,
    part_first,
    part_second,
    other_first,
    other_second,
    cot_own,
    cot_other,
    up,
    vectors,
    bias_up,
    cot,
    residual,
    normed,
    active,
    slope,
    tokens,
):
    place_rows(place[3], cot, cot_own, cot_other)
    place_rows(place[3], tokens, tokens_own, tokens_other)
    gain, shift, bias_out = vectors[5:6, :], vectors[6:7, :], vectors[4:5, :]
    span = tokens.shape[0] // 2
    for s in range(2):
        here = slice(s * span, (s + 1) * span)
        one, two = ((part_first, other_first), (part_second, other_second))[s]
        wide = tokens[here].astype(F32) + (one[...].astype(F32) + two[...].astype(F32)) + bias_out
        residual[here] = wide
        low = (normalize(wide)[0] * gain + shift).astype(BF16)
        normed[here] = low
        hidden = dot(low, up[...]) + bias_up[...]
        square = hidden * hidden
        bent = jnp.tanh(ROOT * (hidden + CUBIC * (square * hidden)))
        active[here] = (0.5 * hidden * (1.0 + bent)).astype(BF16)
        slope[here] = 0.5 * (1.0 + bent) + 0.5 * hidden * (1.0 - bent * bent) * (
            ROOT * (1.0 + 3.0 * CUBIC * square)
        )


def down_weights_kernel(place, active, cot, down_own, *targets):
    *targets, spare = targets
    core = place[3]
    spare[...] = dot(active[...], cot[...], ((0,), (0,))).astype(BF16)
    width = cot.shape[1]
    for j in range(8):
        for k in range(2):
            lanes = slice(k * width, (k + 1) * width)
            here = 192 * j + 48 * k
            down_own[48 * j : 48 * j + 48, lanes] = spare[rows_at(here + 96 * core, 48, 16)]
            targets[j // 3][48 * (j % 3) : 48 * (j % 3) + 48, lanes] = spare[
                rows_at(here + 96 * (1 - core), 48, 16)
            ]


def feed_kernel(
    place,
    residual,
    active,
    slope,
    cot,
    up,
    down,
    grad_hidden,
    result,
    grad_normed,
    low_first,
    low_second,
    sums,
    lifted,
):
    span = cot.shape[0] // 2
    for s in range(2):
        here = slice(s * span, (s + 1) * span)
        upstream = cot[here]
        grad = (dot(upstream, down[...], ((1,), (1,))) * slope[here]).astype(BF16)
        grad_hidden[here] = grad
        back = dot(grad, up[...], ((1,), (1,)))
        grad_normed[here] = back
        (low_first, low_second)[s][...] = back.astype(BF16)
        result[here] = dot(active[here], down[...])
        rows = jnp.concatenate(
            [
                jnp.sum(back * normalize(residual[here])[0], axis=0, keepdims=True),
                jnp.sum(back, axis=0, keepdims=True),
                0.5 * jnp.sum(upstream.astype(F32), axis=0, keepdims=True),
            ],
            axis=0,
        )
        total = jnp.sum(grad.astype(F32), axis=0, keepdims=True)
        if s == 0:
            sums[...] = rows
        else:
            sums[...] = sums[...] + rows
            held = first + total
        first = total
    few = held.shape[1] // 64
    for j in range(16):
        for k in range(4):
            at = (4 * j + k) * few
            lifted[k : k + 1, j * few : (j + 1) * few] = held[:, at : at + few]


def up_weights_kernel(place, normed, grad_hidden, grad_up):
    grad_up[...] = dot(normed[...], grad_hidden[...], ((0,), (0,))).astype(BF16)


def attend_grad_kernel(
    place,
    back_own,
    other_first,
    other_second,
    residual,
    cot,
    vectors,
    weight,
    attended,
    grad_residual,
    deal_own,
    deal_1,
    deal_2,
    deal_3,
    out_own,
    out_other,
    sum_out,
    spare,
    blocks,
):
    core = place[3]
    gain = vectors[5:6, :]
    span = cot.shape[0] // 2
    group = attended.shape[2]
    half = 2 * group
    products = [None, None]
    for s in range(2):
        here = slice(s * span, (s + 1) * span)
        normal, factor = normalize(residual[here])
        wide = cot[here].astype(F32) + norm_back(
            (back_own[here] + (other_first, other_second)[s][...].astype(F32)) * gain,
            normal,
            factor,
        )
        grad_residual[here] = wide
        low = wide.astype(BF16)
        grad = dot(low, weight[...], ((1,), (1,))).astype(BF16)
        total = 0.5 * jnp.sum(wide, axis=0, keepdims=True)
        sum_out[...] = total if s == 0 else sum_out[...] + total
        for g in range(2):
            blocks[2 * s + g] = fold(grad[:, g * group : (g + 1) * group])
            product = dot(attended[2 * s + g], low, ((0,), (0,)))
            products[g] = product if s == 0 else products[g] + product
    deal(place, blocks, (deal_own, deal_1, deal_2, deal_3))
    for g in range(2):
        spare[g * group : (g + 1) * group] = products[g].astype(BF16)
    out_own[...] = spare[:, rows_at(core * half, half, LANES)]
    out_other[...] = spare[:, rows_at((1 - core) * half, half, LANES)]


def attend_back_kernel(
    place,
    rows,
    exact,
    totals,
    seg_row,
    seg_col,
    own,
    r1,
    r2,
    r3,
    joined,
    grad,
    keys_grad,
):
    z = place[2]
    span, group = rows.shape[0] // 4, grad.shape[1]
    grad[rows_at(z * span, span, span)] = unfold(own, group)
    for hop, piece in ((1, r1), (2, r2), (3, r3)):
        grad[rows_at(from_z(z, hop) * span, span, span)] = unfold(piece, group)
    for i in (3, 2, 1, 0):
        here = slice(i * span, (i + 1) * span)
        keys = span * (i + 1)
        bias = seen(seg_col, seg_row, i, span)
        for h in range(3):
            at = h * HEAD_DIM
            lanes = slice(at, at + HEAD_DIM)
            query = rows[here, lanes]
            key = rows[:keys, group + at : group + at + HEAD_DIM]
            value = rows[:keys, 2 * group + at : 2 * group + at + HEAD_DIM]
            upstream = grad[here, lanes]
            delta = jnp.sum(upstream.astype(F32) * exact[here, lanes], axis=-1, keepdims=True)
            probs = jnp.exp(dot(query, key, ((1,), (1,))) + bias - totals[here, h : h + 1])
            slopes = dot(upstream, value, ((1,), (1,)))
            grad_scores = (probs * (slopes - delta)).astype(BF16)
            grad_query = dot(grad_scores, key).astype(BF16)
            joined[here, lanes] = (grad_query.astype(F32) * SCALING).astype(BF16)
            grad_key = dot(grad_scores, query, ((0,), (0,)))
            grad_value = dot(probs.astype(BF16), upstream, ((0,), (0,)))
            if i == 3:
                keys_grad[2 * h] = grad_key
                keys_grad[2 * h + 1] = grad_value
            else:
                keys_grad[2 * h, :keys] = keys_grad[2 * h, :keys] + grad_key
                keys_grad[2 * h + 1, :keys] = keys_grad[2 * h + 1, :keys] + grad_value
    for h in range(3):
        for k in range(2):
            at = (k + 1) * group + h * HEAD_DIM
            joined[:, at : at + HEAD_DIM] = keys_grad[2 * h + k].astype(BF16)


def project_back_kernel(
    place,
    joined,
    weight,
    normed,
    tokens_own,
    tokens_other,
    sum_out,
    sums_two,
    lifted,
    o_own,
    o_x,
    o_y,
    o_xy,
    back_own,
    back_first,
    back_second,
    back_third,
    product,
    small,
):
    core = place[3]
    second = place[2] % 2 == 1
    lines, run_rows, width = tokens_own.shape
    span, group = 2 * run_rows, width // 4
    small[...] = jnp.zeros_like(small)
    small[4:5] = sum_out[...]
    small[5:8] = sums_two[...]
    small[8:12, pl.ds(pl.multiple_of(core * 2 * group, LANES), 2 * group)] = lifted[...]
    mine = pl.ds(pl.multiple_of(core * 2 * group, LANES), 2 * group)
    empty = jnp.zeros((1, group), F32)
    for row, at in ((2, 0), (3, 2 * group)):
        total = jnp.sum(joined[:, at : at + group].astype(F32), axis=0, keepdims=True)
        small[row : row + 1, mine] = jnp.where(
            second,
            jnp.concatenate([empty, total], axis=1),
            jnp.concatenate([total, empty], axis=1),
        )
    for i in range(lines):
        for which, tokens in ((core, tokens_own), (1 - core, tokens_other)):
            here = rows_at(i * span + which * run_rows, run_rows, 16)
            step = dot(joined[here], weight[:, : 3 * group], ((1,), (1,)))
            if tokens is tokens_own:
                back_own[i] = step
            else:
                low = step.astype(BF16)
                for target, start in ((back_first, 0), (back_second, 192), (back_third, 384)):
                    first = max(start, i * run_rows)
                    last = min(start + target.shape[0], (i + 1) * run_rows)
                    if first < last:
                        target[first - start : last - start] = low[
                            first - i * run_rows : last - i * run_rows
                        ]
            normal = normalize(tokens[i].astype(F32))[0]
            small[0:1] = small[0:1] + jnp.sum(step * normal, axis=0, keepdims=True)
            small[1:2] = small[1:2] + jnp.sum(step, axis=0, keepdims=True)
    product[:, : 3 * group] = dot(normed[...], joined[...], ((0,), (0,))).astype(BF16)
    product[:, 3 * group :] = jnp.transpose(small[...])[:, :64].astype(BF16)
    size = o_own.shape[0]
    for index, target in zip(block_index(place), (o_own, o_x, o_y, o_xy)):
        target[...] = product[rows_at(index * size, size, 16)]


def split_kernel(targets, size, block, place):
    y, x = place[0], place[1]
    own, over_x, over_y, low, high = targets
    block(y, x, slice(0, size), own)
    block(y, 1 - x, slice(0, size), over_x)
    block(1 - y, x, slice(0, size), over_y)
    block(1 - y, 1 - x, slice(0, size // 2), low)
    block(1 - y, 1 - x, slice(size // 2, size), high)


def split_down_kernel(place, own, first, second, third, *targets):
    *targets, other = targets
    core, size = place[3], targets[0].shape[0]
    other[:144] = first[...]
    other[144:288] = second[...]
    other[288:] = third[...]

    def block(y, x, rows, target):
        here = rows_at(x * size + rows.start, rows.stop - rows.start, 16)
        target[...] = jnp.where(y == core, own[here], other[here])

    split_kernel(targets, size, block, place)


def split_up_kernel(place, up, out_own, out_other, *targets):
    core, size = place[3], targets[0].shape[0]
    cut = up.shape[1]

    def block(y, x, rows, target):
        count = rows.stop - rows.start
        target[:, :cut] = up[rows_at((2 * y + x) * size + rows.start, count, 16)]
        here = rows_at(x * size + rows.start, count, 16)
        target[:, cut:] = jnp.where(y == core, out_own[here], out_other[here])

    split_kernel(targets, size, block, place)


def collect_kernel(place, over_x, over_y, low, high, sum_x, sum_y):
    half = low.shape[0]
    sum_x[:half] = over_x[:half]
    sum_x[half:] = (over_x[half:].astype(F32) + high[...].astype(F32)).astype(BF16)
    sum_y[:half] = (over_y[:half].astype(F32) + low[...].astype(F32)).astype(BF16)
    sum_y[half:] = over_y[half:]


def spread_kernel(place, own, from_x, from_y, low, high, up, down):
    half = low.shape[0]
    cut = up.shape[2]
    blocks = block_index(place)
    for index, piece in zip(blocks, (own, from_x, from_y)):
        up[index] = piece[:, :cut]
        down[index] = piece[:, cut:]
    up[blocks[3], :half] = low[:, :cut]
    up[blocks[3], half:] = high[:, :cut]
    down[blocks[3], :half] = low[:, cut:]
    down[blocks[3], half:] = high[:, cut:]


def sum_plane_kernel(place, a, b, c, d, own, z1, z2, z3, spare):
    z = place[2]
    spare[...] = (
        (a[...].astype(F32) + b[...].astype(F32)) + (c[...].astype(F32) + d[...].astype(F32))
    ).astype(BF16)
    size = own.shape[0]
    for hop, target in enumerate((own, z1, z2, z3)):
        target[...] = spare[rows_at(lax.rem(z + hop, 4) * size, size, 16)]


def line_deal_kernel(place, own, from_x, from_y, *targets):
    *targets, spare = targets
    spare[...] = (
        own[...].astype(F32) + (from_x[...].astype(F32) + from_y[...].astype(F32))
    ).astype(BF16)
    size = targets[0].shape[0]
    for hop, target in enumerate(targets):
        target[...] = spare[rows_at(lax.rem(place[2] + hop, 4) * size, size, 16)]


def line_down_kernel(place, a, b, c, d, down):
    rows, width = down.shape[0] // 2, down.shape[1]
    for k in range(2):
        here = (slice(0, rows), slice(k * width, (k + 1) * width))
        down[k * rows : (k + 1) * rows] = (a[here].astype(F32) + b[here].astype(F32)) + (
            c[here].astype(F32) + d[here].astype(F32)
        )


def deal_all_kernel(place, up, up_x, up_y, qkv, qkv_x, qkv_y, qkv_xy, *targets):
    *targets, spare = targets
    cut = up.shape[1]
    spare[:, :cut] = (
        up[...].astype(F32) + (up_x[...].astype(F32) + up_y[...].astype(F32))
    ).astype(BF16)
    spare[:, cut:] = (
        (qkv[...].astype(F32) + qkv_x[...].astype(F32))
        + (qkv_y[...].astype(F32) + qkv_xy[...].astype(F32))
    ).astype(BF16)
    size = targets[0].shape[0]
    for hop, target in enumerate(targets):
        target[...] = spare[rows_at(lax.rem(place[2] + hop, 4) * size, size, 16)]


def line_all_kernel(place, own, r1, r2, r3, mine, theirs, spare, *, cut):
    second = place[2] % 2 == 1
    third = (own.shape[1] - cut - 64) // 3
    same = own[...].astype(F32) + r2[...].astype(F32)
    cross = r1[...].astype(F32) + r3[...].astype(F32)
    spare[:, :cut] = (same + cross)[:, :cut]
    first, last = jnp.where(second, cross, same), jnp.where(second, same, cross)
    for k in range(3):
        here = slice(cut + k * third, cut + (k + 1) * third)
        at = cut + 2 * k * third
        spare[:, at : at + third] = first[:, here]
        spare[:, at + third : at + 2 * third] = last[:, here]
    at = cut + 6 * third
    spare[:, at : at + 64] = (same + cross)[:, cut + 3 * third :]
    spare[:, at + 64 :] = jnp.zeros((spare.shape[0], 64), F32)
    rows = mine.shape[0]
    mine[...] = spare[rows_at(place[3] * rows, rows, 8)]
    theirs[...] = spare[rows_at((1 - place[3]) * rows, rows, 8)]


def out_split_kernel(place, b0, bx, by, bxy, own, other, spare):
    core = place[3]
    first = b0.shape[2] - own.shape[1]
    size = b0.shape[0] * b0.shape[1]
    for index, piece in zip(block_index(place), (b0, bx, by, bxy)):
        for k in range(piece.shape[0]):
            here = rows_at(index * size + k * piece.shape[1], piece.shape[1], 16)
            spare[here] = piece[k, :, first:]
    half = own.shape[0]
    own[...] = spare[rows_at(core * half, half, 16)]
    other[...] = spare[rows_at((1 - core) * half, half, 16)]


def out_halves_kernel(place, own, other, out):
    core = place[3]
    half = out.shape[0]
    for which, piece in ((core, own), (1 - core, other)):
        out[:, rows_at(which * half, half, LANES)] = piece[...]


def down_halves_kernel(place, own, other, down):
    core = place[3]
    width = down.shape[1]
    for which, piece in ((core, own), (1 - core, other)):
        for j in range(8):
            for k in range(2):
                down[rows_at(192 * j + 96 * which + 48 * k, 48, 16)] = piece[
                    48 * j : 48 * j + 48, k * width : (k + 1) * width
                ]


def deal_back_kernel(place, own, first, second, third, down, down_x, down_y, *targets):
    *targets, spare, total = targets
    lines, rows, width = own.shape
    spare[0:192] = first[...].astype(F32)
    spare[192:384] = second[...].astype(F32)
    spare[384:] = third[...].astype(F32)
    total[...] = (
        down[...].astype(F32) + (down_x[...].astype(F32) + down_y[...].astype(F32))
    ).astype(BF16)
    size = total.shape[0] // 4
    for hop, target in enumerate(targets):
        k = lax.rem(place[2] + hop, 4)
        target[:size] = total[rows_at(k * size, size, 16)]
        block = (own[k] + spare[rows_at(k * rows, rows, rows)]).astype(BF16)
        target[size:] = fold(block)


def final_kernel(place, own, r1, r2, r3, grad_residual, tokens, vectors, out, held):
    z, core = place[2], place[3]
    rows, width = held.shape[1:]
    start = own.shape[0] - rows // 2
    for hop, piece in enumerate((own, r1, r2, r3)):
        held[from_z(z, hop)] = unfold(piece.at[start:], width)
    gain = vectors[0:1, :]
    for s in range(2):
        here = slice(s * rows, (s + 1) * rows)
        there = rows_at((2 * s + core) * rows, rows, 16)
        normal, factor = normalize(tokens[here].astype(F32))
        grad = (held[2 * s].astype(F32) + held[2 * s + 1].astype(F32)) * gain
        out[here] = (grad_residual[there] + norm_back(grad, normal, factor)).astype(BF16)


def split_local(
    grid,
    tokens,
    segments,
    cotangent,
    ln1_gain,
    ln1_bias,
    w_qkv,
    bias_query,
    bias_value,
    w_out,
    bias_out,
    ln2_gain,
    ln2_bias,
    w_up,
    bias_up,
    w_down,
    bias_down,
):
    count, run_rows, width = tokens.shape
    own_rows = count * run_rows
    all_rows = 2 * own_rows
    span = 2 * run_rows
    half = width // 2
    group = half // 2
    hidden_half = w_up.shape[1] // 2
    shard = w_qkv.shape[0]
    dp, ctx = lax.axis_index("dp"), lax.axis_index("ctx")
    y, x, z, core = dp // grid.nx, dp % grid.nx, ctx // 2, ctx % 2
    place = jnp.stack([y, x, z, core]).astype(jnp.int32)
    first_core = core == 0

    def pick(array, index, axis):
        return lax.dynamic_index_in_dim(array, index, axis, keepdims=False)

    def both(own, other, axis):
        return jnp.where(
            first_core,
            jnp.concatenate([own, other], axis),
            jnp.concatenate([other, own], axis),
        )

    def z_all(value):
        return [value] + [grid.along_z(value, hop) for hop in (1, 2, 3)]

    def after(values, *waited):
        return lax.optimization_barrier((values, waited))[0]

    def z_send(blocks):
        return [grid.along_z(blocks[hop], hop) for hop in (1, 2, 3)]

    flat = tokens.reshape(own_rows, width)
    small = jnp.stack(
        [ln1_gain, ln1_bias, bias_query, bias_value, bias_out, ln2_gain, ln2_bias, bias_down], axis=1
    )
    lifted = bias_up.reshape(4, shard).T
    seg_lanes = jnp.pad(segments.astype(BF16).reshape(8, 32), ((0, shard - 8), (0, 0)))
    vector_lanes = jnp.concatenate(
        [small, lifted, jnp.zeros((shard, 4), BF16), seg_lanes, jnp.zeros((shard, 16), BF16)],
        axis=1,
    )
    split_qkv = w_qkv.reshape(shard, 3, 2, half)
    split_up = w_up.reshape(shard, 2, hidden_half)
    split_out = w_out.reshape(shard, 2, half)
    cut = 3 * group + 64
    size = 8 * shard

    def columns(which):
        chosen = pick(split_qkv, which, 2)
        return jnp.concatenate(
            [
                chosen[:, :, :group].reshape(shard, 3 * group),
                vector_lanes,
                chosen[:, :, group:].reshape(shard, 3 * group),
                vector_lanes,
                pick(split_out, which, 1),
                pick(split_up, which, 1),
            ],
            axis=1,
        )

    piece = both(columns(core), grid.core(columns(1 - core)), 0)
    flat_other = grid.core(flat)
    cot_own = cotangent.reshape(own_rows, width)
    cot_other = grid.core(cot_own)
    second_group = lax.rem(z, 2) == 1
    lanes_out = piece[:, 2 * cut : 2 * cut + half]
    first, last = piece[:, :cut], piece[:, cut : 2 * cut]
    piece_same = jnp.concatenate([jnp.where(second_group, last, first), lanes_out], axis=1)
    piece_cross = jnp.concatenate([jnp.where(second_group, first, last), lanes_out], axis=1)
    line_one = [
        piece_same,
        grid.along_z(piece_cross, 1),
        grid.along_z(piece_same, 2),
        grid.along_z(piece_cross, 3),
    ]
    def order(name, pieces):
        return run(name, order_kernel, place, pieces, [((4,) + pieces[0].shape, BF16)])[0]

    def kernel(name, body, args, outs, scratch=(), far=(), extra=6 << 20):
        return run(name, body, place, args, outs, scratch, far, extra)

    line_one = after(line_one, flat_other, cot_other)
    def order_rows(name, pieces):
        lanes = pieces[0].shape[1]
        return kernel(
            name, order_kernel, pieces, [((4, 2 * shard, lanes), BF16)], far=(1, 2, 3)
        )[0].reshape(size, lanes)

    plane_one = order("order_qkv", line_one)
    from_x, from_y, from_xy = (
        grid.along_x(plane_one),
        grid.along_y(plane_one),
        grid.along_xy(plane_one),
    )
    piece_b = jnp.concatenate([w_down[: 2 * shard], w_down[2 * shard :]], axis=1)

    rest_piece = jnp.concatenate([piece[:, 2 * cut + half :], piece_b], axis=1)
    rest_line = z_all(after(rest_piece, line_one))
    token_pieces = [
        grid.along_z(pick(tokens, lax.rem(z + hop, 4) // 2, 0), hop) for hop in (1, 2, 3)
    ]
    token_pieces = after(token_pieces, plane_one)
    gathered = order("order_tokens", [pick(tokens, z // 2, 0)] + token_pieces)
    gathered_rows = gathered.reshape(4 * run_rows, width)
    gathered_other = jnp.concatenate(
        [grid.core(gathered_rows[:192]), grid.core(gathered_rows[192:384]), grid.core(gathered_rows[384:])]
    ).reshape(gathered.shape)
    out_parts = run(
        "out_split",
        out_split_kernel,
        place,
        [plane_one, from_x, from_y, from_xy],
        [((half, half), BF16)] * 2,
        [((width, half), BF16)],
    )
    segs = plane_one.reshape(4, 2, shard, cut + half)[:, :, :8, 3 * group + 16 : 3 * group + 48]
    segs = segs.reshape(4, 2, 2, 4 * 32).transpose(2, 0, 1, 3).reshape(2, 8 * run_rows)
    segs = pick(segs, z // 2, 0).astype(F32)

    weight_qkv, vectors, normed, packed, exact, totals, *out_deal, bias_up_half = kernel(
        "attend",
        attend_kernel,
        [
            gathered,
            gathered_other,
            after(plane_one, out_parts),
            from_x,
            from_y,
            from_xy,
            segs.reshape(1, -1),
            segs.reshape(-1, 1),
        ],
        [
            ((width, cut), BF16),
            ((16, width), F32),
            ((4 * span, width), BF16),
            ((4 * span, 3 * group), BF16),
            ((4 * span, group), F32),
            ((4 * span, LANES), F32),
        ]
        + [((run_rows, 2 * group), BF16)] * 4
        + [((1, hidden_half), F32)],
        [((4, span, width), BF16), ((4, run_rows, 2 * group), BF16)],
        far=(3, 4, 5),
        extra=14 << 20,
    )
    out_blocks = out_deal[0]
    out_pieces = z_send(out_deal)

    weight_out = kernel(
        "out_halves",
        out_halves_kernel,
        [out_parts[0], grid.core(out_parts[1])],
        [((half, width), BF16)],
    )[0]

    plane_rest = order_rows("order_rest", [rest_line[0]] + after(rest_line[1:], out_blocks))
    attended, *partial = kernel(
        "project_out",
        out_kernel,
        [out_blocks] + out_pieces + [weight_out],
        [((4, span, group), BF16)] + [((own_rows, width), BF16)] * 2,
        far=(1, 2, 3),
    )
    part_other = [grid.core(member) for member in partial]
    over = after((grid.along_x(plane_rest), grid.along_y(plane_rest)), part_other)
    low, high = grid.along_x(over[1][: 4 * shard]), grid.along_y(over[0][4 * shard :])
    weight_up, mixed_down = kernel(
        "spread",
        spread_kernel,
        [plane_rest, *over, low, high],
        [((4, size, hidden_half), BF16), ((4, size, 2 * width), BF16)],
        far=(1, 2, 3, 4),
    )
    weight_up = weight_up.reshape(width, hidden_half)
    mixed_down = mixed_down.reshape(2, half, 2 * width)
    cot, residual, normed_two, active, slope = kernel(
        "hidden",
        hidden_kernel,
        [
            flat,
            flat_other,
            *partial,
            *part_other,
            cot_own,
            cot_other,
            weight_up,
            vectors,
            bias_up_half,
        ],
        [
            ((all_rows, width), BF16),
            ((all_rows, width), F32),
            ((all_rows, width), BF16),
            ((all_rows, hidden_half), BF16),
            ((all_rows, hidden_half), F32),
        ],
        [((all_rows, width), BF16)],
        far=(0, 1, 6, 7),
        extra=14 << 20,
    )
    weight_down = kernel(
        "down_halves",
        down_halves_kernel,
        [pick(mixed_down, core, 0), grid.core(pick(mixed_down, 1 - core, 0))],
        [((hidden_half, width), BF16)],
    )[0]

    def halve(array, which):
        return pick(array.reshape(2, 2, run_rows, width), which, 1).reshape(own_rows, width)

    def split(name, body, parts, lanes, scratch=()):
        results = [((size, lanes), BF16)] * 3 + [((size // 2, lanes), BF16)] * 2
        return kernel(name, body, parts, results, scratch)

    def diagonal(parts):
        return grid.along_x(parts[3]), grid.along_y(parts[4])

    def collect(name, parts, low, high):
        sum_x, sum_y = kernel(
            name, collect_kernel, [parts[1], parts[2], low, high], [(parts[1].shape, BF16)] * 2, far=(2, 3)
        )
        return parts[0], grid.along_x(sum_x), grid.along_y(sum_y), sum_x

    grad_hidden, result, back_two, *back_low, sums_two, lifted = kernel(
        "feed",
        feed_kernel,
        [residual, active, slope, cot, weight_up, weight_down],
        [
            ((all_rows, hidden_half), BF16),
            ((all_rows, width), F32),
            ((all_rows, width), F32),
            ((own_rows, width), BF16),
            ((own_rows, width), BF16),
            ((3, width), F32),
            ((4, half), F32),
        ],
        extra=14 << 20,
    )
    back_other = [grid.core(member) for member in back_low]
    grad_up = kernel(
        "up_weights",
        up_weights_kernel,
        [normed_two, grad_hidden],
        [((width, hidden_half), BF16)],
        extra=10 << 20,
    )[0]


    down_own, *down_other = kernel(
        "down_weights",
        down_weights_kernel,
        after([active, cot], grad_up),
        [((rows, 2 * width), BF16) for rows in (half, 144, 144, 96)],
        [((hidden_half, width), BF16)],
        extra=10 << 20,
    )
    down_recv = [grid.core(member) for member in down_other]
    grad_residual, *grad_deal, out_own, out_other, sum_out = kernel(
        "attend_grad",
        attend_grad_kernel,
        after(
            [back_two, *back_other, residual, cot, vectors, weight_out, attended],
            down_own,
        ),
        [
            ((all_rows, width), F32),
            *[((run_rows, 2 * group), BF16)] * 4,
            ((half, half), BF16),
            ((half, half), BF16),
            ((1, width), F32),
        ],
        [((half, width), BF16), ((4, run_rows, 2 * group), BF16)],
    )
    grad_blocks = grad_deal[0]
    grad_pieces = z_send(grad_deal)
    out_recv = grid.core(out_other)
    def split(name, body, parts, lanes, scratch=()):
        results = [((size, lanes), BF16)] * 3 + [((size // 2, lanes), BF16)] * 2
        return kernel(name, body, parts, results, scratch)

    down_parts = split(
        "split_down",
        split_down_kernel,
        [down_own] + down_recv,
        2 * width,
        [((half, 2 * width), BF16)],
    )
    down_low, down_high = diagonal(down_parts)
    up_parts = split(
        "split_up",
        split_up_kernel,
        after([grad_up, out_own, out_recv], down_parts),
        hidden_half + half,
    )
    up_low, up_high = diagonal(up_parts)
    down_low, down_high = after((down_low, down_high), grad_pieces)
    down_parts = collect("collect_down", down_parts, down_low, down_high)

    result, residual = after((result, residual), up_parts)
    result_other = grid.core(halve(result, 1 - core))
    output = (
        halve(residual, core)
        + (halve(result, core) + result_other)
        + vectors[7:8]
    ).astype(BF16)

    grad_pieces = after(grad_pieces, up_parts, down_parts[3], output)
    grad_joined = kernel(
        "attend_back",
        attend_back_kernel,
        [packed, exact, totals, segs.reshape(1, -1), segs.reshape(-1, 1), grad_blocks]
        + grad_pieces,
        [((4 * span, 3 * group), BF16)],
        [((4 * span, group), BF16), ((6, 4 * span, HEAD_DIM), F32)],
        far=(0, 1, 2, 6, 7, 8),
        extra=14 << 20,
    )[0]
    back_results = kernel(
        "project_back",
        project_back_kernel,
        [grad_joined, weight_qkv, normed, gathered, gathered_other]
        + [sum_out, sums_two, lifted],
        [((size, cut), BF16)] * 4
        + [((4, run_rows, width), F32)]
        + [((192, width), BF16), ((192, width), BF16), ((128, width), BF16)],
        [((width, cut), BF16), ((LANES, width), F32)],
        far=(1, 2, 3, 4),
        extra=10 << 20,
    )
    qkv_parts, back_own, back_low = back_results[:4], back_results[4], back_results[5:]
    up_low, up_high = after((up_low, up_high), back_own)
    up_parts = collect("collect_up", up_parts, up_low, up_high)
    mixed = kernel(
        "deal_back",
        deal_back_kernel,
        [back_own]
        + [grid.core(member) for member in back_low]
        + after(list(down_parts[:3]), up_parts[3]),
        [((2 * shard + run_rows // 2, 2 * width), BF16)] * 4,
        [((4 * run_rows, width), F32), ((size, 2 * width), BF16)],
        far=(5, 6),
    )
    mixed_line = [mixed[0]] + z_send(mixed)
    up_ready = after(list(up_parts[:3]), mixed)
    qkv_parts = [qkv_parts[0]] + after(list(qkv_parts[1:]), up_ready)
    qkv_recv = [grid.along_x(qkv_parts[1]), grid.along_y(qkv_parts[2]), grid.along_xy(qkv_parts[3])]
    up_cut = hidden_half + half
    all_dealt = kernel(
        "deal_all",
        deal_all_kernel,
        after(up_ready, mixed_line) + [qkv_parts[0]] + qkv_recv,
        [((2 * shard, up_cut + cut), BF16)] * 4,
        [((size, up_cut + cut), BF16)],
        far=(1, 2, 4, 5, 6),
    )
    all_line = [all_dealt[0]] + z_send(all_dealt)
    grad_tokens = kernel(
        "final",
        final_kernel,
        mixed_line + [grad_residual, flat, vectors],
        [((own_rows, width), BF16)],
        [((4, run_rows, width), BF16)],
        far=(1, 2, 3, 5),
    )[0]
    grad_down = kernel(
        "line_down", line_down_kernel, mixed_line, [((4 * shard, width), F32)], far=(1, 2, 3)
    )[0]
    all_line = [all_line[0]] + after(all_line[1:], grad_tokens, grad_down)
    mine, theirs = kernel(
        "line_all",
        functools.partial(line_all_kernel, cut=up_cut),
        all_line,
        [((shard, up_cut + 6 * group + LANES), F32)] * 2,
        [((2 * shard, up_cut + 6 * group + LANES), F32)],
        far=(1, 2, 3),
    )
    theirs = grid.core(theirs)
    grad_up_own = both(mine[:, :hidden_half], theirs[:, :hidden_half], 1)
    grad_out_own = both(mine[:, hidden_half:up_cut], theirs[:, hidden_half:up_cut], 1)
    qkv_mine, qkv_theirs = mine[:, up_cut:], theirs[:, up_cut:]
    grad_qkv_own = both(
        qkv_mine[:, : 6 * group].reshape(shard, 3, 1, half),
        qkv_theirs[:, : 6 * group].reshape(shard, 3, 1, half),
        2,
    ).reshape(shard, 6 * half)
    small_sum = (qkv_mine[:, 6 * group : 6 * group + 16] + qkv_theirs[:, 6 * group : 6 * group + 16]).T
    return (
        output.reshape(tokens.shape),
        grad_tokens.reshape(tokens.shape),
        small_sum[0],
        small_sum[1],
        grad_qkv_own,
        small_sum[2],
        small_sum[3],
        grad_out_own,
        small_sum[4],
        small_sum[5],
        small_sum[6],
        grad_up_own,
        small_sum[8:12].reshape(4 * shard),
        grad_down,
        small_sum[7],
    )


def build_local(mesh):
    dp, ctx = mesh.shape["dp"], mesh.shape["ctx"]
    if (dp, ctx) != (4, 8):
        return local_general
    grid = Grid(dp, ctx)
    return lambda *args: split_local(grid, *args)


def solution(mesh):
    return jax.shard_map(
        build_local(mesh),
        mesh=mesh,
        in_specs=(
            P("dp", "ctx", None),
            P("dp", "ctx"),
            P("dp", "ctx", None),
            P(("dp", "ctx")),
            P(("dp", "ctx")),
            P(("dp", "ctx"), None),
            P(("dp", "ctx")),
            P(("dp", "ctx")),
            P(("dp", "ctx"), None),
            P(("dp", "ctx")),
            P(("dp", "ctx")),
            P(("dp", "ctx")),
            P(("dp", "ctx"), None),
            P(("dp", "ctx")),
            P(("dp", "ctx"), None),
            P(("dp", "ctx")),
        ),
        out_specs=(
            P("dp", "ctx", None),
            P("dp", "ctx", None),
            P(("dp", "ctx")),
            P(("dp", "ctx")),
            P(("dp", "ctx"), None),
            P(("dp", "ctx")),
            P(("dp", "ctx")),
            P(("dp", "ctx"), None),
            P(("dp", "ctx")),
            P(("dp", "ctx")),
            P(("dp", "ctx")),
            P(("dp", "ctx"), None),
            P(("dp", "ctx")),
            P(("dp", "ctx"), None),
            P(("dp", "ctx")),
        ),
        check_vma=False,
    )
```

```python
import functools
import math

import jax
import jax.numpy as jnp
from jax import lax
from jax.experimental import pallas as pl
from jax.experimental.pallas import tpu as pltpu
from jax.sharding import PartitionSpec as P

HEADS = 12
HEAD_DIM = 64


EPSILON = 1e-05
NEGATIVE = -1e30
SCALING = 0.125


def layer_norm(values, gain_vec, shift_vec):
    center = values - jnp.mean(values, axis=-1, keepdims=True)
    spread = jnp.mean(center * center, axis=-1, keepdims=True)
    return center * lax.rsqrt(spread + EPSILON) * gain_vec + shift_vec


def split_heads(tensor):
    return tensor.reshape(tensor.shape[0], tensor.shape[1], HEADS, HEAD_DIM)


def visible(seg_query, seg_key, place_query, place_key):
    same_doc = seg_query[:, :, None] == seg_key[:, None, :]
    causal = place_query[None, :, None] >= place_key[None, None, :]
    return (same_doc & causal)[:, None]


def forward_block(
    carry, query_heads, key_rows, value_rows, seg_query, seg_key, place_query, place_key
):
    row_max, row_sum, acc_out = carry
    scores = jnp.einsum(
        "sqhd,skhd->shqk", query_heads, split_heads(key_rows), preferred_element_type=jnp.float32
    )
    allowed = visible(seg_query, seg_key, place_query, place_key)
    scores = jnp.where(allowed, scores, NEGATIVE)
    new_max = jnp.maximum(row_max, jnp.max(scores, axis=-1))
    expanded = jnp.where(allowed, jnp.exp(scores - new_max[..., None]), 0.0)
    factor = jnp.exp(row_max - new_max)
    row_sum = jnp.sum(expanded, axis=-1)
    added = jnp.einsum(
        "shqk,skhd->sqhd",
        expanded.astype(jnp.bfloat16),
        split_heads(value_rows),
        preferred_element_type=jnp.float32,
    )
    acc_out = acc_out * jnp.swapaxes(factor, 1, 2)[..., None] + added
    return (new_max, row_sum, acc_out)


def grad_block(
    query_heads,
    key_heads,
    value_heads,
    grad_heads,
    log_total,
    delta_sum,
    seg_query,
    seg_key,
    place_query,
    place_key,
):
    scores = jnp.einsum(
        "sqhd,skhd->shqk", query_heads, key_heads, preferred_element_type=jnp.float32
    )
    allowed = visible(seg_query, seg_key, place_query, place_key)
    shift_total = jnp.swapaxes(log_total, 1, 2)[..., None]
    probs = jnp.where(allowed, jnp.exp(scores - shift_total), 0.0)
    grad_probs = jnp.einsum(
        "sqhd,skhd->shqk", grad_heads, value_heads, preferred_element_type=jnp.float32
    )
    grad_scores = (probs * (grad_probs - jnp.swapaxes(delta_sum, 1, 2)[..., None])).astype(
        jnp.bfloat16
    )
    return (grad_scores, probs.astype(jnp.bfloat16))


def query_side(mine, theirs):
    query_heads, grad_heads, log_total, delta_sum, seg_mine, place_mine = mine
    key_rows, value_rows, seg_theirs = theirs
    place_theirs = jnp.arange(key_rows.shape[1], dtype=jnp.int32)
    key_heads = split_heads(key_rows)
    outcome = grad_block(
        query_heads,
        key_heads,
        split_heads(value_rows),
        grad_heads,
        log_total,
        delta_sum,
        seg_mine,
        seg_theirs,
        place_mine,
        place_theirs,
    )
    return jnp.einsum("shqk,skhd->sqhd", outcome[0], key_heads, preferred_element_type=jnp.float32)


def key_side(mine, theirs):
    key_heads, value_heads, seg_mine, place_mine = mine
    query_rows, grad_rows, total_high, total_low, delta_high, delta_low, seg_theirs = theirs
    place_theirs = jnp.arange(query_rows.shape[1], dtype=jnp.int32)
    query_heads = split_heads(query_rows)
    grad_heads = split_heads(grad_rows)
    log_total = total_high.astype(jnp.float32) + total_low.astype(jnp.float32)
    delta_sum = delta_high.astype(jnp.float32) + delta_low.astype(jnp.float32)
    grad_scores, probs = grad_block(
        query_heads,
        key_heads,
        value_heads,
        grad_heads,
        log_total,
        delta_sum,
        seg_theirs,
        seg_mine,
        place_theirs,
        place_mine,
    )
    grad_key = jnp.einsum(
        "shqk,sqhd->skhd", grad_scores, query_heads, preferred_element_type=jnp.float32
    )
    grad_value = jnp.einsum(
        "shqk,sqhd->skhd", probs, grad_heads, preferred_element_type=jnp.float32
    )
    return (grad_key, grad_value)


def contract_rows(left, right):
    return lax.dot_general(
        left, right, (((0,), (0,)), ((), ())), preferred_element_type=jnp.float32
    )


def contract_cols(left, right):
    return lax.dot_general(
        left, right, (((1,), (1,)), ((), ())), preferred_element_type=jnp.float32
    )


def local_general(
    tokens,
    segments,
    cotangent,
    ln1_gain,
    ln1_bias,
    w_qkv,
    bias_query,
    bias_value,
    w_out,
    bias_out,
    ln2_gain,
    ln2_bias,
    w_up,
    bias_up,
    w_down,
    bias_down,
):
    count, span_rows, model_width = tokens.shape
    total_rows = count * span_rows
    places = lax.axis_index("ctx") * span_rows + jnp.arange(span_rows, dtype=jnp.int32)
    gathered = (
        lax.all_gather(ln1_gain, ("dp", "ctx"), axis=0, tiled=True),
        lax.all_gather(ln1_bias, ("dp", "ctx"), axis=0, tiled=True),
        lax.all_gather(w_qkv, ("dp", "ctx"), axis=0, tiled=True),
        lax.all_gather(bias_query, ("dp", "ctx"), axis=0, tiled=True),
        lax.all_gather(bias_value, ("dp", "ctx"), axis=0, tiled=True),
        lax.all_gather(w_out, ("dp", "ctx"), axis=0, tiled=True),
        lax.all_gather(bias_out, ("dp", "ctx"), axis=0, tiled=True),
        lax.all_gather(ln2_gain, ("dp", "ctx"), axis=0, tiled=True),
        lax.all_gather(ln2_bias, ("dp", "ctx"), axis=0, tiled=True),
        lax.all_gather(w_up, ("dp", "ctx"), axis=0, tiled=True),
        lax.all_gather(bias_up, ("dp", "ctx"), axis=0, tiled=True),
        lax.all_gather(w_down, ("dp", "ctx"), axis=0, tiled=True),
        lax.all_gather(bias_down, ("dp", "ctx"), axis=0, tiled=True),
    )
    (
        gain_one,
        shift_one,
        qkv_full,
        query_shift,
        value_shift,
        out_full,
        out_shift,
        gain_two,
        shift_two,
        up_full,
        up_shift,
        down_full,
        down_shift,
    ) = gathered
    flat = tokens.reshape(total_rows, model_width).astype(jnp.float32)
    normed = layer_norm(flat, gain_one.astype(jnp.float32), shift_one.astype(jnp.float32)).astype(
        jnp.bfloat16
    )
    projected = jnp.dot(normed, qkv_full, preferred_element_type=jnp.float32)
    row_shape = (count, span_rows, model_width)
    query_rows = (
        ((projected[:, :model_width] + query_shift.astype(jnp.float32)) * SCALING)
        .astype(jnp.bfloat16)
        .reshape(row_shape)
    )
    key_rows = projected[:, model_width : 2 * model_width].astype(jnp.bfloat16).reshape(row_shape)
    value_rows = (
        (projected[:, 2 * model_width :] + value_shift.astype(jnp.float32))
        .astype(jnp.bfloat16)
        .reshape(row_shape)
    )
    query_heads = split_heads(query_rows)
    start_state = (
        jnp.full((count, HEADS, span_rows), NEGATIVE, jnp.float32),
        jnp.zeros((count, HEADS, span_rows), jnp.float32),
        jnp.zeros((count, span_rows, HEADS, HEAD_DIM), jnp.float32),
    )
    piece_keys = lax.all_gather(key_rows, "ctx", axis=1, tiled=True)
    piece_values = lax.all_gather(value_rows, "ctx", axis=1, tiled=True)
    piece_segs = lax.all_gather(segments, "ctx", axis=1, tiled=True)
    piece_places = jnp.arange(piece_keys.shape[1], dtype=jnp.int32)
    row_max, row_sum, acc_out = forward_block(
        start_state,
        query_heads,
        piece_keys,
        piece_values,
        segments,
        piece_segs,
        places,
        piece_places,
    )
    attended_exact = acc_out / jnp.swapaxes(row_sum, 1, 2)[..., None]
    log_total = jnp.swapaxes(row_max + jnp.log(row_sum), 1, 2)
    attended = attended_exact.reshape(total_rows, model_width).astype(jnp.bfloat16)
    residual = (
        flat
        + jnp.dot(attended, out_full, preferred_element_type=jnp.float32)
        + out_shift.astype(jnp.float32)
    )
    normed_two = layer_norm(
        residual, gain_two.astype(jnp.float32), shift_two.astype(jnp.float32)
    ).astype(jnp.bfloat16)
    hidden = jnp.dot(normed_two, up_full, preferred_element_type=jnp.float32) + up_shift.astype(
        jnp.float32
    )
    active = jax.nn.gelu(hidden).astype(jnp.bfloat16)
    result = (
        residual
        + jnp.dot(active, down_full, preferred_element_type=jnp.float32)
        + down_shift.astype(jnp.float32)
    )
    output = result.astype(jnp.bfloat16).reshape(row_shape)
    regathered = (
        lax.all_gather(ln1_gain, ("dp", "ctx"), axis=0, tiled=True),
        lax.all_gather(ln1_bias, ("dp", "ctx"), axis=0, tiled=True),
        lax.all_gather(w_qkv, ("dp", "ctx"), axis=0, tiled=True),
        lax.all_gather(bias_query, ("dp", "ctx"), axis=0, tiled=True),
        lax.all_gather(bias_value, ("dp", "ctx"), axis=0, tiled=True),
        lax.all_gather(w_out, ("dp", "ctx"), axis=0, tiled=True),
        lax.all_gather(bias_out, ("dp", "ctx"), axis=0, tiled=True),
        lax.all_gather(ln2_gain, ("dp", "ctx"), axis=0, tiled=True),
        lax.all_gather(ln2_bias, ("dp", "ctx"), axis=0, tiled=True),
        lax.all_gather(w_up, ("dp", "ctx"), axis=0, tiled=True),
        lax.all_gather(bias_up, ("dp", "ctx"), axis=0, tiled=True),
        lax.all_gather(w_down, ("dp", "ctx"), axis=0, tiled=True),
        lax.all_gather(bias_down, ("dp", "ctx"), axis=0, tiled=True),
    )
    (
        gain_one,
        shift_one,
        qkv_full,
        query_shift,
        value_shift,
        out_full,
        out_shift,
        gain_two,
        shift_two,
        up_full,
        up_shift,
        down_full,
        down_shift,
    ) = regathered
    upstream = cotangent.reshape(total_rows, model_width)
    upstream_wide = upstream.astype(jnp.float32)
    grad_w_down = contract_rows(active, upstream)
    grad_bias_down = jnp.sum(upstream_wide, axis=0)
    grad_active = contract_cols(upstream, down_full)
    gelu_back = jax.vjp(jax.nn.gelu, hidden)[1]
    grad_hidden = gelu_back(grad_active)[0].astype(jnp.bfloat16)
    grad_bias_up = jnp.sum(grad_hidden.astype(jnp.float32), axis=0)
    grad_w_up = contract_rows(normed_two, grad_hidden)
    grad_normed_two = contract_cols(grad_hidden, up_full)
    norm_two_back = jax.vjp(
        layer_norm, residual, gain_two.astype(jnp.float32), shift_two.astype(jnp.float32)
    )[1]
    grad_from_norm, grad_ln2_gain, grad_ln2_bias = norm_two_back(grad_normed_two)
    grad_residual = upstream_wide + grad_from_norm
    grad_bias_out = jnp.sum(grad_residual, axis=0)
    grad_residual_low = grad_residual.astype(jnp.bfloat16)
    grad_w_out = contract_rows(attended, grad_residual_low)
    grad_attended = (
        contract_cols(grad_residual_low, out_full).astype(jnp.bfloat16).reshape(row_shape)
    )
    grad_heads = split_heads(grad_attended)
    delta_sum = jnp.sum(grad_heads.astype(jnp.float32) * attended_exact, axis=-1)
    total_high = log_total.astype(jnp.bfloat16)
    total_low = (log_total - total_high.astype(jnp.float32)).astype(jnp.bfloat16)
    delta_high = delta_sum.astype(jnp.bfloat16)
    delta_low = (delta_sum - delta_high.astype(jnp.float32)).astype(jnp.bfloat16)
    total_used = total_high.astype(jnp.float32) + total_low.astype(jnp.float32)
    delta_used = delta_high.astype(jnp.float32) + delta_low.astype(jnp.float32)
    key_heads = split_heads(key_rows)
    value_heads = split_heads(value_rows)
    query_mine = (query_heads, grad_heads, total_used, delta_used, segments, places)
    key_mine = (key_heads, value_heads, segments, places)
    grad_query = query_side(
        query_mine,
        (
            lax.all_gather(key_rows, "ctx", axis=1, tiled=True),
            lax.all_gather(value_rows, "ctx", axis=1, tiled=True),
            lax.all_gather(segments, "ctx", axis=1, tiled=True),
        ),
    )
    grad_key, grad_value = key_side(
        key_mine,
        (
            lax.all_gather(query_rows, "ctx", axis=1, tiled=True),
            lax.all_gather(grad_attended, "ctx", axis=1, tiled=True),
            lax.all_gather(total_high, "ctx", axis=1, tiled=True),
            lax.all_gather(total_low, "ctx", axis=1, tiled=True),
            lax.all_gather(delta_high, "ctx", axis=1, tiled=True),
            lax.all_gather(delta_low, "ctx", axis=1, tiled=True),
            lax.all_gather(segments, "ctx", axis=1, tiled=True),
        ),
    )
    query_part = (grad_query.astype(jnp.bfloat16) * SCALING).reshape(total_rows, model_width)
    key_part = grad_key.astype(jnp.bfloat16).reshape(total_rows, model_width)
    value_part = grad_value.astype(jnp.bfloat16).reshape(total_rows, model_width)
    grad_projected = jnp.concatenate([query_part, key_part, value_part], axis=1)
    grad_bias_query = jnp.sum(query_part.astype(jnp.float32), axis=0)
    grad_bias_value = jnp.sum(value_part.astype(jnp.float32), axis=0)
    grad_w_qkv = contract_rows(normed, grad_projected)
    grad_normed = contract_cols(grad_projected, qkv_full)
    norm_one_back = jax.vjp(
        layer_norm, flat, gain_one.astype(jnp.float32), shift_one.astype(jnp.float32)
    )[1]
    grad_from_first, grad_ln1_gain, grad_ln1_bias = norm_one_back(grad_normed)
    grad_tokens = (grad_residual + grad_from_first).astype(jnp.bfloat16).reshape(row_shape)
    owned = (
        lax.psum_scatter(grad_ln1_gain, ("dp", "ctx"), scatter_dimension=0, tiled=True),
        lax.psum_scatter(grad_ln1_bias, ("dp", "ctx"), scatter_dimension=0, tiled=True),
        lax.psum_scatter(grad_w_qkv, ("dp", "ctx"), scatter_dimension=0, tiled=True),
        lax.psum_scatter(grad_bias_query, ("dp", "ctx"), scatter_dimension=0, tiled=True),
        lax.psum_scatter(grad_bias_value, ("dp", "ctx"), scatter_dimension=0, tiled=True),
        lax.psum_scatter(grad_w_out, ("dp", "ctx"), scatter_dimension=0, tiled=True),
        lax.psum_scatter(grad_bias_out, ("dp", "ctx"), scatter_dimension=0, tiled=True),
        lax.psum_scatter(grad_ln2_gain, ("dp", "ctx"), scatter_dimension=0, tiled=True),
        lax.psum_scatter(grad_ln2_bias, ("dp", "ctx"), scatter_dimension=0, tiled=True),
        lax.psum_scatter(grad_w_up, ("dp", "ctx"), scatter_dimension=0, tiled=True),
        lax.psum_scatter(grad_bias_up, ("dp", "ctx"), scatter_dimension=0, tiled=True),
        lax.psum_scatter(grad_w_down, ("dp", "ctx"), scatter_dimension=0, tiled=True),
        lax.psum_scatter(grad_bias_down, ("dp", "ctx"), scatter_dimension=0, tiled=True),
    )
    return (
        output,
        grad_tokens,
        owned[0],
        owned[1],
        owned[2],
        owned[3],
        owned[4],
        owned[5],
        owned[6],
        owned[7],
        owned[8],
        owned[9],
        owned[10],
        owned[11],
        owned[12],
    )


AXES = ("dp", "ctx")
WORK = {
    "attend": 8.0,
    "hidden": 5.5,
    "feed": 4.5,
    "attend_back": 10.0,
    "project_back": 5.0,
    "attend_grad": 2.5,
    "project_out": 2.4,
}
PACE = 1.15e9 * 0.01
LANES = 128
BIG = -1e30
ROOT = math.sqrt(2.0 / math.pi)
CUBIC = 0.044715
F32 = jnp.float32
BF16 = jnp.bfloat16


def dot(left, right, contract=((1,), (0,))):
    return lax.dot_general(left, right, (contract, ((), ())), preferred_element_type=F32)


def normalize(values):
    center = values - jnp.mean(values, axis=-1, keepdims=True)
    factor = lax.rsqrt(jnp.mean(center * center, axis=-1, keepdims=True) + EPSILON)
    return center * factor, factor


def norm_back(grad, normal, factor):
    return factor * (
        grad
        - jnp.mean(grad, axis=-1, keepdims=True)
        - normal * jnp.mean(grad * normal, axis=-1, keepdims=True)
    )


def size_of(shape, dtype):
    lanes = -(-shape[-1] // LANES) * LANES
    rows = -(-shape[-2] // 16) * 16 if len(shape) > 1 else 16
    lead = math.prod(shape[:-2]) if len(shape) > 2 else 1
    return lead * rows * lanes * jnp.dtype(dtype).itemsize


def run(name, body, place, args, outs, scratch=(), far=(), extra=8 << 20):
    held = sum(size_of(s, d) for s, d in scratch)
    held += sum(size_of(args[i].shape, args[i].dtype) for i in far)
    held += sum(size_of(s, d) for s, d in outs)
    whole = pl.BlockSpec(memory_space=pltpu.VMEM)
    specs = [pl.BlockSpec(memory_space=pltpu.HBM) if i in far else whole for i in range(len(args))]
    buffers = [pltpu.VMEM(s, d) for s, d in scratch]

    def fetching(place, *refs):
        near, sems = list(refs[: -len(far) - 1]), refs[-1]
        copies = []
        for k, (i, ref) in enumerate(zip(far, refs[-len(far) - 1 : -1])):
            copies.append(pltpu.make_async_copy(near[i], ref, sems.at[k]))
            copies[-1].start()
            near[i] = ref
        for copy in copies:
            copy.wait()
        body(place, *near)

    if far:
        buffers += [pltpu.VMEM(args[i].shape, args[i].dtype) for i in far]
        buffers += [pltpu.SemaphoreType.DMA((len(far),))]
    return pl.pallas_call(
        fetching if far else body,
        name=name,
        out_shape=[jax.ShapeDtypeStruct(s, d) for s, d in outs],
        in_specs=[pl.BlockSpec(memory_space=pltpu.SMEM)] + specs,
        out_specs=[whole] * len(outs),
        scratch_shapes=buffers,
        compiler_params=pltpu.CompilerParams(vmem_limit_bytes=min(held + extra, 56 << 20)),
        cost_estimate=pl.CostEstimate(
            flops=int(WORK.get(name, 1.5) * PACE), bytes_accessed=1, transcendentals=0
        ),
    )(place, *args)


def rows_at(start, size, align):
    return pl.ds(pl.multiple_of(start, align), size)


class Grid:
    def __init__(self, dp, ctx):
        self.dp, self.ctx = dp, ctx
        self.ny, self.nx, self.nz = 2, dp // 2, ctx // 2

    def move(self, value, step):
        pairs = []
        for i in range(self.dp * self.ctx):
            core, z = i % 2, (i // 2) % self.nz
            x, y = (i // self.ctx) % self.nx, i // (self.ctx * self.nx)
            y, x, z, core = step(y, x, z, core)
            pairs.append((i, ((y * self.nx + x) * self.nz + z) * 2 + core))
        return lax.ppermute(value, AXES, pairs)

    def core(self, value):
        return self.move(value, lambda y, x, z, c: (y, x, z, 1 - c))

    def along_x(self, value):
        return self.move(value, lambda y, x, z, c: (y, 1 - x, z, c))

    def along_y(self, value):
        return self.move(value, lambda y, x, z, c: (1 - y, x, z, c))

    def along_xy(self, value):
        return self.move(value, lambda y, x, z, c: (1 - y, 1 - x, z, c))

    def along_z(self, value, hop):
        return self.move(value, lambda y, x, z, c: (y, x, (z + hop) % self.nz, c))


    def lines(self):
        return [[2 * z + core for z in range(self.nz)] for core in range(2)]


def from_z(z, hop):
    return lax.rem(z - hop + 4, 4)


def order_kernel(place, own, r1, r2, r3, out):
    z = place[2]
    out[z] = own[...]
    out[from_z(z, 1)] = r1[...]
    out[from_z(z, 2)] = r2[...]
    out[from_z(z, 3)] = r3[...]


def block_index(place):
    y, x = place[0], place[1]
    return (2 * y + x, 2 * y + 1 - x, 2 * (1 - y) + x, 2 * (1 - y) + 1 - x)


def fold(block):
    rows = block.shape[0] // 2
    return jnp.concatenate([block[:rows], block[rows:]], axis=1)


def deal(place, blocks, targets):
    for hop, target in enumerate(targets):
        target[...] = blocks[lax.rem(place[2] + hop, 4)]


def unfold(ref, lanes):
    return jnp.concatenate([ref[:, :lanes], ref[:, lanes:]], axis=0)


def seen(seg_col, seg_row, i, span):
    keys = span * (i + 1)
    same = seg_col[i * span : (i + 1) * span] == seg_row[:, :keys]
    place_q = i * span + lax.broadcasted_iota(jnp.int32, (span, keys), 0)
    place_k = lax.broadcasted_iota(jnp.int32, (span, keys), 1)
    return jnp.where(same & (place_q >= place_k), 0.0, BIG).astype(F32)


def attend_kernel(
    place,
    own,
    other,
    b0,
    bx,
    by,
    bxy,
    seg_row,
    seg_col,
    weight,
    vectors,
    normed,
    rows,
    exact,
    totals,
    out_own,
    out_1,
    out_2,
    out_3,
    lifted,
    spare,
    out,
):
    core, second = place[3], place[2] % 2 == 1
    lines, run_rows, width = own.shape
    group = width // 4
    span = 2 * run_rows
    part = b0.shape[0] * b0.shape[1]
    cut = weight.shape[1]
    for index, piece in zip(block_index(place), (b0, bx, by, bxy)):
        for k in range(piece.shape[0]):
            here = rows_at(index * part + k * piece.shape[1], piece.shape[1], 16)
            weight[here] = piece[k, :, :cut]
    vectors[...] = jnp.transpose(weight[:, 4 * LANES :].astype(F32))[64:80]
    gain, shift = vectors[0:1, :], vectors[1:2, :]
    mine = pl.ds(pl.multiple_of(core * 2 * group, LANES), 2 * group)
    bias_q, bias_v = vectors[2:3, mine], vectors[3:4, mine]
    bias_q = jnp.where(second, bias_q[:, group:], bias_q[:, :group])
    bias_v = jnp.where(second, bias_v[:, group:], bias_v[:, :group])
    for i in range(lines):
        spare[i, rows_at(core * run_rows, run_rows, 16)] = own[i]
        spare[i, rows_at((1 - core) * run_rows, run_rows, 16)] = other[i]
    for i in range(lines):
        here = slice(i * span, (i + 1) * span)
        value = (normalize(spare[i].astype(F32))[0] * gain + shift).astype(BF16)
        normed[here] = value
        projected = dot(value, weight[:, : 3 * group])
        rows[here, :group] = ((projected[:, :group] + bias_q) * SCALING).astype(BF16)
        rows[here, group : 2 * group] = projected[:, group : 2 * group].astype(BF16)
        rows[here, 2 * group :] = (projected[:, 2 * group :] + bias_v).astype(BF16)
    for i in range(lines):
        here = slice(i * span, (i + 1) * span)
        keys = span * (i + 1)
        bias = seen(seg_col, seg_row, i, span)
        heads = []
        for h in range(3):
            at = h * HEAD_DIM
            query = rows[here, at : at + HEAD_DIM]
            key = rows[:keys, group + at : group + at + HEAD_DIM]
            value = rows[:keys, 2 * group + at : 2 * group + at + HEAD_DIM]
            scores = dot(query, key, ((1,), (1,))) + bias
            peak = jnp.max(scores, axis=-1, keepdims=True)
            expanded = jnp.exp(scores - peak)
            total = jnp.sum(expanded, axis=-1, keepdims=True)
            mixed = dot(expanded.astype(BF16), value) / total
            heads.append(mixed.astype(BF16))
            exact[here, at : at + HEAD_DIM] = mixed
            totals[here, h : h + 1] = peak + jnp.log(total)
        out[i] = fold(jnp.concatenate(heads, axis=1))
    deal(place, out, (out_own, out_1, out_2, out_3))
    held = vectors[8:12, mine]
    few = 2 * group // 16
    for j in range(16):
        for k in range(4):
            at = (4 * j + k) * few
            lifted[:, at : at + few] = held[k : k + 1, j * few : (j + 1) * few]


def out_kernel(place, own, r1, r2, r3, weight, attended, *partial):
    z = place[2]
    span, group = attended.shape[1:]
    attended[z] = unfold(own, group)
    for hop, piece in ((1, r1), (2, r2), (3, r3)):
        attended[from_z(z, hop)] = unfold(piece, group)
    for s in range(2):
        partial[s][...] = (
            dot(attended[2 * s], weight[:group]) + dot(attended[2 * s + 1], weight[group:])
        ).astype(BF16)


def place_rows(core, target, own, other):
    run_rows = own.shape[0] // 2
    for s in range(2):
        for which, piece in ((core, own), (1 - core, other)):
            target[rows_at((2 * s + which) * run_rows, run_rows, 16)] = piece[
                s * run_rows : (s + 1) * run_rows
            ]


def hidden_kernel(
    place,
    tokens_own,
    tokens_other,
    part_first,
    part_second,
    other_first,
    other_second,
    cot_own,
    cot_other,
    up,
    vectors,
    bias_up,
    cot,
    residual,
    normed,
    active,
    slope,
    tokens,
):
    place_rows(place[3], cot, cot_own, cot_other)
    place_rows(place[3], tokens, tokens_own, tokens_other)
    gain, shift, bias_out = vectors[5:6, :], vectors[6:7, :], vectors[4:5, :]
    span = tokens.shape[0] // 2
    for s in range(2):
        here = slice(s * span, (s + 1) * span)
        one, two = ((part_first, other_first), (part_second, other_second))[s]
        wide = tokens[here].astype(F32) + (one[...].astype(F32) + two[...].astype(F32)) + bias_out
        residual[here] = wide
        low = (normalize(wide)[0] * gain + shift).astype(BF16)
        normed[here] = low
        hidden = dot(low, up[...]) + bias_up[...]
        square = hidden * hidden
        bent = jnp.tanh(ROOT * (hidden + CUBIC * (square * hidden)))
        active[here] = (0.5 * hidden * (1.0 + bent)).astype(BF16)
        slope[here] = 0.5 * (1.0 + bent) + 0.5 * hidden * (1.0 - bent * bent) * (
            ROOT * (1.0 + 3.0 * CUBIC * square)
        )


def down_weights_kernel(place, active, cot, down_own, *targets):
    *targets, spare = targets
    core = place[3]
    spare[...] = dot(active[...], cot[...], ((0,), (0,))).astype(BF16)
    width = cot.shape[1]
    for j in range(8):
        for k in range(2):
            lanes = slice(k * width, (k + 1) * width)
            here = 192 * j + 48 * k
            down_own[48 * j : 48 * j + 48, lanes] = spare[rows_at(here + 96 * core, 48, 16)]
            targets[j // 3][48 * (j % 3) : 48 * (j % 3) + 48, lanes] = spare[
                rows_at(here + 96 * (1 - core), 48, 16)
            ]


def feed_kernel(
    place,
    residual,
    active,
    slope,
    cot,
    up,
    down,
    grad_hidden,
    result,
    grad_normed,
    low_first,
    low_second,
    sums,
    lifted,
):
    span = cot.shape[0] // 2
    for s in range(2):
        here = slice(s * span, (s + 1) * span)
        upstream = cot[here]
        grad = (dot(upstream, down[...], ((1,), (1,))) * slope[here]).astype(BF16)
        grad_hidden[here] = grad
        back = dot(grad, up[...], ((1,), (1,)))
        grad_normed[here] = back
        (low_first, low_second)[s][...] = back.astype(BF16)
        result[here] = dot(active[here], down[...])
        rows = jnp.concatenate(
            [
                jnp.sum(back * normalize(residual[here])[0], axis=0, keepdims=True),
                jnp.sum(back, axis=0, keepdims=True),
                0.5 * jnp.sum(upstream.astype(F32), axis=0, keepdims=True),
            ],
            axis=0,
        )
        total = jnp.sum(grad.astype(F32), axis=0, keepdims=True)
        if s == 0:
            sums[...] = rows
        else:
            sums[...] = sums[...] + rows
            held = first + total
        first = total
    few = held.shape[1] // 64
    for j in range(16):
        for k in range(4):
            at = (4 * j + k) * few
            lifted[k : k + 1, j * few : (j + 1) * few] = held[:, at : at + few]


def up_weights_kernel(place, normed, grad_hidden, grad_up):
    grad_up[...] = dot(normed[...], grad_hidden[...], ((0,), (0,))).astype(BF16)


def attend_grad_kernel(
    place,
    back_own,
    other_first,
    other_second,
    residual,
    cot,
    vectors,
    weight,
    attended,
    grad_residual,
    deal_own,
    deal_1,
    deal_2,
    deal_3,
    out_own,
    out_other,
    sum_out,
    spare,
    blocks,
):
    core = place[3]
    gain = vectors[5:6, :]
    span = cot.shape[0] // 2
    group = attended.shape[2]
    half = 2 * group
    products = [None, None]
    for s in range(2):
        here = slice(s * span, (s + 1) * span)
        normal, factor = normalize(residual[here])
        wide = cot[here].astype(F32) + norm_back(
            (back_own[here] + (other_first, other_second)[s][...].astype(F32)) * gain,
            normal,
            factor,
        )
        grad_residual[here] = wide
        low = wide.astype(BF16)
        grad = dot(low, weight[...], ((1,), (1,))).astype(BF16)
        total = 0.5 * jnp.sum(wide, axis=0, keepdims=True)
        sum_out[...] = total if s == 0 else sum_out[...] + total
        for g in range(2):
            blocks[2 * s + g] = fold(grad[:, g * group : (g + 1) * group])
            product = dot(attended[2 * s + g], low, ((0,), (0,)))
            products[g] = product if s == 0 else products[g] + product
    deal(place, blocks, (deal_own, deal_1, deal_2, deal_3))
    for g in range(2):
        spare[g * group : (g + 1) * group] = products[g].astype(BF16)
    out_own[...] = spare[:, rows_at(core * half, half, LANES)]
    out_other[...] = spare[:, rows_at((1 - core) * half, half, LANES)]


def attend_back_kernel(
    place,
    rows,
    exact,
    totals,
    seg_row,
    seg_col,
    own,
    r1,
    r2,
    r3,
    joined,
    grad,
    keys_grad,
):
    z = place[2]
    span, group = rows.shape[0] // 4, grad.shape[1]
    grad[rows_at(z * span, span, span)] = unfold(own, group)
    for hop, piece in ((1, r1), (2, r2), (3, r3)):
        grad[rows_at(from_z(z, hop) * span, span, span)] = unfold(piece, group)
    for i in (3, 2, 1, 0):
        here = slice(i * span, (i + 1) * span)
        keys = span * (i + 1)
        bias = seen(seg_col, seg_row, i, span)
        for h in range(3):
            at = h * HEAD_DIM
            lanes = slice(at, at + HEAD_DIM)
            query = rows[here, lanes]
            key = rows[:keys, group + at : group + at + HEAD_DIM]
            value = rows[:keys, 2 * group + at : 2 * group + at + HEAD_DIM]
            upstream = grad[here, lanes]
            delta = jnp.sum(upstream.astype(F32) * exact[here, lanes], axis=-1, keepdims=True)
            probs = jnp.exp(dot(query, key, ((1,), (1,))) + bias - totals[here, h : h + 1])
            slopes = dot(upstream, value, ((1,), (1,)))
            grad_scores = (probs * (slopes - delta)).astype(BF16)
            grad_query = dot(grad_scores, key).astype(BF16)
            joined[here, lanes] = (grad_query.astype(F32) * SCALING).astype(BF16)
            grad_key = dot(grad_scores, query, ((0,), (0,)))
            grad_value = dot(probs.astype(BF16), upstream, ((0,), (0,)))
            if i == 3:
                keys_grad[2 * h] = grad_key
                keys_grad[2 * h + 1] = grad_value
            else:
                keys_grad[2 * h, :keys] = keys_grad[2 * h, :keys] + grad_key
                keys_grad[2 * h + 1, :keys] = keys_grad[2 * h + 1, :keys] + grad_value
    for h in range(3):
        for k in range(2):
            at = (k + 1) * group + h * HEAD_DIM
            joined[:, at : at + HEAD_DIM] = keys_grad[2 * h + k].astype(BF16)


def project_back_kernel(
    place,
    joined,
    weight,
    normed,
    tokens_own,
    tokens_other,
    sum_out,
    sums_two,
    lifted,
    o_own,
    o_x,
    o_y,
    o_xy,
    back_own,
    back_first,
    back_second,
    back_third,
    product,
    small,
):
    core = place[3]
    second = place[2] % 2 == 1
    lines, run_rows, width = tokens_own.shape
    span, group = 2 * run_rows, width // 4
    small[...] = jnp.zeros_like(small)
    small[4:5] = sum_out[...]
    small[5:8] = sums_two[...]
    small[8:12, pl.ds(pl.multiple_of(core * 2 * group, LANES), 2 * group)] = lifted[...]
    mine = pl.ds(pl.multiple_of(core * 2 * group, LANES), 2 * group)
    empty = jnp.zeros((1, group), F32)
    for row, at in ((2, 0), (3, 2 * group)):
        total = jnp.sum(joined[:, at : at + group].astype(F32), axis=0, keepdims=True)
        small[row : row + 1, mine] = jnp.where(
            second,
            jnp.concatenate([empty, total], axis=1),
            jnp.concatenate([total, empty], axis=1),
        )
    for i in range(lines):
        for which, tokens in ((core, tokens_own), (1 - core, tokens_other)):
            here = rows_at(i * span + which * run_rows, run_rows, 16)
            step = dot(joined[here], weight[:, : 3 * group], ((1,), (1,)))
            if tokens is tokens_own:
                back_own[i] = step
            else:
                low = step.astype(BF16)
                for target, start in ((back_first, 0), (back_second, 192), (back_third, 384)):
                    first = max(start, i * run_rows)
                    last = min(start + target.shape[0], (i + 1) * run_rows)
                    if first < last:
                        target[first - start : last - start] = low[
                            first - i * run_rows : last - i * run_rows
                        ]
            normal = normalize(tokens[i].astype(F32))[0]
            small[0:1] = small[0:1] + jnp.sum(step * normal, axis=0, keepdims=True)
            small[1:2] = small[1:2] + jnp.sum(step, axis=0, keepdims=True)
    product[:, : 3 * group] = dot(normed[...], joined[...], ((0,), (0,))).astype(BF16)
    product[:, 3 * group :] = jnp.transpose(small[...])[:, :64].astype(BF16)
    size = o_own.shape[0]
    for index, target in zip(block_index(place), (o_own, o_x, o_y, o_xy)):
        target[...] = product[rows_at(index * size, size, 16)]


def split_kernel(targets, size, block, place):
    y, x = place[0], place[1]
    own, over_x, over_y, low, high = targets
    block(y, x, slice(0, size), own)
    block(y, 1 - x, slice(0, size), over_x)
    block(1 - y, x, slice(0, size), over_y)
    block(1 - y, 1 - x, slice(0, size // 2), low)
    block(1 - y, 1 - x, slice(size // 2, size), high)


def split_down_kernel(place, own, first, second, third, *targets):
    *targets, other = targets
    core, size = place[3], targets[0].shape[0]
    other[:144] = first[...]
    other[144:288] = second[...]
    other[288:] = third[...]

    def block(y, x, rows, target):
        here = rows_at(x * size + rows.start, rows.stop - rows.start, 16)
        target[...] = jnp.where(y == core, own[here], other[here])

    split_kernel(targets, size, block, place)


def split_up_kernel(place, up, out_own, out_other, *targets):
    core, size = place[3], targets[0].shape[0]
    cut = up.shape[1]

    def block(y, x, rows, target):
        count = rows.stop - rows.start
        target[:, :cut] = up[rows_at((2 * y + x) * size + rows.start, count, 16)]
        here = rows_at(x * size + rows.start, count, 16)
        target[:, cut:] = jnp.where(y == core, out_own[here], out_other[here])

    split_kernel(targets, size, block, place)


def collect_kernel(place, over_x, over_y, low, high, sum_x, sum_y):
    half = low.shape[0]
    sum_x[:half] = over_x[:half]
    sum_x[half:] = (over_x[half:].astype(F32) + high[...].astype(F32)).astype(BF16)
    sum_y[:half] = (over_y[:half].astype(F32) + low[...].astype(F32)).astype(BF16)
    sum_y[half:] = over_y[half:]


def spread_kernel(place, own, from_x, from_y, low, high, up, down):
    half = low.shape[0]
    cut = up.shape[2]
    blocks = block_index(place)
    for index, piece in zip(blocks, (own, from_x, from_y)):
        up[index] = piece[:, :cut]
        down[index] = piece[:, cut:]
    up[blocks[3], :half] = low[:, :cut]
    up[blocks[3], half:] = high[:, :cut]
    down[blocks[3], :half] = low[:, cut:]
    down[blocks[3], half:] = high[:, cut:]


def line_down_kernel(place, a, b, c, d, down):
    rows, width = down.shape[0] // 2, down.shape[1]
    for k in range(2):
        here = (slice(0, rows), slice(k * width, (k + 1) * width))
        down[k * rows : (k + 1) * rows] = (a[here].astype(F32) + b[here].astype(F32)) + (
            c[here].astype(F32) + d[here].astype(F32)
        )


def deal_all_kernel(place, up, up_x, up_y, qkv, qkv_x, qkv_y, qkv_xy, *targets):
    *targets, spare = targets
    cut = up.shape[1]
    spare[:, :cut] = (
        up[...].astype(F32) + (up_x[...].astype(F32) + up_y[...].astype(F32))
    ).astype(BF16)
    spare[:, cut:] = (
        (qkv[...].astype(F32) + qkv_x[...].astype(F32))
        + (qkv_y[...].astype(F32) + qkv_xy[...].astype(F32))
    ).astype(BF16)
    size = targets[0].shape[0]
    for hop, target in enumerate(targets):
        target[...] = spare[rows_at(lax.rem(place[2] + hop, 4) * size, size, 16)]


def line_all_kernel(place, own, r1, r2, r3, mine, theirs, spare, *, cut):
    second = place[2] % 2 == 1
    third = (own.shape[1] - cut - 64) // 3
    same = own[...].astype(F32) + r2[...].astype(F32)
    cross = r1[...].astype(F32) + r3[...].astype(F32)
    spare[:, :cut] = (same + cross)[:, :cut]
    first, last = jnp.where(second, cross, same), jnp.where(second, same, cross)
    for k in range(3):
        here = slice(cut + k * third, cut + (k + 1) * third)
        at = cut + 2 * k * third
        spare[:, at : at + third] = first[:, here]
        spare[:, at + third : at + 2 * third] = last[:, here]
    at = cut + 6 * third
    spare[:, at : at + 64] = (same + cross)[:, cut + 3 * third :]
    spare[:, at + 64 :] = jnp.zeros((spare.shape[0], 64), F32)
    rows = mine.shape[0]
    mine[...] = spare[rows_at(place[3] * rows, rows, 8)]
    theirs[...] = spare[rows_at((1 - place[3]) * rows, rows, 8)]


def out_split_kernel(place, b0, bx, by, bxy, own, other, spare):
    core = place[3]
    first = b0.shape[2] - own.shape[1]
    size = b0.shape[0] * b0.shape[1]
    for index, piece in zip(block_index(place), (b0, bx, by, bxy)):
        for k in range(piece.shape[0]):
            here = rows_at(index * size + k * piece.shape[1], piece.shape[1], 16)
            spare[here] = piece[k, :, first:]
    half = own.shape[0]
    own[...] = spare[rows_at(core * half, half, 16)]
    other[...] = spare[rows_at((1 - core) * half, half, 16)]


def out_halves_kernel(place, own, other, out):
    core = place[3]
    half = out.shape[0]
    for which, piece in ((core, own), (1 - core, other)):
        out[:, rows_at(which * half, half, LANES)] = piece[...]


def down_halves_kernel(place, own, other, down):
    core = place[3]
    width = down.shape[1]
    for which, piece in ((core, own), (1 - core, other)):
        for j in range(8):
            for k in range(2):
                down[rows_at(192 * j + 96 * which + 48 * k, 48, 16)] = piece[
                    48 * j : 48 * j + 48, k * width : (k + 1) * width
                ]


def deal_back_kernel(place, own, first, second, third, down, down_x, down_y, *targets):
    *targets, spare, total = targets
    lines, rows, width = own.shape
    spare[0:192] = first[...].astype(F32)
    spare[192:384] = second[...].astype(F32)
    spare[384:] = third[...].astype(F32)
    total[...] = (
        down[...].astype(F32) + (down_x[...].astype(F32) + down_y[...].astype(F32))
    ).astype(BF16)
    size = total.shape[0] // 4
    for hop, target in enumerate(targets):
        k = lax.rem(place[2] + hop, 4)
        target[:size] = total[rows_at(k * size, size, 16)]
        block = (own[k] + spare[rows_at(k * rows, rows, rows)]).astype(BF16)
        target[size:] = fold(block)


def final_kernel(place, own, r1, r2, r3, grad_residual, tokens, vectors, out, held):
    z, core = place[2], place[3]
    rows, width = held.shape[1:]
    start = own.shape[0] - rows // 2
    for hop, piece in enumerate((own, r1, r2, r3)):
        held[from_z(z, hop)] = unfold(piece.at[start:], width)
    gain = vectors[0:1, :]
    for s in range(2):
        here = slice(s * rows, (s + 1) * rows)
        there = rows_at((2 * s + core) * rows, rows, 16)
        normal, factor = normalize(tokens[here].astype(F32))
        grad = (held[2 * s].astype(F32) + held[2 * s + 1].astype(F32)) * gain
        out[here] = (grad_residual[there] + norm_back(grad, normal, factor)).astype(BF16)


def split_local(
    grid,
    tokens,
    segments,
    cotangent,
    ln1_gain,
    ln1_bias,
    w_qkv,
    bias_query,
    bias_value,
    w_out,
    bias_out,
    ln2_gain,
    ln2_bias,
    w_up,
    bias_up,
    w_down,
    bias_down,
):
    count, run_rows, width = tokens.shape
    own_rows = count * run_rows
    all_rows = 2 * own_rows
    span = 2 * run_rows
    half = width // 2
    group = half // 2
    hidden_half = w_up.shape[1] // 2
    shard = w_qkv.shape[0]
    dp, ctx = lax.axis_index("dp"), lax.axis_index("ctx")
    y, x, z, core = dp // grid.nx, dp % grid.nx, ctx // 2, ctx % 2
    place = jnp.stack([y, x, z, core]).astype(jnp.int32)
    first_core = core == 0

    def pick(array, index, axis):
        return lax.dynamic_index_in_dim(array, index, axis, keepdims=False)

    def both(own, other, axis):
        return jnp.where(
            first_core,
            jnp.concatenate([own, other], axis),
            jnp.concatenate([other, own], axis),
        )

    def z_all(value):
        return [value] + [grid.along_z(value, hop) for hop in (1, 2, 3)]

    def after(values, *waited):
        return lax.optimization_barrier((values, waited))[0]

    def z_send(blocks):
        return [grid.along_z(blocks[hop], hop) for hop in (1, 2, 3)]

    flat = tokens.reshape(own_rows, width)
    small = jnp.stack(
        [ln1_gain, ln1_bias, bias_query, bias_value, bias_out, ln2_gain, ln2_bias, bias_down], axis=1
    )
    lifted = bias_up.reshape(4, shard).T
    seg_lanes = jnp.pad(segments.astype(BF16).reshape(8, 32), ((0, shard - 8), (0, 0)))
    vector_lanes = jnp.concatenate(
        [small, lifted, jnp.zeros((shard, 4), BF16), seg_lanes, jnp.zeros((shard, 16), BF16)],
        axis=1,
    )
    split_qkv = w_qkv.reshape(shard, 3, 2, half)
    split_up = w_up.reshape(shard, 2, hidden_half)
    split_out = w_out.reshape(shard, 2, half)
    cut = 3 * group + 64
    size = 8 * shard

    def columns(which):
        chosen = pick(split_qkv, which, 2)
        return jnp.concatenate(
            [
                chosen[:, :, :group].reshape(shard, 3 * group),
                vector_lanes,
                chosen[:, :, group:].reshape(shard, 3 * group),
                vector_lanes,
                pick(split_out, which, 1),
                pick(split_up, which, 1),
            ],
            axis=1,
        )

    flat_other = grid.core(flat)
    cot_own = cotangent.reshape(own_rows, width)
    cot_other = grid.core(cot_own)
    piece = both(columns(core), after(grid.core(columns(1 - core)), flat_other, cot_other), 0)
    second_group = lax.rem(z, 2) == 1
    lanes_out = piece[:, 2 * cut : 2 * cut + half]
    first, last = piece[:, :cut], piece[:, cut : 2 * cut]
    piece_same = jnp.concatenate([jnp.where(second_group, last, first), lanes_out], axis=1)
    piece_cross = jnp.concatenate([jnp.where(second_group, first, last), lanes_out], axis=1)
    line_one = [
        piece_same,
        grid.along_z(piece_cross, 1),
        grid.along_z(piece_same, 2),
        grid.along_z(piece_cross, 3),
    ]
    def order(name, pieces):
        return run(name, order_kernel, place, pieces, [((4,) + pieces[0].shape, BF16)])[0]

    def kernel(name, body, args, outs, scratch=(), far=(), extra=6 << 20):
        return run(name, body, place, args, outs, scratch, far, extra)

    def order_rows(name, pieces):
        lanes = pieces[0].shape[1]
        return kernel(
            name, order_kernel, pieces, [((4, 2 * shard, lanes), BF16)], far=(1, 2, 3)
        )[0].reshape(size, lanes)

    plane_one = order("order_qkv", line_one)
    from_x, from_y, from_xy = (
        grid.along_x(plane_one),
        grid.along_y(plane_one),
        grid.along_xy(plane_one),
    )
    piece_b = jnp.concatenate([w_down[: 2 * shard], w_down[2 * shard :]], axis=1)

    rest_piece = jnp.concatenate([piece[:, 2 * cut + half :], piece_b], axis=1)
    rest_line = z_all(after(rest_piece, line_one))
    waiting = after(tokens, line_one)
    token_pieces = [
        grid.along_z(pick(waiting, lax.rem(z + hop, 4) // 2, 0), hop) for hop in (1, 2, 3)
    ]
    token_pieces = after(token_pieces, plane_one)
    gathered = order("order_tokens", [pick(tokens, z // 2, 0)] + token_pieces)
    gathered_rows = gathered.reshape(4 * run_rows, width)
    gathered_other = jnp.concatenate(
        [grid.core(gathered_rows[:192]), grid.core(gathered_rows[192:384]), grid.core(gathered_rows[384:])]
    ).reshape(gathered.shape)
    out_parts = run(
        "out_split",
        out_split_kernel,
        place,
        [plane_one, from_x, from_y, from_xy],
        [((half, half), BF16)] * 2,
        [((width, half), BF16)],
    )
    segs = plane_one.reshape(4, 2, shard, cut + half)[:, :, :8, 3 * group + 16 : 3 * group + 48]
    segs = segs.reshape(4, 2, 2, 4 * 32).transpose(2, 0, 1, 3).reshape(2, 8 * run_rows)
    segs = pick(segs, z // 2, 0).astype(F32)

    weight_qkv, vectors, normed, packed, exact, totals, *out_deal, bias_up_half = kernel(
        "attend",
        attend_kernel,
        [
            gathered,
            gathered_other,
            after(plane_one, out_parts),
            from_x,
            from_y,
            from_xy,
            segs.reshape(1, -1),
            segs.reshape(-1, 1),
        ],
        [
            ((width, cut), BF16),
            ((16, width), F32),
            ((4 * span, width), BF16),
            ((4 * span, 3 * group), BF16),
            ((4 * span, group), F32),
            ((4 * span, LANES), F32),
        ]
        + [((run_rows, 2 * group), BF16)] * 4
        + [((1, hidden_half), F32)],
        [((4, span, width), BF16), ((4, run_rows, 2 * group), BF16)],
        far=(3, 4, 5),
        extra=14 << 20,
    )
    out_blocks = out_deal[0]
    out_pieces = z_send(out_deal)

    weight_out = kernel(
        "out_halves",
        out_halves_kernel,
        [out_parts[0], grid.core(out_parts[1])],
        [((half, width), BF16)],
    )[0]

    plane_rest = order_rows("order_rest", [rest_line[0]] + after(rest_line[1:], out_blocks))
    attended, *partial = kernel(
        "project_out",
        out_kernel,
        [out_blocks] + out_pieces + [weight_out],
        [((4, span, group), BF16)] + [((own_rows, width), BF16)] * 2,
        far=(1, 2, 3),
    )
    part_other = [grid.core(member) for member in partial]
    over = after((grid.along_x(plane_rest), grid.along_y(plane_rest)), part_other)
    low, high = grid.along_x(over[1][: 4 * shard]), grid.along_y(over[0][4 * shard :])
    weight_up, mixed_down = kernel(
        "spread",
        spread_kernel,
        [plane_rest, *over, low, high],
        [((4, size, hidden_half), BF16), ((4, size, 2 * width), BF16)],
        far=(1, 2, 3, 4),
    )
    weight_up = weight_up.reshape(width, hidden_half)
    mixed_down = mixed_down.reshape(2, half, 2 * width)
    cot, residual, normed_two, active, slope = kernel(
        "hidden",
        hidden_kernel,
        [
            flat,
            flat_other,
            *partial,
            *part_other,
            cot_own,
            cot_other,
            weight_up,
            vectors,
            bias_up_half,
        ],
        [
            ((all_rows, width), BF16),
            ((all_rows, width), F32),
            ((all_rows, width), BF16),
            ((all_rows, hidden_half), BF16),
            ((all_rows, hidden_half), F32),
        ],
        [((all_rows, width), BF16)],
        far=(0, 1, 6, 7),
        extra=14 << 20,
    )
    weight_down = kernel(
        "down_halves",
        down_halves_kernel,
        [pick(mixed_down, core, 0), grid.core(pick(mixed_down, 1 - core, 0))],
        [((hidden_half, width), BF16)],
    )[0]

    def halve(array, which):
        return pick(array.reshape(2, 2, run_rows, width), which, 1).reshape(own_rows, width)

    def split(name, body, parts, lanes, scratch=()):
        results = [((size, lanes), BF16)] * 3 + [((size // 2, lanes), BF16)] * 2
        return kernel(name, body, parts, results, scratch)

    def diagonal(parts):
        return grid.along_x(parts[3]), grid.along_y(parts[4])

    def collect(name, parts, low, high):
        sum_x, sum_y = kernel(
            name, collect_kernel, [parts[1], parts[2], low, high], [(parts[1].shape, BF16)] * 2, far=(2, 3)
        )
        return parts[0], grid.along_x(sum_x), grid.along_y(sum_y), sum_x

    grad_hidden, result, back_two, *back_low, sums_two, lifted = kernel(
        "feed",
        feed_kernel,
        [residual, active, slope, cot, weight_up, weight_down],
        [
            ((all_rows, hidden_half), BF16),
            ((all_rows, width), F32),
            ((all_rows, width), F32),
            ((own_rows, width), BF16),
            ((own_rows, width), BF16),
            ((3, width), F32),
            ((4, half), F32),
        ],
        extra=14 << 20,
    )
    back_other = [grid.core(member) for member in back_low]
    grad_up = kernel(
        "up_weights",
        up_weights_kernel,
        [normed_two, grad_hidden],
        [((width, hidden_half), BF16)],
        extra=10 << 20,
    )[0]


    down_own, *down_other = kernel(
        "down_weights",
        down_weights_kernel,
        after([active, cot], grad_up),
        [((rows, 2 * width), BF16) for rows in (half, 144, 144, 96)],
        [((hidden_half, width), BF16)],
        extra=10 << 20,
    )
    down_recv = [grid.core(member) for member in down_other]
    grad_residual, *grad_deal, out_own, out_other, sum_out = kernel(
        "attend_grad",
        attend_grad_kernel,
        after(
            [back_two, *back_other, residual, cot, vectors, weight_out, attended],
            down_own,
        ),
        [
            ((all_rows, width), F32),
            *[((run_rows, 2 * group), BF16)] * 4,
            ((half, half), BF16),
            ((half, half), BF16),
            ((1, width), F32),
        ],
        [((half, width), BF16), ((4, run_rows, 2 * group), BF16)],
    )
    grad_blocks = grad_deal[0]
    grad_pieces = z_send(grad_deal)
    out_recv = grid.core(out_other)
    def split(name, body, parts, lanes, scratch=()):
        results = [((size, lanes), BF16)] * 3 + [((size // 2, lanes), BF16)] * 2
        return kernel(name, body, parts, results, scratch)

    down_parts = split(
        "split_down",
        split_down_kernel,
        [down_own] + down_recv,
        2 * width,
        [((half, 2 * width), BF16)],
    )
    down_low, down_high = diagonal(down_parts)
    up_parts = split(
        "split_up",
        split_up_kernel,
        after([grad_up, out_own, out_recv], down_parts),
        hidden_half + half,
    )
    up_low, up_high = diagonal(up_parts)
    down_low, down_high = after((down_low, down_high), grad_pieces)
    down_parts = collect("collect_down", down_parts, down_low, down_high)

    result, residual = after((result, residual), up_parts)
    result_other = grid.core(halve(result, 1 - core))
    output = (
        halve(residual, core)
        + (halve(result, core) + result_other)
        + vectors[7:8]
    ).astype(BF16)

    grad_pieces = after(grad_pieces, up_parts, down_parts[3], output)
    grad_joined = kernel(
        "attend_back",
        attend_back_kernel,
        [packed, exact, totals, segs.reshape(1, -1), segs.reshape(-1, 1), grad_blocks]
        + grad_pieces,
        [((4 * span, 3 * group), BF16)],
        [((4 * span, group), BF16), ((6, 4 * span, HEAD_DIM), F32)],
        far=(0, 1, 2, 6, 7, 8),
        extra=14 << 20,
    )[0]
    back_results = kernel(
        "project_back",
        project_back_kernel,
        [grad_joined, weight_qkv, normed, gathered, gathered_other]
        + [sum_out, sums_two, lifted],
        [((size, cut), BF16)] * 4
        + [((4, run_rows, width), F32)]
        + [((192, width), BF16), ((192, width), BF16), ((128, width), BF16)],
        [((width, cut), BF16), ((LANES, width), F32)],
        far=(1, 2, 3, 4),
        extra=10 << 20,
    )
    qkv_parts, back_own, back_low = back_results[:4], back_results[4], back_results[5:]
    up_low, up_high = after((up_low, up_high), back_own)
    up_parts = collect("collect_up", up_parts, up_low, up_high)
    mixed = kernel(
        "deal_back",
        deal_back_kernel,
        [back_own]
        + [grid.core(member) for member in back_low]
        + after(list(down_parts[:3]), up_parts[3]),
        [((2 * shard + run_rows // 2, 2 * width), BF16)] * 4,
        [((4 * run_rows, width), F32), ((size, 2 * width), BF16)],
        far=(5, 6),
    )
    mixed_line = [mixed[0]] + z_send(mixed)
    up_ready = after(list(up_parts[:3]), mixed)
    qkv_parts = [qkv_parts[0]] + after(list(qkv_parts[1:]), up_ready)
    qkv_recv = [grid.along_x(qkv_parts[1]), grid.along_y(qkv_parts[2]), grid.along_xy(qkv_parts[3])]
    up_cut = hidden_half + half
    all_dealt = kernel(
        "deal_all",
        deal_all_kernel,
        after(up_ready, mixed_line) + [qkv_parts[0]] + qkv_recv,
        [((2 * shard, up_cut + cut), BF16)] * 4,
        [((size, up_cut + cut), BF16)],
        far=(1, 2, 4, 5, 6),
    )
    all_line = [all_dealt[0]] + z_send(all_dealt)
    grad_tokens = kernel(
        "final",
        final_kernel,
        mixed_line + [grad_residual, flat, vectors],
        [((own_rows, width), BF16)],
        [((4, run_rows, width), BF16)],
        far=(1, 2, 3, 5),
    )[0]
    grad_down = kernel(
        "line_down", line_down_kernel, mixed_line, [((4 * shard, width), F32)], far=(1, 2, 3)
    )[0]
    all_line = [all_line[0]] + after(all_line[1:], grad_tokens, grad_down)
    mine, theirs = kernel(
        "line_all",
        functools.partial(line_all_kernel, cut=up_cut),
        all_line,
        [((shard, up_cut + 6 * group + LANES), F32)] * 2,
        [((2 * shard, up_cut + 6 * group + LANES), F32)],
        far=(1, 2, 3),
    )
    theirs = grid.core(theirs)
    grad_up_own = both(mine[:, :hidden_half], theirs[:, :hidden_half], 1)
    grad_out_own = both(mine[:, hidden_half:up_cut], theirs[:, hidden_half:up_cut], 1)
    qkv_mine, qkv_theirs = mine[:, up_cut:], theirs[:, up_cut:]
    grad_qkv_own = both(
        qkv_mine[:, : 6 * group].reshape(shard, 3, 1, half),
        qkv_theirs[:, : 6 * group].reshape(shard, 3, 1, half),
        2,
    ).reshape(shard, 6 * half)
    small_sum = (qkv_mine[:, 6 * group : 6 * group + 16] + qkv_theirs[:, 6 * group : 6 * group + 16]).T
    return (
        output.reshape(tokens.shape),
        grad_tokens.reshape(tokens.shape),
        small_sum[0],
        small_sum[1],
        grad_qkv_own,
        small_sum[2],
        small_sum[3],
        grad_out_own,
        small_sum[4],
        small_sum[5],
        small_sum[6],
        grad_up_own,
        small_sum[8:12].reshape(4 * shard),
        grad_down,
        small_sum[7],
    )


def build_local(mesh):
    dp, ctx = mesh.shape["dp"], mesh.shape["ctx"]
    if (dp, ctx) != (4, 8):
        return local_general
    grid = Grid(dp, ctx)
    return lambda *args: split_local(grid, *args)


def solution(mesh):
    return jax.shard_map(
        build_local(mesh),
        mesh=mesh,
        in_specs=(
            P("dp", "ctx", None),
            P("dp", "ctx"),
            P("dp", "ctx", None),
            P(("dp", "ctx")),
            P(("dp", "ctx")),
            P(("dp", "ctx"), None),
            P(("dp", "ctx")),
            P(("dp", "ctx")),
            P(("dp", "ctx"), None),
            P(("dp", "ctx")),
            P(("dp", "ctx")),
            P(("dp", "ctx")),
            P(("dp", "ctx"), None),
            P(("dp", "ctx")),
            P(("dp", "ctx"), None),
            P(("dp", "ctx")),
        ),
        out_specs=(
            P("dp", "ctx", None),
            P("dp", "ctx", None),
            P(("dp", "ctx")),
            P(("dp", "ctx")),
            P(("dp", "ctx"), None),
            P(("dp", "ctx")),
            P(("dp", "ctx")),
            P(("dp", "ctx"), None),
            P(("dp", "ctx")),
            P(("dp", "ctx")),
            P(("dp", "ctx")),
            P(("dp", "ctx"), None),
            P(("dp", "ctx")),
            P(("dp", "ctx"), None),
            P(("dp", "ctx")),
        ),
        check_vma=False,
    )
```

```python
import functools
import math

import jax
import jax.numpy as jnp
from jax import lax
from jax.experimental import pallas as pl
from jax.experimental.pallas import tpu as pltpu
from jax.sharding import PartitionSpec as P

HEADS = 12
HEAD_DIM = 64


EPSILON = 1e-05
NEGATIVE = -1e30
SCALING = 0.125


def layer_norm(values, gain_vec, shift_vec):
    center = values - jnp.mean(values, axis=-1, keepdims=True)
    spread = jnp.mean(center * center, axis=-1, keepdims=True)
    return center * lax.rsqrt(spread + EPSILON) * gain_vec + shift_vec


def split_heads(tensor):
    return tensor.reshape(tensor.shape[0], tensor.shape[1], HEADS, HEAD_DIM)


def visible(seg_query, seg_key, place_query, place_key):
    same_doc = seg_query[:, :, None] == seg_key[:, None, :]
    causal = place_query[None, :, None] >= place_key[None, None, :]
    return (same_doc & causal)[:, None]


def forward_block(
    carry, query_heads, key_rows, value_rows, seg_query, seg_key, place_query, place_key
):
    row_max, row_sum, acc_out = carry
    scores = jnp.einsum(
        "sqhd,skhd->shqk", query_heads, split_heads(key_rows), preferred_element_type=jnp.float32
    )
    allowed = visible(seg_query, seg_key, place_query, place_key)
    scores = jnp.where(allowed, scores, NEGATIVE)
    new_max = jnp.maximum(row_max, jnp.max(scores, axis=-1))
    expanded = jnp.where(allowed, jnp.exp(scores - new_max[..., None]), 0.0)
    factor = jnp.exp(row_max - new_max)
    row_sum = jnp.sum(expanded, axis=-1)
    added = jnp.einsum(
        "shqk,skhd->sqhd",
        expanded.astype(jnp.bfloat16),
        split_heads(value_rows),
        preferred_element_type=jnp.float32,
    )
    acc_out = acc_out * jnp.swapaxes(factor, 1, 2)[..., None] + added
    return (new_max, row_sum, acc_out)


def grad_block(
    query_heads,
    key_heads,
    value_heads,
    grad_heads,
    log_total,
    delta_sum,
    seg_query,
    seg_key,
    place_query,
    place_key,
):
    scores = jnp.einsum(
        "sqhd,skhd->shqk", query_heads, key_heads, preferred_element_type=jnp.float32
    )
    allowed = visible(seg_query, seg_key, place_query, place_key)
    shift_total = jnp.swapaxes(log_total, 1, 2)[..., None]
    probs = jnp.where(allowed, jnp.exp(scores - shift_total), 0.0)
    grad_probs = jnp.einsum(
        "sqhd,skhd->shqk", grad_heads, value_heads, preferred_element_type=jnp.float32
    )
    grad_scores = (probs * (grad_probs - jnp.swapaxes(delta_sum, 1, 2)[..., None])).astype(
        jnp.bfloat16
    )
    return (grad_scores, probs.astype(jnp.bfloat16))


def query_side(mine, theirs):
    query_heads, grad_heads, log_total, delta_sum, seg_mine, place_mine = mine
    key_rows, value_rows, seg_theirs = theirs
    place_theirs = jnp.arange(key_rows.shape[1], dtype=jnp.int32)
    key_heads = split_heads(key_rows)
    outcome = grad_block(
        query_heads,
        key_heads,
        split_heads(value_rows),
        grad_heads,
        log_total,
        delta_sum,
        seg_mine,
        seg_theirs,
        place_mine,
        place_theirs,
    )
    return jnp.einsum("shqk,skhd->sqhd", outcome[0], key_heads, preferred_element_type=jnp.float32)


def key_side(mine, theirs):
    key_heads, value_heads, seg_mine, place_mine = mine
    query_rows, grad_rows, total_high, total_low, delta_high, delta_low, seg_theirs = theirs
    place_theirs = jnp.arange(query_rows.shape[1], dtype=jnp.int32)
    query_heads = split_heads(query_rows)
    grad_heads = split_heads(grad_rows)
    log_total = total_high.astype(jnp.float32) + total_low.astype(jnp.float32)
    delta_sum = delta_high.astype(jnp.float32) + delta_low.astype(jnp.float32)
    grad_scores, probs = grad_block(
        query_heads,
        key_heads,
        value_heads,
        grad_heads,
        log_total,
        delta_sum,
        seg_theirs,
        seg_mine,
        place_theirs,
        place_mine,
    )
    grad_key = jnp.einsum(
        "shqk,sqhd->skhd", grad_scores, query_heads, preferred_element_type=jnp.float32
    )
    grad_value = jnp.einsum(
        "shqk,sqhd->skhd", probs, grad_heads, preferred_element_type=jnp.float32
    )
    return (grad_key, grad_value)


def contract_rows(left, right):
    return lax.dot_general(
        left, right, (((0,), (0,)), ((), ())), preferred_element_type=jnp.float32
    )


def contract_cols(left, right):
    return lax.dot_general(
        left, right, (((1,), (1,)), ((), ())), preferred_element_type=jnp.float32
    )


def local_general(
    tokens,
    segments,
    cotangent,
    ln1_gain,
    ln1_bias,
    w_qkv,
    bias_query,
    bias_value,
    w_out,
    bias_out,
    ln2_gain,
    ln2_bias,
    w_up,
    bias_up,
    w_down,
    bias_down,
):
    count, span_rows, model_width = tokens.shape
    total_rows = count * span_rows
    places = lax.axis_index("ctx") * span_rows + jnp.arange(span_rows, dtype=jnp.int32)
    gathered = (
        lax.all_gather(ln1_gain, ("dp", "ctx"), axis=0, tiled=True),
        lax.all_gather(ln1_bias, ("dp", "ctx"), axis=0, tiled=True),
        lax.all_gather(w_qkv, ("dp", "ctx"), axis=0, tiled=True),
        lax.all_gather(bias_query, ("dp", "ctx"), axis=0, tiled=True),
        lax.all_gather(bias_value, ("dp", "ctx"), axis=0, tiled=True),
        lax.all_gather(w_out, ("dp", "ctx"), axis=0, tiled=True),
        lax.all_gather(bias_out, ("dp", "ctx"), axis=0, tiled=True),
        lax.all_gather(ln2_gain, ("dp", "ctx"), axis=0, tiled=True),
        lax.all_gather(ln2_bias, ("dp", "ctx"), axis=0, tiled=True),
        lax.all_gather(w_up, ("dp", "ctx"), axis=0, tiled=True),
        lax.all_gather(bias_up, ("dp", "ctx"), axis=0, tiled=True),
        lax.all_gather(w_down, ("dp", "ctx"), axis=0, tiled=True),
        lax.all_gather(bias_down, ("dp", "ctx"), axis=0, tiled=True),
    )
    (
        gain_one,
        shift_one,
        qkv_full,
        query_shift,
        value_shift,
        out_full,
        out_shift,
        gain_two,
        shift_two,
        up_full,
        up_shift,
        down_full,
        down_shift,
    ) = gathered
    flat = tokens.reshape(total_rows, model_width).astype(jnp.float32)
    normed = layer_norm(flat, gain_one.astype(jnp.float32), shift_one.astype(jnp.float32)).astype(
        jnp.bfloat16
    )
    projected = jnp.dot(normed, qkv_full, preferred_element_type=jnp.float32)
    row_shape = (count, span_rows, model_width)
    query_rows = (
        ((projected[:, :model_width] + query_shift.astype(jnp.float32)) * SCALING)
        .astype(jnp.bfloat16)
        .reshape(row_shape)
    )
    key_rows = projected[:, model_width : 2 * model_width].astype(jnp.bfloat16).reshape(row_shape)
    value_rows = (
        (projected[:, 2 * model_width :] + value_shift.astype(jnp.float32))
        .astype(jnp.bfloat16)
        .reshape(row_shape)
    )
    query_heads = split_heads(query_rows)
    start_state = (
        jnp.full((count, HEADS, span_rows), NEGATIVE, jnp.float32),
        jnp.zeros((count, HEADS, span_rows), jnp.float32),
        jnp.zeros((count, span_rows, HEADS, HEAD_DIM), jnp.float32),
    )
    piece_keys = lax.all_gather(key_rows, "ctx", axis=1, tiled=True)
    piece_values = lax.all_gather(value_rows, "ctx", axis=1, tiled=True)
    piece_segs = lax.all_gather(segments, "ctx", axis=1, tiled=True)
    piece_places = jnp.arange(piece_keys.shape[1], dtype=jnp.int32)
    row_max, row_sum, acc_out = forward_block(
        start_state,
        query_heads,
        piece_keys,
        piece_values,
        segments,
        piece_segs,
        places,
        piece_places,
    )
    attended_exact = acc_out / jnp.swapaxes(row_sum, 1, 2)[..., None]
    log_total = jnp.swapaxes(row_max + jnp.log(row_sum), 1, 2)
    attended = attended_exact.reshape(total_rows, model_width).astype(jnp.bfloat16)
    residual = (
        flat
        + jnp.dot(attended, out_full, preferred_element_type=jnp.float32)
        + out_shift.astype(jnp.float32)
    )
    normed_two = layer_norm(
        residual, gain_two.astype(jnp.float32), shift_two.astype(jnp.float32)
    ).astype(jnp.bfloat16)
    hidden = jnp.dot(normed_two, up_full, preferred_element_type=jnp.float32) + up_shift.astype(
        jnp.float32
    )
    active = jax.nn.gelu(hidden).astype(jnp.bfloat16)
    result = (
        residual
        + jnp.dot(active, down_full, preferred_element_type=jnp.float32)
        + down_shift.astype(jnp.float32)
    )
    output = result.astype(jnp.bfloat16).reshape(row_shape)
    regathered = (
        lax.all_gather(ln1_gain, ("dp", "ctx"), axis=0, tiled=True),
        lax.all_gather(ln1_bias, ("dp", "ctx"), axis=0, tiled=True),
        lax.all_gather(w_qkv, ("dp", "ctx"), axis=0, tiled=True),
        lax.all_gather(bias_query, ("dp", "ctx"), axis=0, tiled=True),
        lax.all_gather(bias_value, ("dp", "ctx"), axis=0, tiled=True),
        lax.all_gather(w_out, ("dp", "ctx"), axis=0, tiled=True),
        lax.all_gather(bias_out, ("dp", "ctx"), axis=0, tiled=True),
        lax.all_gather(ln2_gain, ("dp", "ctx"), axis=0, tiled=True),
        lax.all_gather(ln2_bias, ("dp", "ctx"), axis=0, tiled=True),
        lax.all_gather(w_up, ("dp", "ctx"), axis=0, tiled=True),
        lax.all_gather(bias_up, ("dp", "ctx"), axis=0, tiled=True),
        lax.all_gather(w_down, ("dp", "ctx"), axis=0, tiled=True),
        lax.all_gather(bias_down, ("dp", "ctx"), axis=0, tiled=True),
    )
    (
        gain_one,
        shift_one,
        qkv_full,
        query_shift,
        value_shift,
        out_full,
        out_shift,
        gain_two,
        shift_two,
        up_full,
        up_shift,
        down_full,
        down_shift,
    ) = regathered
    upstream = cotangent.reshape(total_rows, model_width)
    upstream_wide = upstream.astype(jnp.float32)
    grad_w_down = contract_rows(active, upstream)
    grad_bias_down = jnp.sum(upstream_wide, axis=0)
    grad_active = contract_cols(upstream, down_full)
    gelu_back = jax.vjp(jax.nn.gelu, hidden)[1]
    grad_hidden = gelu_back(grad_active)[0].astype(jnp.bfloat16)
    grad_bias_up = jnp.sum(grad_hidden.astype(jnp.float32), axis=0)
    grad_w_up = contract_rows(normed_two, grad_hidden)
    grad_normed_two = contract_cols(grad_hidden, up_full)
    norm_two_back = jax.vjp(
        layer_norm, residual, gain_two.astype(jnp.float32), shift_two.astype(jnp.float32)
    )[1]
    grad_from_norm, grad_ln2_gain, grad_ln2_bias = norm_two_back(grad_normed_two)
    grad_residual = upstream_wide + grad_from_norm
    grad_bias_out = jnp.sum(grad_residual, axis=0)
    grad_residual_low = grad_residual.astype(jnp.bfloat16)
    grad_w_out = contract_rows(attended, grad_residual_low)
    grad_attended = (
        contract_cols(grad_residual_low, out_full).astype(jnp.bfloat16).reshape(row_shape)
    )
    grad_heads = split_heads(grad_attended)
    delta_sum = jnp.sum(grad_heads.astype(jnp.float32) * attended_exact, axis=-1)
    total_high = log_total.astype(jnp.bfloat16)
    total_low = (log_total - total_high.astype(jnp.float32)).astype(jnp.bfloat16)
    delta_high = delta_sum.astype(jnp.bfloat16)
    delta_low = (delta_sum - delta_high.astype(jnp.float32)).astype(jnp.bfloat16)
    total_used = total_high.astype(jnp.float32) + total_low.astype(jnp.float32)
    delta_used = delta_high.astype(jnp.float32) + delta_low.astype(jnp.float32)
    key_heads = split_heads(key_rows)
    value_heads = split_heads(value_rows)
    query_mine = (query_heads, grad_heads, total_used, delta_used, segments, places)
    key_mine = (key_heads, value_heads, segments, places)
    grad_query = query_side(
        query_mine,
        (
            lax.all_gather(key_rows, "ctx", axis=1, tiled=True),
            lax.all_gather(value_rows, "ctx", axis=1, tiled=True),
            lax.all_gather(segments, "ctx", axis=1, tiled=True),
        ),
    )
    grad_key, grad_value = key_side(
        key_mine,
        (
            lax.all_gather(query_rows, "ctx", axis=1, tiled=True),
            lax.all_gather(grad_attended, "ctx", axis=1, tiled=True),
            lax.all_gather(total_high, "ctx", axis=1, tiled=True),
            lax.all_gather(total_low, "ctx", axis=1, tiled=True),
            lax.all_gather(delta_high, "ctx", axis=1, tiled=True),
            lax.all_gather(delta_low, "ctx", axis=1, tiled=True),
            lax.all_gather(segments, "ctx", axis=1, tiled=True),
        ),
    )
    query_part = (grad_query.astype(jnp.bfloat16) * SCALING).reshape(total_rows, model_width)
    key_part = grad_key.astype(jnp.bfloat16).reshape(total_rows, model_width)
    value_part = grad_value.astype(jnp.bfloat16).reshape(total_rows, model_width)
    grad_projected = jnp.concatenate([query_part, key_part, value_part], axis=1)
    grad_bias_query = jnp.sum(query_part.astype(jnp.float32), axis=0)
    grad_bias_value = jnp.sum(value_part.astype(jnp.float32), axis=0)
    grad_w_qkv = contract_rows(normed, grad_projected)
    grad_normed = contract_cols(grad_projected, qkv_full)
    norm_one_back = jax.vjp(
        layer_norm, flat, gain_one.astype(jnp.float32), shift_one.astype(jnp.float32)
    )[1]
    grad_from_first, grad_ln1_gain, grad_ln1_bias = norm_one_back(grad_normed)
    grad_tokens = (grad_residual + grad_from_first).astype(jnp.bfloat16).reshape(row_shape)
    owned = (
        lax.psum_scatter(grad_ln1_gain, ("dp", "ctx"), scatter_dimension=0, tiled=True),
        lax.psum_scatter(grad_ln1_bias, ("dp", "ctx"), scatter_dimension=0, tiled=True),
        lax.psum_scatter(grad_w_qkv, ("dp", "ctx"), scatter_dimension=0, tiled=True),
        lax.psum_scatter(grad_bias_query, ("dp", "ctx"), scatter_dimension=0, tiled=True),
        lax.psum_scatter(grad_bias_value, ("dp", "ctx"), scatter_dimension=0, tiled=True),
        lax.psum_scatter(grad_w_out, ("dp", "ctx"), scatter_dimension=0, tiled=True),
        lax.psum_scatter(grad_bias_out, ("dp", "ctx"), scatter_dimension=0, tiled=True),
        lax.psum_scatter(grad_ln2_gain, ("dp", "ctx"), scatter_dimension=0, tiled=True),
        lax.psum_scatter(grad_ln2_bias, ("dp", "ctx"), scatter_dimension=0, tiled=True),
        lax.psum_scatter(grad_w_up, ("dp", "ctx"), scatter_dimension=0, tiled=True),
        lax.psum_scatter(grad_bias_up, ("dp", "ctx"), scatter_dimension=0, tiled=True),
        lax.psum_scatter(grad_w_down, ("dp", "ctx"), scatter_dimension=0, tiled=True),
        lax.psum_scatter(grad_bias_down, ("dp", "ctx"), scatter_dimension=0, tiled=True),
    )
    return (
        output,
        grad_tokens,
        owned[0],
        owned[1],
        owned[2],
        owned[3],
        owned[4],
        owned[5],
        owned[6],
        owned[7],
        owned[8],
        owned[9],
        owned[10],
        owned[11],
        owned[12],
    )


AXES = ("dp", "ctx")
WORK = {
    "attend": 8.0,
    "hidden": 5.5,
    "feed": 4.5,
    "attend_back": 10.0,
    "project_back": 5.0,
    "attend_grad": 2.5,
    "project_out": 2.4,
}
PACE = 1.15e9 * 0.01
LANES = 128
BIG = -1e30
ROOT = math.sqrt(2.0 / math.pi)
CUBIC = 0.044715
F32 = jnp.float32
BF16 = jnp.bfloat16


def dot(left, right, contract=((1,), (0,))):
    return lax.dot_general(left, right, (contract, ((), ())), preferred_element_type=F32)


def normalize(values):
    center = values - jnp.mean(values, axis=-1, keepdims=True)
    factor = lax.rsqrt(jnp.mean(center * center, axis=-1, keepdims=True) + EPSILON)
    return center * factor, factor


def norm_back(grad, normal, factor):
    return factor * (
        grad
        - jnp.mean(grad, axis=-1, keepdims=True)
        - normal * jnp.mean(grad * normal, axis=-1, keepdims=True)
    )


def size_of(shape, dtype):
    lanes = -(-shape[-1] // LANES) * LANES
    rows = -(-shape[-2] // 16) * 16 if len(shape) > 1 else 16
    lead = math.prod(shape[:-2]) if len(shape) > 2 else 1
    return lead * rows * lanes * jnp.dtype(dtype).itemsize


def run(name, body, place, args, outs, scratch=(), far=(), extra=8 << 20):
    held = sum(size_of(s, d) for s, d in scratch)
    held += sum(size_of(args[i].shape, args[i].dtype) for i in far)
    held += sum(size_of(s, d) for s, d in outs)
    whole = pl.BlockSpec(memory_space=pltpu.VMEM)
    specs = [pl.BlockSpec(memory_space=pltpu.HBM) if i in far else whole for i in range(len(args))]
    buffers = [pltpu.VMEM(s, d) for s, d in scratch]

    def fetching(place, *refs):
        near, sems = list(refs[: -len(far) - 1]), refs[-1]
        copies = []
        for k, (i, ref) in enumerate(zip(far, refs[-len(far) - 1 : -1])):
            copies.append(pltpu.make_async_copy(near[i], ref, sems.at[k]))
            copies[-1].start()
            near[i] = ref
        for copy in copies:
            copy.wait()
        body(place, *near)

    if far:
        buffers += [pltpu.VMEM(args[i].shape, args[i].dtype) for i in far]
        buffers += [pltpu.SemaphoreType.DMA((len(far),))]
    return pl.pallas_call(
        fetching if far else body,
        name=name,
        out_shape=[jax.ShapeDtypeStruct(s, d) for s, d in outs],
        in_specs=[pl.BlockSpec(memory_space=pltpu.SMEM)] + specs,
        out_specs=[whole] * len(outs),
        scratch_shapes=buffers,
        compiler_params=pltpu.CompilerParams(vmem_limit_bytes=min(held + extra, 56 << 20)),
        cost_estimate=pl.CostEstimate(
            flops=int(WORK.get(name, 1.5) * PACE), bytes_accessed=1, transcendentals=0
        ),
    )(place, *args)


def rows_at(start, size, align):
    return pl.ds(pl.multiple_of(start, align), size)


class Grid:
    def __init__(self, dp, ctx):
        self.dp, self.ctx = dp, ctx
        self.ny, self.nx, self.nz = 2, dp // 2, ctx // 2

    def move(self, value, step):
        pairs = []
        for i in range(self.dp * self.ctx):
            core, z = i % 2, (i // 2) % self.nz
            x, y = (i // self.ctx) % self.nx, i // (self.ctx * self.nx)
            y, x, z, core = step(y, x, z, core)
            pairs.append((i, ((y * self.nx + x) * self.nz + z) * 2 + core))
        return lax.ppermute(value, AXES, pairs)

    def core(self, value):
        return self.move(value, lambda y, x, z, c: (y, x, z, 1 - c))

    def along_x(self, value):
        return self.move(value, lambda y, x, z, c: (y, 1 - x, z, c))

    def along_y(self, value):
        return self.move(value, lambda y, x, z, c: (1 - y, x, z, c))

    def along_xy(self, value):
        return self.move(value, lambda y, x, z, c: (1 - y, 1 - x, z, c))

    def along_z(self, value, hop):
        return self.move(value, lambda y, x, z, c: (y, x, (z + hop) % self.nz, c))


    def lines(self):
        return [[2 * z + core for z in range(self.nz)] for core in range(2)]


def from_z(z, hop):
    return lax.rem(z - hop + 4, 4)


def order_kernel(place, own, r1, r2, r3, out):
    z = place[2]
    out[z] = own[...]
    out[from_z(z, 1)] = r1[...]
    out[from_z(z, 2)] = r2[...]
    out[from_z(z, 3)] = r3[...]


def block_index(place):
    y, x = place[0], place[1]
    return (2 * y + x, 2 * y + 1 - x, 2 * (1 - y) + x, 2 * (1 - y) + 1 - x)


def fold(block):
    rows = block.shape[0] // 2
    return jnp.concatenate([block[:rows], block[rows:]], axis=1)


def deal(place, blocks, targets):
    for hop, target in enumerate(targets):
        target[...] = blocks[lax.rem(place[2] + hop, 4)]


def unfold(ref, lanes):
    return jnp.concatenate([ref[:, :lanes], ref[:, lanes:]], axis=0)


def seen(seg_col, seg_row, i, span):
    keys = span * (i + 1)
    same = seg_col[i * span : (i + 1) * span] == seg_row[:, :keys]
    place_q = i * span + lax.broadcasted_iota(jnp.int32, (span, keys), 0)
    place_k = lax.broadcasted_iota(jnp.int32, (span, keys), 1)
    return jnp.where(same & (place_q >= place_k), 0.0, BIG).astype(F32)


def attend_kernel(
    place,
    own,
    other,
    b0,
    bx,
    by,
    bxy,
    seg_row,
    seg_col,
    weight,
    vectors,
    normed,
    rows,
    exact,
    totals,
    out_own,
    out_1,
    out_2,
    out_3,
    lifted,
    spare,
    out,
):
    core, second = place[3], place[2] % 2 == 1
    lines, run_rows, width = own.shape
    group = width // 4
    span = 2 * run_rows
    part = b0.shape[0] * b0.shape[1]
    cut = weight.shape[1]
    for index, piece in zip(block_index(place), (b0, bx, by, bxy)):
        for k in range(piece.shape[0]):
            here = rows_at(index * part + k * piece.shape[1], piece.shape[1], 16)
            weight[here] = piece[k, :, :cut]
    vectors[...] = jnp.transpose(weight[:, 4 * LANES :].astype(F32))[64:80]
    gain, shift = vectors[0:1, :], vectors[1:2, :]
    mine = pl.ds(pl.multiple_of(core * 2 * group, LANES), 2 * group)
    bias_q, bias_v = vectors[2:3, mine], vectors[3:4, mine]
    bias_q = jnp.where(second, bias_q[:, group:], bias_q[:, :group])
    bias_v = jnp.where(second, bias_v[:, group:], bias_v[:, :group])
    for i in range(lines):
        spare[i, rows_at(core * run_rows, run_rows, 16)] = own[i]
        spare[i, rows_at((1 - core) * run_rows, run_rows, 16)] = other[i]
    for i in range(lines):
        here = slice(i * span, (i + 1) * span)
        value = (normalize(spare[i].astype(F32))[0] * gain + shift).astype(BF16)
        normed[here] = value
        projected = dot(value, weight[:, : 3 * group])
        rows[here, :group] = ((projected[:, :group] + bias_q) * SCALING).astype(BF16)
        rows[here, group : 2 * group] = projected[:, group : 2 * group].astype(BF16)
        rows[here, 2 * group :] = (projected[:, 2 * group :] + bias_v).astype(BF16)
    for i in range(lines):
        here = slice(i * span, (i + 1) * span)
        keys = span * (i + 1)
        bias = seen(seg_col, seg_row, i, span)
        heads = []
        for h in range(3):
            at = h * HEAD_DIM
            query = rows[here, at : at + HEAD_DIM]
            key = rows[:keys, group + at : group + at + HEAD_DIM]
            value = rows[:keys, 2 * group + at : 2 * group + at + HEAD_DIM]
            scores = dot(query, key, ((1,), (1,))) + bias
            peak = jnp.max(scores, axis=-1, keepdims=True)
            expanded = jnp.exp(scores - peak)
            total = jnp.sum(expanded, axis=-1, keepdims=True)
            mixed = dot(expanded.astype(BF16), value) / total
            heads.append(mixed.astype(BF16))
            exact[here, at : at + HEAD_DIM] = mixed
            totals[here, h : h + 1] = peak + jnp.log(total)
        out[i] = fold(jnp.concatenate(heads, axis=1))
    deal(place, out, (out_own, out_1, out_2, out_3))
    held = vectors[8:12, mine]
    few = 2 * group // 16
    for j in range(16):
        for k in range(4):
            at = (4 * j + k) * few
            lifted[:, at : at + few] = held[k : k + 1, j * few : (j + 1) * few]


def out_kernel(place, own, r1, r2, r3, weight, attended, *partial):
    z = place[2]
    span, group = attended.shape[1:]
    attended[z] = unfold(own, group)
    for hop, piece in ((1, r1), (2, r2), (3, r3)):
        attended[from_z(z, hop)] = unfold(piece, group)
    for s in range(2):
        partial[s][...] = (
            dot(attended[2 * s], weight[:group]) + dot(attended[2 * s + 1], weight[group:])
        ).astype(BF16)


def place_rows(core, target, own, other):
    run_rows = own.shape[0] // 2
    for s in range(2):
        for which, piece in ((core, own), (1 - core, other)):
            target[rows_at((2 * s + which) * run_rows, run_rows, 16)] = piece[
                s * run_rows : (s + 1) * run_rows
            ]


def hidden_kernel(
    place,
    tokens_own,
    tokens_other,
    part_first,
    part_second,
    other_first,
    other_second,
    cot_own,
    cot_other,
    up,
    vectors,
    bias_up,
    cot,
    residual,
    normed,
    active,
    slope,
    tokens,
):
    place_rows(place[3], cot, cot_own, cot_other)
    place_rows(place[3], tokens, tokens_own, tokens_other)
    gain, shift, bias_out = vectors[5:6, :], vectors[6:7, :], vectors[4:5, :]
    span = tokens.shape[0] // 2
    for s in range(2):
        here = slice(s * span, (s + 1) * span)
        one, two = ((part_first, other_first), (part_second, other_second))[s]
        wide = tokens[here].astype(F32) + (one[...].astype(F32) + two[...].astype(F32)) + bias_out
        residual[here] = wide
        low = (normalize(wide)[0] * gain + shift).astype(BF16)
        normed[here] = low
        hidden = dot(low, up[...]) + bias_up[...]
        square = hidden * hidden
        bent = jnp.tanh(ROOT * (hidden + CUBIC * (square * hidden)))
        active[here] = (0.5 * hidden * (1.0 + bent)).astype(BF16)
        slope[here] = 0.5 * (1.0 + bent) + 0.5 * hidden * (1.0 - bent * bent) * (
            ROOT * (1.0 + 3.0 * CUBIC * square)
        )


def down_weights_kernel(place, active, cot, down_own, *targets):
    *targets, spare = targets
    core = place[3]
    spare[...] = dot(active[...], cot[...], ((0,), (0,))).astype(BF16)
    width = cot.shape[1]
    for j in range(8):
        for k in range(2):
            lanes = slice(k * width, (k + 1) * width)
            here = 192 * j + 48 * k
            down_own[48 * j : 48 * j + 48, lanes] = spare[rows_at(here + 96 * core, 48, 16)]
            targets[j // 3][48 * (j % 3) : 48 * (j % 3) + 48, lanes] = spare[
                rows_at(here + 96 * (1 - core), 48, 16)
            ]


def feed_kernel(
    place,
    residual,
    active,
    slope,
    cot,
    up,
    down,
    grad_hidden,
    result,
    grad_normed,
    low_first,
    low_second,
    sums,
    lifted,
):
    span = cot.shape[0] // 2
    for s in range(2):
        here = slice(s * span, (s + 1) * span)
        upstream = cot[here]
        grad = (dot(upstream, down[...], ((1,), (1,))) * slope[here]).astype(BF16)
        grad_hidden[here] = grad
        back = dot(grad, up[...], ((1,), (1,)))
        grad_normed[here] = back
        (low_first, low_second)[s][...] = back.astype(BF16)
        result[here] = dot(active[here], down[...])
        rows = jnp.concatenate(
            [
                jnp.sum(back * normalize(residual[here])[0], axis=0, keepdims=True),
                jnp.sum(back, axis=0, keepdims=True),
                0.5 * jnp.sum(upstream.astype(F32), axis=0, keepdims=True),
            ],
            axis=0,
        )
        total = jnp.sum(grad.astype(F32), axis=0, keepdims=True)
        if s == 0:
            sums[...] = rows
        else:
            sums[...] = sums[...] + rows
            held = first + total
        first = total
    few = held.shape[1] // 64
    for j in range(16):
        for k in range(4):
            at = (4 * j + k) * few
            lifted[k : k + 1, j * few : (j + 1) * few] = held[:, at : at + few]


def up_weights_kernel(place, normed, grad_hidden, grad_up):
    grad_up[...] = dot(normed[...], grad_hidden[...], ((0,), (0,))).astype(BF16)


def attend_grad_kernel(
    place,
    back_own,
    other_first,
    other_second,
    residual,
    cot,
    vectors,
    weight,
    attended,
    grad_residual,
    deal_own,
    deal_1,
    deal_2,
    deal_3,
    out_own,
    out_other,
    sum_out,
    spare,
    blocks,
):
    core = place[3]
    gain = vectors[5:6, :]
    span = cot.shape[0] // 2
    group = attended.shape[2]
    half = 2 * group
    products = [None, None]
    for s in range(2):
        here = slice(s * span, (s + 1) * span)
        normal, factor = normalize(residual[here])
        wide = cot[here].astype(F32) + norm_back(
            (back_own[here] + (other_first, other_second)[s][...].astype(F32)) * gain,
            normal,
            factor,
        )
        grad_residual[here] = wide
        low = wide.astype(BF16)
        grad = dot(low, weight[...], ((1,), (1,))).astype(BF16)
        total = 0.5 * jnp.sum(wide, axis=0, keepdims=True)
        sum_out[...] = total if s == 0 else sum_out[...] + total
        for g in range(2):
            blocks[2 * s + g] = fold(grad[:, g * group : (g + 1) * group])
            product = dot(attended[2 * s + g], low, ((0,), (0,)))
            products[g] = product if s == 0 else products[g] + product
    deal(place, blocks, (deal_own, deal_1, deal_2, deal_3))
    for g in range(2):
        spare[g * group : (g + 1) * group] = products[g].astype(BF16)
    out_own[...] = spare[:, rows_at(core * half, half, LANES)]
    out_other[...] = spare[:, rows_at((1 - core) * half, half, LANES)]


def attend_back_kernel(
    place,
    rows,
    exact,
    totals,
    seg_row,
    seg_col,
    own,
    r1,
    r2,
    r3,
    joined,
    grad,
    keys_grad,
):
    z = place[2]
    span, group = rows.shape[0] // 4, grad.shape[1]
    grad[rows_at(z * span, span, span)] = unfold(own, group)
    for hop, piece in ((1, r1), (2, r2), (3, r3)):
        grad[rows_at(from_z(z, hop) * span, span, span)] = unfold(piece, group)
    for i in (3, 2, 1, 0):
        here = slice(i * span, (i + 1) * span)
        keys = span * (i + 1)
        bias = seen(seg_col, seg_row, i, span)
        for h in range(3):
            at = h * HEAD_DIM
            lanes = slice(at, at + HEAD_DIM)
            query = rows[here, lanes]
            key = rows[:keys, group + at : group + at + HEAD_DIM]
            value = rows[:keys, 2 * group + at : 2 * group + at + HEAD_DIM]
            upstream = grad[here, lanes]
            delta = jnp.sum(upstream.astype(F32) * exact[here, lanes], axis=-1, keepdims=True)
            probs = jnp.exp(dot(query, key, ((1,), (1,))) + bias - totals[here, h : h + 1])
            slopes = dot(upstream, value, ((1,), (1,)))
            grad_scores = (probs * (slopes - delta)).astype(BF16)
            grad_query = dot(grad_scores, key).astype(BF16)
            joined[here, lanes] = (grad_query.astype(F32) * SCALING).astype(BF16)
            grad_key = dot(grad_scores, query, ((0,), (0,)))
            grad_value = dot(probs.astype(BF16), upstream, ((0,), (0,)))
            if i == 3:
                keys_grad[2 * h] = grad_key
                keys_grad[2 * h + 1] = grad_value
            else:
                keys_grad[2 * h, :keys] = keys_grad[2 * h, :keys] + grad_key
                keys_grad[2 * h + 1, :keys] = keys_grad[2 * h + 1, :keys] + grad_value
    for h in range(3):
        for k in range(2):
            at = (k + 1) * group + h * HEAD_DIM
            joined[:, at : at + HEAD_DIM] = keys_grad[2 * h + k].astype(BF16)


def project_back_kernel(
    place,
    joined,
    weight,
    normed,
    tokens_own,
    tokens_other,
    sum_out,
    sums_two,
    lifted,
    o_own,
    o_x,
    o_y,
    o_xy,
    back_own,
    back_first,
    back_second,
    back_third,
    product,
    small,
):
    core = place[3]
    second = place[2] % 2 == 1
    lines, run_rows, width = tokens_own.shape
    span, group = 2 * run_rows, width // 4
    small[...] = jnp.zeros_like(small)
    small[4:5] = sum_out[...]
    small[5:8] = sums_two[...]
    small[8:12, pl.ds(pl.multiple_of(core * 2 * group, LANES), 2 * group)] = lifted[...]
    mine = pl.ds(pl.multiple_of(core * 2 * group, LANES), 2 * group)
    empty = jnp.zeros((1, group), F32)
    for row, at in ((2, 0), (3, 2 * group)):
        total = jnp.sum(joined[:, at : at + group].astype(F32), axis=0, keepdims=True)
        small[row : row + 1, mine] = jnp.where(
            second,
            jnp.concatenate([empty, total], axis=1),
            jnp.concatenate([total, empty], axis=1),
        )
    for i in range(lines):
        for which, tokens in ((core, tokens_own), (1 - core, tokens_other)):
            here = rows_at(i * span + which * run_rows, run_rows, 16)
            step = dot(joined[here], weight[:, : 3 * group], ((1,), (1,)))
            if tokens is tokens_own:
                back_own[i] = step
            else:
                low = step.astype(BF16)
                for target, start in ((back_first, 0), (back_second, 192), (back_third, 384)):
                    first = max(start, i * run_rows)
                    last = min(start + target.shape[0], (i + 1) * run_rows)
                    if first < last:
                        target[first - start : last - start] = low[
                            first - i * run_rows : last - i * run_rows
                        ]
            normal = normalize(tokens[i].astype(F32))[0]
            small[0:1] = small[0:1] + jnp.sum(step * normal, axis=0, keepdims=True)
            small[1:2] = small[1:2] + jnp.sum(step, axis=0, keepdims=True)
    product[:, : 3 * group] = dot(normed[...], joined[...], ((0,), (0,))).astype(BF16)
    product[:, 3 * group :] = jnp.transpose(small[...])[:, :64].astype(BF16)
    size = o_own.shape[0]
    for index, target in zip(block_index(place), (o_own, o_x, o_y, o_xy)):
        target[...] = product[rows_at(index * size, size, 16)]


def split_kernel(targets, size, block, place):
    y, x = place[0], place[1]
    own, over_x, over_y, low, high = targets
    block(y, x, slice(0, size), own)
    block(y, 1 - x, slice(0, size), over_x)
    block(1 - y, x, slice(0, size), over_y)
    block(1 - y, 1 - x, slice(0, size // 2), low)
    block(1 - y, 1 - x, slice(size // 2, size), high)


def split_down_kernel(place, own, first, second, third, *targets):
    *targets, other = targets
    core, size = place[3], targets[0].shape[0]
    other[:144] = first[...]
    other[144:288] = second[...]
    other[288:] = third[...]

    def block(y, x, rows, target):
        here = rows_at(x * size + rows.start, rows.stop - rows.start, 16)
        target[...] = jnp.where(y == core, own[here], other[here])

    split_kernel(targets, size, block, place)


def split_up_kernel(place, up, out_own, out_other, *targets):
    core, size = place[3], targets[0].shape[0]
    cut = up.shape[1]

    def block(y, x, rows, target):
        count = rows.stop - rows.start
        target[:, :cut] = up[rows_at((2 * y + x) * size + rows.start, count, 16)]
        here = rows_at(x * size + rows.start, count, 16)
        target[:, cut:] = jnp.where(y == core, out_own[here], out_other[here])

    split_kernel(targets, size, block, place)


def collect_kernel(place, over_x, over_y, low, high, sum_x, sum_y):
    half = low.shape[0]
    sum_x[:half] = over_x[:half]
    sum_x[half:] = (over_x[half:].astype(F32) + high[...].astype(F32)).astype(BF16)
    sum_y[:half] = (over_y[:half].astype(F32) + low[...].astype(F32)).astype(BF16)
    sum_y[half:] = over_y[half:]


def spread_kernel(place, own, from_x, from_y, low, high, up, down):
    half = low.shape[0]
    cut = up.shape[2]
    blocks = block_index(place)
    for index, piece in zip(blocks, (own, from_x, from_y)):
        up[index] = piece[:, :cut]
        down[index] = piece[:, cut:]
    up[blocks[3], :half] = low[:, :cut]
    up[blocks[3], half:] = high[:, :cut]
    down[blocks[3], :half] = low[:, cut:]
    down[blocks[3], half:] = high[:, cut:]


def line_down_kernel(place, a, b, c, d, down):
    rows, width = down.shape[0] // 2, down.shape[1]
    for k in range(2):
        here = (slice(0, rows), slice(k * width, (k + 1) * width))
        down[k * rows : (k + 1) * rows] = (a[here].astype(F32) + b[here].astype(F32)) + (
            c[here].astype(F32) + d[here].astype(F32)
        )


def deal_all_kernel(place, up, up_x, up_y, qkv, qkv_x, qkv_y, qkv_xy, *targets):
    *targets, spare = targets
    cut = up.shape[1]
    spare[:, :cut] = (
        up[...].astype(F32) + (up_x[...].astype(F32) + up_y[...].astype(F32))
    ).astype(BF16)
    spare[:, cut:] = (
        (qkv[...].astype(F32) + qkv_x[...].astype(F32))
        + (qkv_y[...].astype(F32) + qkv_xy[...].astype(F32))
    ).astype(BF16)
    size = targets[0].shape[0]
    for hop, target in enumerate(targets):
        target[...] = spare[rows_at(lax.rem(place[2] + hop, 4) * size, size, 16)]


def line_all_kernel(place, own, r1, r2, r3, mine, theirs, spare, *, cut):
    second = place[2] % 2 == 1
    third = (own.shape[1] - cut - 64) // 3
    same = own[...].astype(F32) + r2[...].astype(F32)
    cross = r1[...].astype(F32) + r3[...].astype(F32)
    spare[:, :cut] = (same + cross)[:, :cut]
    first, last = jnp.where(second, cross, same), jnp.where(second, same, cross)
    for k in range(3):
        here = slice(cut + k * third, cut + (k + 1) * third)
        at = cut + 2 * k * third
        spare[:, at : at + third] = first[:, here]
        spare[:, at + third : at + 2 * third] = last[:, here]
    at = cut + 6 * third
    spare[:, at : at + 64] = (same + cross)[:, cut + 3 * third :]
    spare[:, at + 64 :] = jnp.zeros((spare.shape[0], 64), F32)
    rows = mine.shape[0]
    mine[...] = spare[rows_at(place[3] * rows, rows, 8)]
    theirs[...] = spare[rows_at((1 - place[3]) * rows, rows, 8)]


def out_split_kernel(place, b0, bx, by, bxy, own, other, spare):
    core = place[3]
    first = b0.shape[2] - own.shape[1]
    size = b0.shape[0] * b0.shape[1]
    for index, piece in zip(block_index(place), (b0, bx, by, bxy)):
        for k in range(piece.shape[0]):
            here = rows_at(index * size + k * piece.shape[1], piece.shape[1], 16)
            spare[here] = piece[k, :, first:]
    half = own.shape[0]
    own[...] = spare[rows_at(core * half, half, 16)]
    other[...] = spare[rows_at((1 - core) * half, half, 16)]


def out_halves_kernel(place, own, other, out):
    core = place[3]
    half = out.shape[0]
    for which, piece in ((core, own), (1 - core, other)):
        out[:, rows_at(which * half, half, LANES)] = piece[...]


def down_halves_kernel(place, own, other, down):
    core = place[3]
    width = down.shape[1]
    for which, piece in ((core, own), (1 - core, other)):
        for j in range(8):
            for k in range(2):
                down[rows_at(192 * j + 96 * which + 48 * k, 48, 16)] = piece[
                    48 * j : 48 * j + 48, k * width : (k + 1) * width
                ]


def deal_back_kernel(place, own, first, second, third, down, down_x, down_y, *targets):
    *targets, spare, total = targets
    lines, rows, width = own.shape
    spare[0:192] = first[...].astype(F32)
    spare[192:384] = second[...].astype(F32)
    spare[384:] = third[...].astype(F32)
    total[...] = (
        down[...].astype(F32) + (down_x[...].astype(F32) + down_y[...].astype(F32))
    ).astype(BF16)
    size = total.shape[0] // 4
    for hop, target in enumerate(targets):
        k = lax.rem(place[2] + hop, 4)
        target[:size] = total[rows_at(k * size, size, 16)]
        block = (own[k] + spare[rows_at(k * rows, rows, rows)]).astype(BF16)
        target[size:] = fold(block)


def final_kernel(place, own, r1, r2, r3, grad_residual, tokens, vectors, out, held):
    z, core = place[2], place[3]
    rows, width = held.shape[1:]
    start = own.shape[0] - rows // 2
    for hop, piece in enumerate((own, r1, r2, r3)):
        held[from_z(z, hop)] = unfold(piece.at[start:], width)
    gain = vectors[0:1, :]
    for s in range(2):
        here = slice(s * rows, (s + 1) * rows)
        there = rows_at((2 * s + core) * rows, rows, 16)
        normal, factor = normalize(tokens[here].astype(F32))
        grad = (held[2 * s].astype(F32) + held[2 * s + 1].astype(F32)) * gain
        out[here] = (grad_residual[there] + norm_back(grad, normal, factor)).astype(BF16)


def split_local(
    grid,
    tokens,
    segments,
    cotangent,
    ln1_gain,
    ln1_bias,
    w_qkv,
    bias_query,
    bias_value,
    w_out,
    bias_out,
    ln2_gain,
    ln2_bias,
    w_up,
    bias_up,
    w_down,
    bias_down,
):
    count, run_rows, width = tokens.shape
    own_rows = count * run_rows
    all_rows = 2 * own_rows
    span = 2 * run_rows
    half = width // 2
    group = half // 2
    hidden_half = w_up.shape[1] // 2
    shard = w_qkv.shape[0]
    dp, ctx = lax.axis_index("dp"), lax.axis_index("ctx")
    y, x, z, core = dp // grid.nx, dp % grid.nx, ctx // 2, ctx % 2
    place = jnp.stack([y, x, z, core]).astype(jnp.int32)
    first_core = core == 0

    def pick(array, index, axis):
        return lax.dynamic_index_in_dim(array, index, axis, keepdims=False)

    def both(own, other, axis):
        return jnp.where(
            first_core,
            jnp.concatenate([own, other], axis),
            jnp.concatenate([other, own], axis),
        )

    def z_all(value):
        return [value] + [grid.along_z(value, hop) for hop in (1, 2, 3)]

    def after(values, *waited):
        return lax.optimization_barrier((values, waited))[0]

    def z_send(blocks):
        return [grid.along_z(blocks[hop], hop) for hop in (1, 2, 3)]

    flat = tokens.reshape(own_rows, width)
    small = jnp.stack(
        [ln1_gain, ln1_bias, bias_query, bias_value, bias_out, ln2_gain, ln2_bias, bias_down], axis=1
    )
    lifted = bias_up.reshape(4, shard).T
    seg_lanes = jnp.pad(segments.astype(BF16).reshape(8, 32), ((0, shard - 8), (0, 0)))
    vector_lanes = jnp.concatenate(
        [small, lifted, jnp.zeros((shard, 4), BF16), seg_lanes, jnp.zeros((shard, 16), BF16)],
        axis=1,
    )
    split_qkv = w_qkv.reshape(shard, 3, 2, half)
    split_up = w_up.reshape(shard, 2, hidden_half)
    split_out = w_out.reshape(shard, 2, half)
    cut = 3 * group + 64
    size = 8 * shard

    def columns(which):
        chosen = pick(split_qkv, which, 2)
        return jnp.concatenate(
            [
                chosen[:, :, :group].reshape(shard, 3 * group),
                vector_lanes,
                chosen[:, :, group:].reshape(shard, 3 * group),
                vector_lanes,
                pick(split_out, which, 1),
                pick(split_up, which, 1),
            ],
            axis=1,
        )

    flat_other = grid.core(flat)
    cot_own = cotangent.reshape(own_rows, width)
    cot_other = grid.core(cot_own)
    piece = both(columns(core), after(grid.core(columns(1 - core)), flat_other, cot_other), 0)
    second_group = lax.rem(z, 2) == 1
    lanes_out = piece[:, 2 * cut : 2 * cut + half]
    first, last = piece[:, :cut], piece[:, cut : 2 * cut]
    piece_same = jnp.concatenate([jnp.where(second_group, last, first), lanes_out], axis=1)
    piece_cross = jnp.concatenate([jnp.where(second_group, first, last), lanes_out], axis=1)
    line_one = [
        piece_same,
        grid.along_z(piece_cross, 1),
        grid.along_z(piece_same, 2),
        grid.along_z(piece_cross, 3),
    ]
    def order(name, pieces):
        return run(name, order_kernel, place, pieces, [((4,) + pieces[0].shape, BF16)])[0]

    def kernel(name, body, args, outs, scratch=(), far=(), extra=6 << 20):
        return run(name, body, place, args, outs, scratch, far, extra)

    def order_rows(name, pieces):
        lanes = pieces[0].shape[1]
        return kernel(
            name, order_kernel, pieces, [((4, 2 * shard, lanes), BF16)], far=(1, 2, 3)
        )[0].reshape(size, lanes)

    plane_one = order("order_qkv", line_one)
    from_x, from_y, from_xy = (
        grid.along_x(plane_one),
        grid.along_y(plane_one),
        grid.along_xy(plane_one),
    )
    piece_b = jnp.concatenate([w_down[: 2 * shard], w_down[2 * shard :]], axis=1)

    rest_piece = jnp.concatenate([piece[:, 2 * cut + half :], piece_b], axis=1)
    rest_line = z_all(after(rest_piece, line_one))
    waiting = after(tokens, line_one)
    token_pieces = [
        grid.along_z(pick(waiting, lax.rem(z + hop, 4) // 2, 0), hop) for hop in (1, 2, 3)
    ]
    token_pieces = after(token_pieces, plane_one)
    gathered = order("order_tokens", [pick(tokens, z // 2, 0)] + token_pieces)
    gathered_rows = gathered.reshape(4 * run_rows, width)
    gathered_other = jnp.concatenate(
        [grid.core(gathered_rows[:192]), grid.core(gathered_rows[192:384]), grid.core(gathered_rows[384:])]
    ).reshape(gathered.shape)
    out_parts = run(
        "out_split",
        out_split_kernel,
        place,
        [plane_one, from_x, from_y, from_xy],
        [((half, half), BF16)] * 2,
        [((width, half), BF16)],
    )
    segs = plane_one.reshape(4, 2, shard, cut + half)[:, :, :8, 3 * group + 16 : 3 * group + 48]
    segs = segs.reshape(4, 2, 2, 4 * 32).transpose(2, 0, 1, 3).reshape(2, 8 * run_rows)
    segs = pick(segs, z // 2, 0).astype(F32)

    weight_qkv, vectors, normed, packed, exact, totals, *out_deal, bias_up_half = kernel(
        "attend",
        attend_kernel,
        [
            gathered,
            gathered_other,
            after(plane_one, out_parts),
            from_x,
            from_y,
            from_xy,
            segs.reshape(1, -1),
            segs.reshape(-1, 1),
        ],
        [
            ((width, cut), BF16),
            ((16, width), F32),
            ((4 * span, width), BF16),
            ((4 * span, 3 * group), BF16),
            ((4 * span, group), F32),
            ((4 * span, LANES), F32),
        ]
        + [((run_rows, 2 * group), BF16)] * 4
        + [((1, hidden_half), F32)],
        [((4, span, width), BF16), ((4, run_rows, 2 * group), BF16)],
        far=(3, 4, 5),
        extra=14 << 20,
    )
    out_blocks = out_deal[0]
    out_pieces = z_send(out_deal)

    weight_out = kernel(
        "out_halves",
        out_halves_kernel,
        [out_parts[0], grid.core(out_parts[1])],
        [((half, width), BF16)],
    )[0]

    plane_rest = order_rows("order_rest", [rest_line[0]] + after(rest_line[1:], out_blocks))
    attended, *partial = kernel(
        "project_out",
        out_kernel,
        [out_blocks] + out_pieces + [weight_out],
        [((4, span, group), BF16)] + [((own_rows, width), BF16)] * 2,
        far=(1, 2, 3),
    )
    part_other = [grid.core(member) for member in partial]
    over = after((grid.along_x(plane_rest), grid.along_y(plane_rest)), part_other)
    low, high = grid.along_x(over[1][: 4 * shard]), grid.along_y(over[0][4 * shard :])
    weight_up, mixed_down = kernel(
        "spread",
        spread_kernel,
        [plane_rest, *over, low, high],
        [((4, size, hidden_half), BF16), ((4, size, 2 * width), BF16)],
        far=(1, 2, 3, 4),
    )
    weight_up = weight_up.reshape(width, hidden_half)
    mixed_down = mixed_down.reshape(2, half, 2 * width)
    cot, residual, normed_two, active, slope = kernel(
        "hidden",
        hidden_kernel,
        [
            flat,
            flat_other,
            *partial,
            *part_other,
            cot_own,
            cot_other,
            weight_up,
            vectors,
            bias_up_half,
        ],
        [
            ((all_rows, width), BF16),
            ((all_rows, width), F32),
            ((all_rows, width), BF16),
            ((all_rows, hidden_half), BF16),
            ((all_rows, hidden_half), F32),
        ],
        [((all_rows, width), BF16)],
        far=(0, 1, 6, 7),
        extra=14 << 20,
    )
    weight_down = kernel(
        "down_halves",
        down_halves_kernel,
        [pick(mixed_down, core, 0), grid.core(pick(mixed_down, 1 - core, 0))],
        [((hidden_half, width), BF16)],
    )[0]

    def halve(array, which):
        return pick(array.reshape(2, 2, run_rows, width), which, 1).reshape(own_rows, width)

    def split(name, body, parts, lanes, scratch=()):
        results = [((size, lanes), BF16)] * 3 + [((size // 2, lanes), BF16)] * 2
        return kernel(name, body, parts, results, scratch)

    def diagonal(parts):
        return grid.along_x(parts[3]), grid.along_y(parts[4])

    def collect(name, parts, low, high):
        sum_x, sum_y = kernel(
            name, collect_kernel, [parts[1], parts[2], low, high], [(parts[1].shape, BF16)] * 2, far=(2, 3)
        )
        return parts[0], grid.along_x(sum_x), grid.along_y(sum_y), sum_x

    grad_hidden, result, back_two, *back_low, sums_two, lifted = kernel(
        "feed",
        feed_kernel,
        [residual, active, slope, cot, weight_up, weight_down],
        [
            ((all_rows, hidden_half), BF16),
            ((all_rows, width), F32),
            ((all_rows, width), F32),
            ((own_rows, width), BF16),
            ((own_rows, width), BF16),
            ((3, width), F32),
            ((4, half), F32),
        ],
        extra=14 << 20,
    )
    back_other = [grid.core(member) for member in back_low]
    grad_up = kernel(
        "up_weights",
        up_weights_kernel,
        [normed_two, grad_hidden],
        [((width, hidden_half), BF16)],
        extra=10 << 20,
    )[0]


    down_own, *down_other = kernel(
        "down_weights",
        down_weights_kernel,
        after([active, cot], grad_up),
        [((rows, 2 * width), BF16) for rows in (half, 144, 144, 96)],
        [((hidden_half, width), BF16)],
        extra=10 << 20,
    )
    down_recv = [grid.core(member) for member in down_other]
    grad_residual, *grad_deal, out_own, out_other, sum_out = kernel(
        "attend_grad",
        attend_grad_kernel,
        after(
            [back_two, *back_other, residual, cot, vectors, weight_out, attended],
            down_own,
        ),
        [
            ((all_rows, width), F32),
            *[((run_rows, 2 * group), BF16)] * 4,
            ((half, half), BF16),
            ((half, half), BF16),
            ((1, width), F32),
        ],
        [((half, width), BF16), ((4, run_rows, 2 * group), BF16)],
    )
    grad_blocks = grad_deal[0]
    grad_pieces = z_send(grad_deal)
    out_recv = grid.core(out_other)
    def split(name, body, parts, lanes, scratch=()):
        results = [((size, lanes), BF16)] * 3 + [((size // 2, lanes), BF16)] * 2
        return kernel(name, body, parts, results, scratch)

    down_parts = split(
        "split_down",
        split_down_kernel,
        [down_own] + down_recv,
        2 * width,
        [((half, 2 * width), BF16)],
    )
    down_low, down_high = diagonal(down_parts)
    up_parts = split(
        "split_up",
        split_up_kernel,
        after([grad_up, out_own, out_recv], down_parts),
        hidden_half + half,
    )
    up_low, up_high = diagonal(up_parts)
    down_low, down_high = after((down_low, down_high), grad_pieces)
    down_parts = collect("collect_down", down_parts, down_low, down_high)

    result, residual = after((result, residual), up_parts)
    result_other = grid.core(halve(result, 1 - core))

    grad_pieces = after(grad_pieces, up_parts, down_parts[3], result_other)
    grad_joined = kernel(
        "attend_back",
        attend_back_kernel,
        [packed, exact, totals, segs.reshape(1, -1), segs.reshape(-1, 1), grad_blocks]
        + grad_pieces,
        [((4 * span, 3 * group), BF16)],
        [((4 * span, group), BF16), ((6, 4 * span, HEAD_DIM), F32)],
        far=(0, 1, 2, 6, 7, 8),
        extra=14 << 20,
    )[0]
    back_results = kernel(
        "project_back",
        project_back_kernel,
        [grad_joined, weight_qkv, normed, gathered, gathered_other]
        + [sum_out, sums_two, lifted],
        [((size, cut), BF16)] * 4
        + [((4, run_rows, width), F32)]
        + [((192, width), BF16), ((192, width), BF16), ((128, width), BF16)],
        [((width, cut), BF16), ((LANES, width), F32)],
        far=(1, 2, 3, 4),
        extra=10 << 20,
    )
    qkv_parts, back_own, back_low = back_results[:4], back_results[4], back_results[5:]
    up_low, up_high = after((up_low, up_high), back_own)
    up_parts = collect("collect_up", up_parts, up_low, up_high)
    mixed = kernel(
        "deal_back",
        deal_back_kernel,
        [back_own]
        + [grid.core(member) for member in back_low]
        + after(list(down_parts[:3]), up_parts[3]),
        [((2 * shard + run_rows // 2, 2 * width), BF16)] * 4,
        [((4 * run_rows, width), F32), ((size, 2 * width), BF16)],
        far=(5, 6),
    )
    mixed_line = [mixed[0]] + z_send(mixed)
    up_ready = after(list(up_parts[:3]), mixed)
    qkv_parts = [qkv_parts[0]] + after(list(qkv_parts[1:]), up_ready)
    qkv_recv = [grid.along_x(qkv_parts[1]), grid.along_y(qkv_parts[2]), grid.along_xy(qkv_parts[3])]
    up_cut = hidden_half + half
    all_dealt = kernel(
        "deal_all",
        deal_all_kernel,
        after(up_ready, mixed_line) + [qkv_parts[0]] + qkv_recv,
        [((2 * shard, up_cut + cut), BF16)] * 4,
        [((size, up_cut + cut), BF16)],
        far=(1, 2, 4, 5, 6),
    )
    all_line = [all_dealt[0]] + z_send(all_dealt)
    grad_tokens = kernel(
        "final",
        final_kernel,
        mixed_line + [grad_residual, flat, vectors],
        [((own_rows, width), BF16)],
        [((4, run_rows, width), BF16)],
        far=(1, 2, 3, 5),
    )[0]
    grad_down = kernel(
        "line_down", line_down_kernel, mixed_line, [((4 * shard, width), F32)], far=(1, 2, 3)
    )[0]
    result, residual = after((result, residual), all_dealt)
    output = (
        halve(residual, core)
        + (halve(result, core) + result_other)
        + vectors[7:8]
    ).astype(BF16)
    all_line = [all_line[0]] + after(all_line[1:], grad_tokens, grad_down, output)
    mine, theirs = kernel(
        "line_all",
        functools.partial(line_all_kernel, cut=up_cut),
        all_line,
        [((shard, up_cut + 6 * group + LANES), F32)] * 2,
        [((2 * shard, up_cut + 6 * group + LANES), F32)],
        far=(1, 2, 3),
    )
    theirs = grid.core(theirs)
    grad_up_own = both(mine[:, :hidden_half], theirs[:, :hidden_half], 1)
    grad_out_own = both(mine[:, hidden_half:up_cut], theirs[:, hidden_half:up_cut], 1)
    qkv_mine, qkv_theirs = mine[:, up_cut:], theirs[:, up_cut:]
    grad_qkv_own = both(
        qkv_mine[:, : 6 * group].reshape(shard, 3, 1, half),
        qkv_theirs[:, : 6 * group].reshape(shard, 3, 1, half),
        2,
    ).reshape(shard, 6 * half)
    small_sum = (qkv_mine[:, 6 * group : 6 * group + 16] + qkv_theirs[:, 6 * group : 6 * group + 16]).T
    return (
        output.reshape(tokens.shape),
        grad_tokens.reshape(tokens.shape),
        small_sum[0],
        small_sum[1],
        grad_qkv_own,
        small_sum[2],
        small_sum[3],
        grad_out_own,
        small_sum[4],
        small_sum[5],
        small_sum[6],
        grad_up_own,
        small_sum[8:12].reshape(4 * shard),
        grad_down,
        small_sum[7],
    )


def build_local(mesh):
    dp, ctx = mesh.shape["dp"], mesh.shape["ctx"]
    if (dp, ctx) != (4, 8):
        return local_general
    grid = Grid(dp, ctx)
    return lambda *args: split_local(grid, *args)


def solution(mesh):
    return jax.shard_map(
        build_local(mesh),
        mesh=mesh,
        in_specs=(
            P("dp", "ctx", None),
            P("dp", "ctx"),
            P("dp", "ctx", None),
            P(("dp", "ctx")),
            P(("dp", "ctx")),
            P(("dp", "ctx"), None),
            P(("dp", "ctx")),
            P(("dp", "ctx")),
            P(("dp", "ctx"), None),
            P(("dp", "ctx")),
            P(("dp", "ctx")),
            P(("dp", "ctx")),
            P(("dp", "ctx"), None),
            P(("dp", "ctx")),
            P(("dp", "ctx"), None),
            P(("dp", "ctx")),
        ),
        out_specs=(
            P("dp", "ctx", None),
            P("dp", "ctx", None),
            P(("dp", "ctx")),
            P(("dp", "ctx")),
            P(("dp", "ctx"), None),
            P(("dp", "ctx")),
            P(("dp", "ctx")),
            P(("dp", "ctx"), None),
            P(("dp", "ctx")),
            P(("dp", "ctx")),
            P(("dp", "ctx")),
            P(("dp", "ctx"), None),
            P(("dp", "ctx")),
            P(("dp", "ctx"), None),
            P(("dp", "ctx")),
        ),
        check_vma=False,
    )
```
